512 devices in a mesh: space: 16 (over y, x_lo), mode: 32 (over x_hi, z, core).
Axes of the slice: x: 4 (x_hi: 2, x_lo: 2; x = x_hi * 2 + x_lo), y: 8, z: 8, core: 2. Of those that a mesh axis runs over, the one named last changes fastest.
Arguments:
- members: bfloat16 [80, 524288], P(None, ('space', 'mode')), may hold values from -6 to 6
- modes: bfloat16 [128, 524288], P('mode', 'space'), may hold values from -6 to 6
- obs_weights: bfloat16 [2048, 128, 128], P('space'), may hold values from -0.5 to 0.5
- innovations: float32 [2048, 128], P('space'), may hold values from -6 to 6
- tile_start: int32 [2048], P('space'), may hold values from 0 to 32896, as said below
Outputs:
- increment: float32 [524288], P(('space', 'mode'))
- coefficients: float32 [80, 128], P(None, 'mode')
The draws below stay inside these ranges and needn't reach their ends.
Inputs may be any that keep to these rules, and one draw needn't show every extreme that they name: In every horizontal tile the first block's tile_start lies in 0 .. 64 and the last block's in 32832 .. 32896; the first block of the slab starts at 0 and the last at 32896.
All inputs are finite; a program needn't handle non-finite values.
Results may differ from the reference program's by a relative error of at most 0.0003.
Values may be sent and summed in bfloat16 or wider, within the bound.
No kernel may reach another device: no remote copies, remote signals or barrier semaphores. Data moves between devices by JAX's collectives and lax.ppermute only.
A program may use at most 64 MiB of HBM per device.

```python
import jax
import jax.numpy as jnp
from jax import lax

MEMBERS = 80
MODES = 128
CELLS_DEV = 32768
CELLS = 524288
TILE = 128
OBS_BLOCK = 128
BLK_DEV = 128
BLOCKS = 2048


def draw_tile_start(key, part):
    key = jax.random.fold_in(key, 11)
    key_base, key_low, key_high = jax.random.split(key, 3)
    base = jax.random.randint(key_base, (BLOCKS,), 0, CELLS_DEV + TILE + 1, dtype=jnp.int32)
    low = jax.random.randint(key_low, (BLOCKS,), 0, TILE // 2 + 1, dtype=jnp.int32)
    high = jax.random.randint(key_high, (BLOCKS,), CELLS_DEV + TILE // 2, CELLS_DEV + TILE + 1, dtype=jnp.int32)
    within = jnp.arange(BLOCKS, dtype=jnp.int32) % BLK_DEV
    result = jnp.where(within == 0, low, jnp.where(within == BLK_DEV - 1, high, base))
    result = result.at[0].set(0).at[BLOCKS - 1].set(CELLS_DEV + TILE)
    return result.astype(jnp.int32)


def levels(stream_key, extent, shards, least, largest):
    level = 1.0
    for axis_at, parts in shards:
        steps = jax.random.uniform(jax.random.fold_in(jax.random.fold_in(stream_key, 6), axis_at), (parts,), jnp.float32, least / len(shards), largest / len(shards))
        level = level * jnp.repeat(jnp.exp(steps), extent[axis_at] // parts).reshape((-1,) + (1,) * (len(extent) - 1 - axis_at))
    return level


def gaussian(key, shape, scale, limit, pieces=(), held_as=jnp.bfloat16):
    drawn = scale * jax.random.normal(key, shape, jnp.float32)
    if pieces:
        drawn = drawn * levels(key, shape, pieces, -0.22, 0.18)
    return jnp.clip(drawn, -limit, limit).astype(held_as)


def setup_inputs(seed: int = 0) -> dict:
    splits = jax.random.split(jax.random.key(seed), 6)
    members = gaussian(splits[0], (MEMBERS, CELLS), 1.0, 6.0, ((1, 512),))
    modes = gaussian(splits[1], (MODES, CELLS), 1.0, 6.0, ((0, 32), (1, 16)))
    obs_weights = gaussian(splits[2], (BLOCKS, OBS_BLOCK, TILE), TILE ** -0.5, 0.5, ((0, 16),))
    innovations = gaussian(splits[3], (BLOCKS, OBS_BLOCK), 1.0, 6.0, ((0, 16),), jnp.float32)
    tile_start = draw_tile_start(jax.random.fold_in(splits[5], 71), 0)
    return dict(members=members, modes=modes, obs_weights=obs_weights, innovations=innovations, tile_start=tile_start)


def reference(members, modes, obs_weights, innovations, tile_start):
    block_adj = jnp.einsum('bo,bot->bt', innovations, obs_weights.astype(jnp.float32), precision=lax.Precision.HIGHEST)
    owner = (jnp.arange(BLOCKS, dtype=jnp.int32) // BLK_DEV).astype(jnp.int32)
    first = owner * CELLS_DEV - TILE + tile_start
    positions = (first[:, None] + jnp.arange(TILE, dtype=jnp.int32)[None, :]) % CELLS
    weights_field = jnp.zeros((CELLS,), jnp.float32).at[positions.astype(jnp.int32)].add(block_adj)
    member_vals = members.astype(jnp.float32)
    mode_vals = modes.astype(jnp.float32)
    coefficients = jnp.dot(member_vals * weights_field[None, :], mode_vals.T, precision=lax.Precision.HIGHEST)
    spread = jnp.sum(coefficients * coefficients)
    factor = 1.0 / jnp.sqrt(1.0 + spread / (MEMBERS * MODES))
    mixed = jnp.dot(coefficients.T, member_vals, precision=lax.Precision.HIGHEST)
    increment = lax.optimization_barrier(jnp.sum(mode_vals * mixed, axis=0)) * (factor / (MEMBERS - 1))
    return (increment, coefficients)
```

```python
import jax
import jax.numpy as jnp
from jax import lax
from jax.sharding import PartitionSpec as P

MEMBERS = 80
MODE_DEV = 4
CELLS_DEV = 32768
TILE = 128


def from_behind(block, axis, distance):
    devices = range(lax.axis_size(axis))
    route = [((i - distance) % len(devices), i) for i in devices]
    return lax.ppermute(block, axis, route)


def lay_strip(block_adj, tile_start):
    seg_count = CELLS_DEV // TILE + 3
    segment = tile_start // TILE
    offset = tile_start % TILE
    padded = jnp.concatenate([block_adj, jnp.zeros_like(block_adj)], axis=1)
    for level in range((TILE - 1).bit_length()):
        rolled = jnp.roll(padded, 2**level, axis=1)
        picked = offset // 2**level % 2 == 1
        padded = jnp.where(picked[:, None], rolled, padded)
    lower_half = padded[:, :TILE]
    upper_half = padded[:, TILE:]
    seg_ids = jnp.arange(seg_count, dtype=jnp.int32)[:, None]
    onehot_low = (seg_ids == segment[None, :]).astype(jnp.float32)
    onehot_high = (seg_ids == segment[None, :] + 1).astype(jnp.float32)
    segs = jnp.dot(onehot_low, lower_half, precision=lax.Precision.HIGHEST)
    segs = segs + jnp.dot(onehot_high, upper_half, precision=lax.Precision.HIGHEST)
    return segs.reshape(-1)[: CELLS_DEV + 2 * TILE]


def on_device(members, modes, obs_weights, innovations, tile_start):
    mode_count = lax.axis_size("mode")
    space_count = lax.axis_size("space")
    mode_index = lax.axis_index("mode")
    own_count = CELLS_DEV // mode_count
    total_modes = MODE_DEV * mode_count
    all_modes = lax.all_to_all(modes, "mode", split_axis=1, concat_axis=0, tiled=True).astype(
        jnp.float32
    )
    block_adj = jnp.einsum(
        "bo,bot->bt", innovations, obs_weights.astype(jnp.float32), precision=lax.Precision.HIGHEST
    )
    strip = lay_strip(block_adj, tile_start)
    from_right = from_behind(strip[:TILE], "space", -1)
    from_left = from_behind(strip[CELLS_DEV + TILE :], "space", 1)
    weights_field = strip[TILE : TILE + CELLS_DEV]
    weights_field = weights_field.at[CELLS_DEV - TILE :].add(from_right).at[:TILE].add(from_left)
    own_weights = lax.dynamic_slice_in_dim(weights_field, mode_index * own_count, own_count, 0)
    members_f = members.astype(jnp.float32)
    weighted = members_f * own_weights[None, :]
    local_terms = jnp.dot(all_modes, weighted.T, precision=lax.Precision.HIGHEST)
    chunks = lax.all_to_all(
        local_terms.reshape(mode_count, MODE_DEV * MEMBERS), "mode", split_axis=0, concat_axis=0, tiled=True
    )
    own_chunk = jnp.sum(chunks, axis=0)
    gathered = lax.all_gather(own_chunk, ("space", "mode"), axis=0, tiled=False)
    summed = jnp.sum(gathered.reshape(space_count, mode_count, MODE_DEV * MEMBERS), axis=0)
    coeff_all = summed.reshape(total_modes, MEMBERS)
    coefficients = lax.dynamic_slice_in_dim(coeff_all, mode_index * MODE_DEV, MODE_DEV, 0).T
    spread = jnp.sum(coeff_all * coeff_all)
    factor = 1.0 / jnp.sqrt(1.0 + spread / (MEMBERS * total_modes))
    mixed = jnp.dot(coeff_all, members_f, precision=lax.Precision.HIGHEST)
    increment = jnp.sum(all_modes * mixed, axis=0) * (factor / (MEMBERS - 1))
    return (increment, coefficients)


def solution(mesh):
    in_specs = (
        P(None, ("space", "mode")),
        P("mode", "space"),
        P("space", None, None),
        P("space", None),
        P("space"),
    )
    out_specs = (P(("space", "mode")), P(None, "mode"))
    return jax.shard_map(
        on_device, mesh=mesh, in_specs=in_specs, out_specs=out_specs, check_vma=False
    )
```

```python
import jax
import jax.numpy as jnp
from jax import lax
from jax.sharding import PartitionSpec as P

MEMBERS = 80
MODE_DEV = 4
CELLS_DEV = 32768
TILE = 128


def from_behind(block, axis, distance):
    devices = range(lax.axis_size(axis))
    route = [((i - distance) % len(devices), i) for i in devices]
    return lax.ppermute(block, axis, route)


def lay_strip(block_adj, tile_start):
    seg_count = CELLS_DEV // TILE + 3
    segment = tile_start // TILE
    offset = tile_start % TILE
    padded = jnp.concatenate([block_adj, jnp.zeros_like(block_adj)], axis=1)
    for level in range((TILE - 1).bit_length()):
        rolled = jnp.roll(padded, 2**level, axis=1)
        picked = offset // 2**level % 2 == 1
        padded = jnp.where(picked[:, None], rolled, padded)
    lower_half = padded[:, :TILE]
    upper_half = padded[:, TILE:]
    seg_ids = jnp.arange(seg_count, dtype=jnp.int32)[:, None]
    onehot_low = (seg_ids == segment[None, :]).astype(jnp.float32)
    onehot_high = (seg_ids == segment[None, :] + 1).astype(jnp.float32)
    segs = jnp.dot(onehot_low, lower_half, precision=lax.Precision.HIGHEST)
    segs = segs + jnp.dot(onehot_high, upper_half, precision=lax.Precision.HIGHEST)
    return segs.reshape(-1)[: CELLS_DEV + 2 * TILE]


def on_device(members, modes, obs_weights, innovations, tile_start):
    mode_count = lax.axis_size("mode")
    space_count = lax.axis_size("space")
    mode_index = lax.axis_index("mode")
    own_count = CELLS_DEV // mode_count
    total_modes = MODE_DEV * mode_count
    all_modes = lax.all_to_all(modes, "mode", split_axis=1, concat_axis=0, tiled=True).astype(
        jnp.float32
    )
    block_adj = jnp.einsum(
        "bo,bot->bt", innovations, obs_weights.astype(jnp.float32), precision=lax.Precision.HIGHEST
    )
    strip = lay_strip(block_adj, tile_start)
    from_right = from_behind(strip[:TILE], "space", -1)
    from_left = from_behind(strip[CELLS_DEV + TILE :], "space", 1)
    weights_field = strip[TILE : TILE + CELLS_DEV]
    weights_field = weights_field.at[CELLS_DEV - TILE :].add(from_right).at[:TILE].add(from_left)
    own_weights = lax.dynamic_slice_in_dim(weights_field, mode_index * own_count, own_count, 0)
    members_f = members.astype(jnp.float32)
    weighted = members_f * own_weights[None, :]
    local_terms = jnp.dot(all_modes, weighted.T, precision=lax.Precision.HIGHEST)
    tiles = jnp.pad(
        local_terms.reshape(mode_count, MODE_DEV, MEMBERS), ((0, 0), (0, 8 - MODE_DEV), (0, 128 - MEMBERS))
    )
    own_tile = jnp.sum(lax.all_to_all(tiles, "mode", split_axis=0, concat_axis=0, tiled=True), axis=0)
    spaces = lax.all_gather(own_tile, "space", axis=0, tiled=True)
    own_sum = jnp.sum(spaces.reshape(space_count, 8, 128), axis=0)
    gathered = lax.all_gather(own_sum, "mode", axis=0, tiled=True)
    coeff_all = gathered.reshape(mode_count, 8, 128)[:, :MODE_DEV, :MEMBERS].reshape(total_modes, MEMBERS)
    coefficients = lax.dynamic_slice_in_dim(coeff_all, mode_index * MODE_DEV, MODE_DEV, 0).T
    spread = jnp.sum(coeff_all * coeff_all)
    factor = 1.0 / jnp.sqrt(1.0 + spread / (MEMBERS * total_modes))
    mixed = jnp.dot(coeff_all, members_f, precision=lax.Precision.HIGHEST)
    increment = jnp.sum(all_modes * mixed, axis=0) * (factor / (MEMBERS - 1))
    return (increment, coefficients)


def solution(mesh):
    in_specs = (
        P(None, ("space", "mode")),
        P("mode", "space"),
        P("space", None, None),
        P("space", None),
        P("space"),
    )
    out_specs = (P(("space", "mode")), P(None, "mode"))
    return jax.shard_map(
        on_device, mesh=mesh, in_specs=in_specs, out_specs=out_specs, check_vma=False
    )
```

```python
import functools

import jax
import jax.numpy as jnp
from jax import lax
from jax.experimental import pallas as pl
from jax.experimental.pallas import tpu as pltpu
from jax.sharding import PartitionSpec as P

MEMBERS = 80
MODE_DEV = 4
MODES = 128
CELLS_DEV = 32768
TILE = 128
BLK_DEV = 128
OWN = 1024
OWN_TILES = OWN // TILE
LANES = 128
SUBLANES = 8
VMEM = pl.BlockSpec(memory_space=pltpu.VMEM)


def split2(x):
    high = x.astype(jnp.bfloat16)
    return high, (x - high.astype(jnp.float32)).astype(jnp.bfloat16)


def field_kernel(mode_count, start_ref, innov_ref, obs_ref, own_ref, halo_ref, ids, held, acc, sems):
    m = lax.axis_index("mode")
    lo = m * OWN
    least = jnp.where(m == 0, lo - 2 * TILE, lo - TILE)
    bound = jnp.where(m == mode_count - 1, lo + OWN + TILE, lo + OWN)

    def scan(b, count):
        cell = start_ref[b] - TILE
        ids[count] = b
        return count + jnp.where((cell > least) & (cell < bound), 1, 0)

    count = lax.fori_loop(0, BLK_DEV, scan, jnp.int32(0), unroll=8)

    def fetch(i):
        return pltpu.make_async_copy(obs_ref.at[ids[i]], held.at[i], sems.at[i])

    def begin(i, carry):
        fetch(i).start()
        return carry

    lax.fori_loop(0, count, begin, 0)
    acc[...] = jnp.zeros_like(acc)
    lane = lax.broadcasted_iota(jnp.int32, (1, LANES), 1)

    def add(i, carry):
        b = ids[i]
        row = innov_ref[pl.ds(b, 1), :]
        high = row.astype(jnp.bfloat16).astype(jnp.float32)
        mid = (row - high).astype(jnp.bfloat16).astype(jnp.float32)
        low = row - high - mid
        parts = jnp.concatenate([high, mid, low, jnp.zeros((SUBLANES - 3, LANES), jnp.float32)], axis=0)
        fetch(i).wait()
        adj = jnp.dot(parts.astype(jnp.bfloat16), held[i], preferred_element_type=jnp.float32)
        place = start_ref[b] - TILE - (lo - 2 * TILE)
        seg = lax.shift_right_logical(place, 7)
        off = lax.bitwise_and(place, TILE - 1)
        adj = adj + pltpu.roll(adj, SUBLANES - 1, 0) + pltpu.roll(adj, SUBLANES - 2, 0)
        rolled = pltpu.roll(adj, off, 1)[0:1, :]
        acc[pl.ds(seg, 1), :] += jnp.where(lane >= off, rolled, 0.0)
        acc[pl.ds(seg + 1, 1), :] += jnp.where(lane < off, rolled, 0.0)
        return carry

    lax.fori_loop(0, count, add, 0)
    own_ref[...] = acc[2 : 2 + OWN_TILES, :]
    halo_ref[...] = jnp.where(m == 0, acc[1:2, :], acc[2 + OWN_TILES : 3 + OWN_TILES, :])


def field(tile_start, innovations, obs_weights, mode_count):
    return pl.pallas_call(
        functools.partial(field_kernel, mode_count),
        out_shape=(
            jax.ShapeDtypeStruct((OWN_TILES, LANES), jnp.float32),
            jax.ShapeDtypeStruct((1, LANES), jnp.float32),
        ),
        in_specs=[pl.BlockSpec(memory_space=pltpu.SMEM), VMEM, pl.BlockSpec(memory_space=pl.ANY)],
        out_specs=(VMEM, VMEM),
        scratch_shapes=[
            pltpu.SMEM((BLK_DEV,), jnp.int32),
            pltpu.VMEM((BLK_DEV, TILE, TILE), jnp.bfloat16),
            pltpu.VMEM((2 * SUBLANES, LANES), jnp.float32),
            pltpu.SemaphoreType.DMA((BLK_DEV,)),
        ],
        compiler_params=pltpu.CompilerParams(vmem_limit_bytes=56 * 2**20),
        cost_estimate=pl.CostEstimate(flops=2**22, bytes_accessed=2**22, transcendentals=0),
        name="field",
    )(tile_start, innovations, obs_weights)


def project_kernel(mode_count, own_ref, halo_ref, members_ref, modes_ref, out_ref):
    m = lax.axis_index("mode")
    halo = halo_ref[...]
    row = lax.broadcasted_iota(jnp.int32, (OWN_TILES, LANES), 0)
    takes = ((row == 0) & (m == 0)) | ((row == OWN_TILES - 1) & (m == mode_count - 1))
    weights = own_ref[...] + jnp.where(takes, halo, 0.0)
    total = jnp.zeros((MODES, MEMBERS), jnp.float32)
    contract = (((1,), (1,)), ((), ()))
    highs, lows = [], []
    for j in range(OWN_TILES):
        cells = slice(j * TILE, (j + 1) * TILE)
        high, low = split2(members_ref[:, cells].astype(jnp.float32) * weights[j : j + 1, :])
        highs.append(high)
        lows.append(low)
    modes = modes_ref[...]
    total = lax.dot_general(modes, jnp.concatenate(highs, 1), contract, preferred_element_type=jnp.float32)
    total += lax.dot_general(modes, jnp.concatenate(lows, 1), contract, preferred_element_type=jnp.float32)
    out_ref[...] = jnp.zeros_like(out_ref)
    out_ref[:, 0:MEMBERS] = total


def project(own, halo, members, modes, mode_count):
    return pl.pallas_call(
        functools.partial(project_kernel, mode_count),
        out_shape=jax.ShapeDtypeStruct((MODES, LANES), jnp.float32),
        in_specs=[VMEM] * 4,
        out_specs=VMEM,
        compiler_params=pltpu.CompilerParams(vmem_limit_bytes=8 * 2**20),
        name="project",
    )(own, halo, members, modes)


def finish_kernel(total_count, coeff_ref, members_ref, modes_ref, inc_ref, own_ref):
    m = lax.axis_index("mode")
    coeff = coeff_ref[:, 0:MEMBERS]
    own_ref[...] = coeff_ref[pl.ds(m * MODE_DEV, MODE_DEV), 0:MEMBERS]
    spread = jnp.sum(jnp.sum(coeff * coeff, axis=0, keepdims=True), axis=1, keepdims=True)
    factor = lax.rsqrt(1.0 + spread / total_count)
    high, low = split2(coeff)
    members = members_ref[...]
    mixed = jnp.dot(high, members, preferred_element_type=jnp.float32)
    mixed += jnp.dot(low, members, preferred_element_type=jnp.float32)
    mixed = mixed * modes_ref[...].astype(jnp.float32)
    summed = jnp.sum(mixed, axis=0, keepdims=True) * (factor / (MEMBERS - 1))
    for j in range(OWN_TILES):
        inc_ref[j : j + 1, :] = summed[:, j * TILE : (j + 1) * TILE]


def finish(coeff, members, modes):
    return pl.pallas_call(
        functools.partial(finish_kernel, MEMBERS * MODES),
        out_shape=(
            jax.ShapeDtypeStruct((OWN_TILES, LANES), jnp.float32),
            jax.ShapeDtypeStruct((MODE_DEV, MEMBERS), jnp.float32),
        ),
        in_specs=[VMEM] * 3,
        out_specs=(VMEM, VMEM),
        compiler_params=pltpu.CompilerParams(vmem_limit_bytes=8 * 2**20),
        name="finish",
    )(coeff, members, modes)


def exchange(x, axis):
    return lax.all_to_all(x, axis, split_axis=0, concat_axis=0, tiled=True)


def on_device(members, modes, obs_weights, innovations, tile_start):
    mode_count = lax.axis_size("mode")
    space_count = lax.axis_size("space")
    all_modes = lax.all_to_all(modes, "mode", split_axis=1, concat_axis=0, tiled=True)
    own, halo = field(tile_start, innovations, obs_weights, mode_count)
    route = []
    for s in range(space_count):
        behind, ahead = (s - 1) % space_count, (s + 1) % space_count
        route.append((s * mode_count, behind * mode_count + mode_count - 1))
        route.append((s * mode_count + mode_count - 1, ahead * mode_count))
    halo = lax.ppermute(halo, ("space", "mode"), route)
    terms = project(own, halo, members, all_modes, mode_count)
    chunk = MODES // space_count
    parts = exchange(terms.reshape(space_count, chunk, LANES), "space")
    part = jnp.sum(parts, axis=0)
    parts = exchange(jnp.broadcast_to(part[None], (mode_count, chunk, LANES)), "mode")
    part = jnp.sum(parts, axis=0)
    coeff = exchange(jnp.broadcast_to(part[None], (space_count, chunk, LANES)), "space")
    increment, own_coeff = finish(coeff.reshape(MODES, LANES), members, all_modes)
    return increment.reshape(OWN), own_coeff.T


def solution(mesh):
    in_specs = (
        P(None, ("space", "mode")),
        P("mode", "space"),
        P("space", None, None),
        P("space", None),
        P("space"),
    )
    out_specs = (P(("space", "mode")), P(None, "mode"))
    return jax.shard_map(
        on_device, mesh=mesh, in_specs=in_specs, out_specs=out_specs, check_vma=False
    )
```

```python
import functools

import jax
import jax.numpy as jnp
from jax import lax
from jax.experimental import pallas as pl
from jax.experimental.pallas import tpu as pltpu
from jax.sharding import PartitionSpec as P

MEMBERS = 80
MODE_DEV = 4
MODES = 128
CELLS_DEV = 32768
TILE = 128
BLK_DEV = 128
OWN = 1024
OWN_TILES = OWN // TILE
LANES = 128
SUBLANES = 8
VMEM = pl.BlockSpec(memory_space=pltpu.VMEM)


def split2(x):
    high = x.astype(jnp.bfloat16)
    return high, (x - high.astype(jnp.float32)).astype(jnp.bfloat16)


def field_kernel(mode_count, start_ref, innov_ref, obs_ref, own_ref, halo_ref, ids, held, acc, sems):
    m = lax.axis_index("mode")
    lo = m * OWN
    least = jnp.where(m == 0, lo - 2 * TILE, lo - TILE)
    bound = jnp.where(m == mode_count - 1, lo + OWN + TILE, lo + OWN)

    def scan(b, count):
        cell = start_ref[b] - TILE
        ids[count] = b
        return count + jnp.where((cell > least) & (cell < bound), 1, 0)

    count = lax.fori_loop(0, BLK_DEV, scan, jnp.int32(0), unroll=8)

    def fetch(i):
        return pltpu.make_async_copy(obs_ref.at[ids[i]], held.at[i], sems.at[i])

    def begin(i, carry):
        fetch(i).start()
        return carry

    lax.fori_loop(0, count, begin, 0)
    acc[...] = jnp.zeros_like(acc)
    lane = lax.broadcasted_iota(jnp.int32, (1, LANES), 1)

    def add(i, carry):
        b = ids[i]
        row = innov_ref[pl.ds(b, 1), :]
        high = row.astype(jnp.bfloat16).astype(jnp.float32)
        mid = (row - high).astype(jnp.bfloat16).astype(jnp.float32)
        low = row - high - mid
        parts = jnp.concatenate([high, mid, low, jnp.zeros((SUBLANES - 3, LANES), jnp.float32)], axis=0)
        fetch(i).wait()
        adj = jnp.dot(parts.astype(jnp.bfloat16), held[i], preferred_element_type=jnp.float32)
        place = start_ref[b] - TILE - (lo - 2 * TILE)
        seg = lax.shift_right_logical(place, 7)
        off = lax.bitwise_and(place, TILE - 1)
        adj = adj + pltpu.roll(adj, SUBLANES - 1, 0) + pltpu.roll(adj, SUBLANES - 2, 0)
        rolled = pltpu.roll(adj, off, 1)[0:1, :]
        acc[pl.ds(seg, 1), :] += jnp.where(lane >= off, rolled, 0.0)
        acc[pl.ds(seg + 1, 1), :] += jnp.where(lane < off, rolled, 0.0)
        return carry

    lax.fori_loop(0, count, add, 0)
    own_ref[...] = acc[2 : 2 + OWN_TILES, :]
    halo_ref[...] = jnp.where(m == 0, acc[1:2, :], acc[2 + OWN_TILES : 3 + OWN_TILES, :])


def field(tile_start, innovations, obs_weights, mode_count):
    return pl.pallas_call(
        functools.partial(field_kernel, mode_count),
        out_shape=(
            jax.ShapeDtypeStruct((OWN_TILES, LANES), jnp.float32),
            jax.ShapeDtypeStruct((1, LANES), jnp.float32),
        ),
        in_specs=[pl.BlockSpec(memory_space=pltpu.SMEM), VMEM, pl.BlockSpec(memory_space=pl.ANY)],
        out_specs=(VMEM, VMEM),
        scratch_shapes=[
            pltpu.SMEM((BLK_DEV,), jnp.int32),
            pltpu.VMEM((BLK_DEV, TILE, TILE), jnp.bfloat16),
            pltpu.VMEM((2 * SUBLANES, LANES), jnp.float32),
            pltpu.SemaphoreType.DMA((BLK_DEV,)),
        ],
        compiler_params=pltpu.CompilerParams(vmem_limit_bytes=56 * 2**20),
        cost_estimate=pl.CostEstimate(flops=2**22, bytes_accessed=2**22, transcendentals=0),
        name="field",
    )(tile_start, innovations, obs_weights)


def project_kernel(mode_count, own_ref, halo_ref, members_ref, modes_ref, out_ref):
    m = lax.axis_index("mode")
    halo = halo_ref[...]
    row = lax.broadcasted_iota(jnp.int32, (OWN_TILES, LANES), 0)
    takes = ((row == 0) & (m == 0)) | ((row == OWN_TILES - 1) & (m == mode_count - 1))
    weights = own_ref[...] + jnp.where(takes, halo, 0.0)
    contract = (((1,), (1,)), ((), ()))
    highs, lows = [], []
    for j in range(OWN_TILES):
        cells = slice(j * TILE, (j + 1) * TILE)
        high, low = split2(members_ref[:, cells].astype(jnp.float32) * weights[j : j + 1, :])
        highs.append(high)
        lows.append(low)
    modes = modes_ref[...]
    total = lax.dot_general(jnp.concatenate(highs, 1), modes, contract, preferred_element_type=jnp.float32)
    total += lax.dot_general(jnp.concatenate(lows, 1), modes, contract, preferred_element_type=jnp.float32)
    out_ref[...] = total


def project(own, halo, members, modes, mode_count):
    return pl.pallas_call(
        functools.partial(project_kernel, mode_count),
        out_shape=jax.ShapeDtypeStruct((MEMBERS, MODES), jnp.float32),
        in_specs=[VMEM] * 4,
        out_specs=VMEM,
        compiler_params=pltpu.CompilerParams(vmem_limit_bytes=8 * 2**20),
        name="project",
    )(own, halo, members, modes)


def finish_kernel(total_count, coeff_ref, members_ref, modes_ref, inc_ref, own_ref, turned):
    m = lax.axis_index("mode")
    coeff = coeff_ref[...].T
    turned[...] = coeff
    own_ref[...] = turned[pl.ds(m * MODE_DEV, MODE_DEV), :]
    spread = jnp.sum(jnp.sum(coeff * coeff, axis=0, keepdims=True), axis=1, keepdims=True)
    factor = lax.rsqrt(1.0 + spread / total_count)
    high, low = split2(coeff)
    members = members_ref[...]
    mixed = jnp.dot(high, members, preferred_element_type=jnp.float32)
    mixed += jnp.dot(low, members, preferred_element_type=jnp.float32)
    mixed = mixed * modes_ref[...].astype(jnp.float32)
    summed = jnp.sum(mixed, axis=0, keepdims=True) * (factor / (MEMBERS - 1))
    for j in range(OWN_TILES):
        inc_ref[j : j + 1, :] = summed[:, j * TILE : (j + 1) * TILE]


def finish(coeff, members, modes):
    return pl.pallas_call(
        functools.partial(finish_kernel, MEMBERS * MODES),
        out_shape=(
            jax.ShapeDtypeStruct((OWN_TILES, LANES), jnp.float32),
            jax.ShapeDtypeStruct((MODE_DEV, MEMBERS), jnp.float32),
        ),
        in_specs=[VMEM] * 3,
        out_specs=(VMEM, VMEM),
        scratch_shapes=[pltpu.VMEM((MODES, MEMBERS), jnp.float32)],
        compiler_params=pltpu.CompilerParams(vmem_limit_bytes=8 * 2**20),
        name="finish",
    )(coeff, members, modes)


def gather_sum(x, axis):
    parts = lax.all_gather(x, axis, axis=0, tiled=True)
    return jnp.sum(parts.reshape((lax.axis_size(axis),) + x.shape), axis=0)


def on_device(members, modes, obs_weights, innovations, tile_start):
    mode_count = lax.axis_size("mode")
    space_count = lax.axis_size("space")
    all_modes = lax.all_to_all(modes, "mode", split_axis=1, concat_axis=0, tiled=True)
    own, halo = field(tile_start, innovations, obs_weights, mode_count)
    route = []
    for s in range(space_count):
        behind, ahead = (s - 1) % space_count, (s + 1) % space_count
        route.append((s * mode_count, behind * mode_count + mode_count - 1))
        route.append((s * mode_count + mode_count - 1, ahead * mode_count))
    halo = lax.ppermute(halo, ("space", "mode"), route)
    terms = project(own, halo, members, all_modes, mode_count)
    terms = gather_sum(terms, "space")
    coeff = gather_sum(terms, "mode")
    increment, own_coeff = finish(coeff, members, all_modes)
    return increment.reshape(OWN), own_coeff.T


def solution(mesh):
    in_specs = (
        P(None, ("space", "mode")),
        P("mode", "space"),
        P("space", None, None),
        P("space", None),
        P("space"),
    )
    out_specs = (P(("space", "mode")), P(None, "mode"))
    return jax.shard_map(
        on_device, mesh=mesh, in_specs=in_specs, out_specs=out_specs, check_vma=False
    )
```

```python
import functools

import jax
import jax.numpy as jnp
from jax import lax
from jax.experimental import pallas as pl
from jax.experimental.pallas import tpu as pltpu
from jax.sharding import Mesh
from jax.sharding import PartitionSpec as P

MEMBERS = 80
MODE_DEV = 4
MODES = 128
CELLS_DEV = 32768
TILE = 128
BLK_DEV = 128
OWN = 1024
CORES = 2
WORK = CORES * OWN
OWN_TILES = OWN // TILE
WORK_TILES = WORK // TILE
LANES = 128
SUBLANES = 8
GROUP = 4
VMEM = pl.BlockSpec(memory_space=pltpu.VMEM)
SMALL = pltpu.CompilerParams(vmem_limit_bytes=12 * 2**20)


def split2(x):
    high = x.astype(jnp.bfloat16)
    return high, (x - high.astype(jnp.float32)).astype(jnp.bfloat16)


def dot(a, b, dims):
    return lax.dot_general(a, b, (dims, ((), ())), preferred_element_type=jnp.float32)


def field_kernel(pair_count, start_ref, innov_ref, obs_ref, work_ref, halo_ref, ids, places, held, acc, sems):
    p = lax.axis_index("pair")
    lo = p * WORK
    least = jnp.where(p == 0, lo - 2 * TILE, lo - TILE)
    bound = jnp.where(p == pair_count - 1, lo + WORK + TILE, lo + WORK)

    def scan(b, count):
        cell = start_ref[b] - TILE
        ids[count] = b
        places[count] = cell - lo + 2 * TILE
        return count + jnp.where((cell > least) & (cell < bound), 1, 0)

    count = lax.fori_loop(0, BLK_DEV, scan, jnp.int32(0), unroll=8)

    def fetch(i):
        return pltpu.make_async_copy(obs_ref.at[ids[i]], held.at[i], sems.at[i])

    def begin(i, carry):
        fetch(i).start()
        return carry

    lax.fori_loop(0, count, begin, 0)
    acc[...] = jnp.zeros_like(acc)
    lane = lax.broadcasted_iota(jnp.int32, (1, LANES), 1)

    def add(g, carry):
        for u in range(GROUP):

            @pl.when(g * GROUP + u < count)
            def _():
                fetch(g * GROUP + u).wait()

        found = []
        for u in range(GROUP):
            i = g * GROUP + u
            valid = i < count
            b = jnp.where(valid, ids[i], 0)
            place = jnp.where(valid, places[i], 0)
            row = innov_ref[pl.ds(b, 1), :]
            high = row.astype(jnp.bfloat16).astype(jnp.float32)
            mid = (row - high).astype(jnp.bfloat16).astype(jnp.float32)
            low = row - high - mid
            parts = jnp.concatenate([high, mid, low, jnp.zeros((SUBLANES - 3, LANES), jnp.float32)], axis=0)
            adj = dot(parts.astype(jnp.bfloat16), held[i], ((1,), (0,)))
            adj = adj + pltpu.roll(adj, SUBLANES - 1, 0) + pltpu.roll(adj, SUBLANES - 2, 0)
            off = lax.bitwise_and(place, TILE - 1)
            rolled = pltpu.roll(adj, off, 1)[0:1, :]
            rolled = jnp.where(valid, rolled, 0.0)
            found.append((lax.shift_right_logical(place, 7), off, rolled))
        for seg, off, rolled in found:
            acc[pl.ds(seg, 1), :] += jnp.where(lane >= off, rolled, 0.0)
            acc[pl.ds(seg + 1, 1), :] += jnp.where(lane < off, rolled, 0.0)
        return carry

    lax.fori_loop(0, lax.shift_right_logical(count + GROUP - 1, 2), add, 0)
    work_ref[...] = acc[2 : 2 + WORK_TILES, :]
    halo_ref[...] = jnp.where(p == 0, acc[1:2, :], acc[2 + WORK_TILES : 3 + WORK_TILES, :])


def field(tile_start, innovations, obs_weights, pair_count):
    return pl.pallas_call(
        functools.partial(field_kernel, pair_count),
        out_shape=(
            jax.ShapeDtypeStruct((WORK_TILES, LANES), jnp.float32),
            jax.ShapeDtypeStruct((1, LANES), jnp.float32),
        ),
        in_specs=[pl.BlockSpec(memory_space=pltpu.SMEM), VMEM, pl.BlockSpec(memory_space=pltpu.HBM)],
        out_specs=(VMEM, VMEM),
        scratch_shapes=[
            pltpu.SMEM((BLK_DEV + GROUP,), jnp.int32),
            pltpu.SMEM((BLK_DEV + GROUP,), jnp.int32),
            pltpu.VMEM((BLK_DEV + GROUP, TILE, TILE), jnp.bfloat16),
            pltpu.VMEM((WORK_TILES + SUBLANES, LANES), jnp.float32),
            pltpu.SemaphoreType.DMA((BLK_DEV,)),
        ],
        compiler_params=SMALL,
        cost_estimate=pl.CostEstimate(flops=2**22, bytes_accessed=2**22, transcendentals=0),
        name="field",
    )(tile_start, innovations, obs_weights)


def halves(core):
    return [pl.multiple_of(c * OWN, OWN) for c in (core, 1 - core)]


def project_kernel(pair_count, chunks, work_ref, halo_ref, own_ref, other_ref, modes_ref, out_ref):
    p = lax.axis_index("pair")
    core = lax.axis_index("core")
    halo = halo_ref[...]
    row = lax.broadcasted_iota(jnp.int32, (OWN_TILES, LANES), 0)
    first = (row == 0) & (p == 0)
    last = (row == OWN_TILES - 1) & (p == pair_count - 1)
    total = None
    for member_ref, at, c in zip((own_ref, other_ref), halves(core), (core, 1 - core)):
        weights = work_ref[pl.ds(pl.multiple_of(c * OWN_TILES, OWN_TILES), OWN_TILES), :]
        takes = (first & (c == 0)) | (last & (c == 1))
        weights = weights + jnp.where(takes, halo, 0.0)
        highs, lows = [], []
        for j in range(OWN_TILES):
            cells = slice(j * TILE, (j + 1) * TILE)
            high, low = split2(member_ref[:, cells].astype(jnp.float32) * weights[j : j + 1, :])
            highs.append(high)
            lows.append(low)
        modes = modes_ref[:, pl.ds(at, OWN)]
        part = dot(modes, jnp.concatenate(highs, 1), ((1,), (1,)))
        part += dot(modes, jnp.concatenate(lows, 1), ((1,), (1,)))
        total = part if total is None else total + part
    out_ref[...] = jnp.zeros_like(out_ref)
    for c in range(chunks):
        out_ref[c, :, 0:MEMBERS] = total[c * MODE_DEV : (c + 1) * MODE_DEV, :]


def project(work, halo, own, other, modes, pair_count, chunks):
    return pl.pallas_call(
        functools.partial(project_kernel, pair_count, chunks),
        out_shape=jax.ShapeDtypeStruct((chunks, MODE_DEV, LANES), jnp.float32),
        in_specs=[VMEM] * 5,
        out_specs=VMEM,
        compiler_params=SMALL,
        name="project",
    )(work, halo, own, other, modes)


def mix_kernel(chunks, coeff_ref, own_ref, other_ref, modes_ref, keep_ref, send_ref, coeff_out_ref):
    core = lax.axis_index("core")
    coeff_out_ref[...] = coeff_ref[lax.axis_index("pair"), :, 0:MEMBERS]
    coeff = jnp.concatenate([coeff_ref[c, :, 0:MEMBERS] for c in range(chunks)], axis=0)
    spread = jnp.sum(jnp.sum(coeff * coeff, axis=0, keepdims=True), axis=1, keepdims=True)
    spread = jnp.broadcast_to(spread, (SUBLANES, LANES))
    high, low = split2(coeff)
    for member_ref, at, out_ref in zip((other_ref, own_ref), halves(core)[::-1], (send_ref, keep_ref)):
        members = member_ref[...]
        mixed = dot(high, members, ((1,), (0,))) + dot(low, members, ((1,), (0,)))
        mixed = mixed * modes_ref[:, pl.ds(at, OWN)].astype(jnp.float32)
        summed = jnp.sum(mixed, axis=0, keepdims=True)
        for j in range(OWN_TILES):
            out_ref[j : j + 1, :] = summed[:, j * TILE : (j + 1) * TILE]
        out_ref[OWN_TILES:, :] = spread


def mix(coeff, own, other, modes, chunks):
    both = jax.ShapeDtypeStruct((OWN_TILES + SUBLANES, LANES), jnp.float32)
    return pl.pallas_call(
        functools.partial(mix_kernel, chunks),
        out_shape=(both, both, jax.ShapeDtypeStruct((MODE_DEV, MEMBERS), jnp.float32)),
        in_specs=[VMEM] * 4,
        out_specs=(VMEM,) * 3,
        compiler_params=SMALL,
        name="mix",
    )(coeff, own, other, modes)


def scale_kernel(keep_ref, got_ref, inc_ref):
    total = keep_ref[...] + got_ref[...]
    factor = lax.rsqrt(1.0 + total[OWN_TILES:, :] / (MEMBERS * MODES)) / (MEMBERS - 1)
    inc_ref[...] = total[:OWN_TILES, :] * factor


def scale(keep, got):
    return pl.pallas_call(
        scale_kernel,
        out_shape=jax.ShapeDtypeStruct((OWN_TILES, LANES), jnp.float32),
        in_specs=[VMEM] * 2,
        out_specs=VMEM,
        compiler_params=SMALL,
        name="scale",
    )(keep, got)


def exchange(x, axis):
    return lax.all_to_all(x, axis, split_axis=0, concat_axis=0, tiled=True)


def swap(x):
    return lax.ppermute(x, "core", [(0, 1), (1, 0)])


def everywhere(x, axis):
    return exchange(jnp.broadcast_to(x[None], (lax.axis_size(axis),) + x.shape), axis)


def on_device(members, modes, obs_weights, innovations, tile_start):
    pairs = lax.axis_size("pair")
    spaces = lax.axis_size("space")
    modes = lax.all_to_all(modes, "pair", split_axis=1, concat_axis=0, tiled=True)
    other = swap(members)
    obs_weights = pltpu.with_memory_space_constraint(obs_weights, pltpu.HBM)
    work, halo = field(tile_start, innovations, obs_weights, pairs)
    route = []
    for s in range(spaces):
        behind, ahead = (s - 1) % spaces, (s + 1) % spaces
        route.append((s * pairs, behind * pairs + pairs - 1))
        route.append((s * pairs + pairs - 1, ahead * pairs))
    halo = lax.ppermute(halo, ("space", "pair"), route)
    terms = project(work, halo, members, other, modes, pairs, spaces)
    part = jnp.sum(exchange(terms, "space"), axis=0)
    part = jnp.sum(everywhere(part, "pair"), axis=0)
    coeff = everywhere(part, "space")
    keep, send, own_coeff = mix(coeff, members, other, modes, spaces)
    increment = scale(keep, swap(send))
    return increment.reshape(OWN), own_coeff.T


def solution(mesh):
    devices = mesh.devices
    finer = Mesh(devices.reshape(devices.shape[0], -1, CORES), ("space", "pair", "core"))
    in_specs = (
        P(None, ("space", "pair", "core")),
        P(("pair", "core"), "space"),
        P("space", None, None),
        P("space", None),
        P("space"),
    )
    out_specs = (P(("space", "pair", "core")), P(None, ("pair", "core")))
    return jax.shard_map(
        on_device, mesh=finer, in_specs=in_specs, out_specs=out_specs, check_vma=False
    )
```

```python
import functools

import jax
import jax.numpy as jnp
from jax import lax
from jax.experimental import pallas as pl
from jax.experimental.pallas import tpu as pltpu
from jax.sharding import Mesh
from jax.sharding import PartitionSpec as P

MEMBERS = 80
MODE_DEV = 4
MODES = 128
CELLS_DEV = 32768
TILE = 128
BLK_DEV = 128
OWN = 1024
OWN_TILES = OWN // TILE
LANES = 128
SUBLANES = 8
GROUP = 4
VMEM = pl.BlockSpec(memory_space=pltpu.VMEM)
SMALL = pltpu.CompilerParams(vmem_limit_bytes=12 * 2**20)
MODE = ("xhi", "z", "core")
SPACE = ("y", "xlo")
RING = ("xlo", "xhi", "core")


def mode_index():
    at = lax.axis_index("xhi") * lax.axis_size("z") + lax.axis_index("z")
    return at * lax.axis_size("core") + lax.axis_index("core")


def split2(x):
    high = x.astype(jnp.bfloat16)
    return high, (x - high.astype(jnp.float32)).astype(jnp.bfloat16)


def field_kernel(last, start_ref, innov_ref, obs_ref, own_ref, halo_ref, starts, ids, rows, held, acc, start_sem, sems):
    m = mode_index()
    copy = pltpu.make_async_copy(start_ref, starts, start_sem)
    copy.start()
    base = m * OWN - TILE
    least = jnp.where(m == 0, 0, TILE)
    bound = jnp.where(m == last, OWN + 3 * TILE, OWN + 2 * TILE)
    acc[...] = jnp.zeros_like(acc)
    copy.wait()

    def fetch(i, b):
        return (
            pltpu.make_async_copy(obs_ref.at[b], held.at[i], sems.at[0, i]),
            pltpu.make_async_copy(innov_ref.at[b], rows.at[i], sems.at[1, i]),
        )

    def scan(b, count):
        place = starts[b] - base
        hit = (place > least) & (place < bound)

        @pl.when(hit)
        def _():
            ids[count] = b
            for part in fetch(count, b):
                part.start()

        return count + jnp.where(hit, 1, 0)

    count = lax.fori_loop(0, BLK_DEV, scan, jnp.int32(0), unroll=8)
    lane = lax.broadcasted_iota(jnp.int32, (1, LANES), 1)

    def add(g, carry):
        for u in range(GROUP):

            @pl.when(g * GROUP + u < count)
            def _():
                for part in fetch(g * GROUP + u, ids[g * GROUP + u]):
                    part.wait()

        found = []
        for u in range(GROUP):
            i = g * GROUP + u
            valid = i < count
            place = jnp.where(valid, starts[jnp.where(valid, ids[i], 0)] - base, 0)
            row = rows[i]
            high = row.astype(jnp.bfloat16).astype(jnp.float32)
            mid = (row - high).astype(jnp.bfloat16).astype(jnp.float32)
            low = row - high - mid
            parts = jnp.concatenate([high, mid, low, jnp.zeros((SUBLANES - 3, LANES), jnp.float32)], axis=0)
            adj = jnp.dot(parts.astype(jnp.bfloat16), held[i], preferred_element_type=jnp.float32)
            adj = adj + pltpu.roll(adj, SUBLANES - 1, 0) + pltpu.roll(adj, SUBLANES - 2, 0)
            off = lax.bitwise_and(place, TILE - 1)
            rolled = jnp.where(valid, pltpu.roll(adj, off, 1)[0:1, :], 0.0)
            found.append((lax.shift_right_logical(place, 7), off, rolled))
        for seg, off, rolled in found:
            acc[pl.ds(seg, 1), :] += jnp.where(lane >= off, rolled, 0.0)
            acc[pl.ds(seg + 1, 1), :] += jnp.where(lane < off, rolled, 0.0)
        return carry

    lax.fori_loop(0, lax.shift_right_logical(count + GROUP - 1, 2), add, 0)
    own_ref[...] = acc[2 : 2 + OWN_TILES, :]
    halo_ref[...] = jnp.where(m == 0, acc[1:2, :], acc[2 + OWN_TILES : 3 + OWN_TILES, :])


def field(tile_start, innovations, obs_weights, last):
    hbm = [pl.BlockSpec(memory_space=pltpu.HBM)] * 3
    rows = innovations.reshape(BLK_DEV, 1, LANES)
    operands = [pltpu.with_memory_space_constraint(x, pltpu.HBM) for x in (tile_start, rows, obs_weights)]
    return pl.pallas_call(
        functools.partial(field_kernel, last),
        out_shape=(
            jax.ShapeDtypeStruct((OWN_TILES, LANES), jnp.float32),
            jax.ShapeDtypeStruct((1, LANES), jnp.float32),
        ),
        in_specs=hbm,
        out_specs=(VMEM, VMEM),
        scratch_shapes=[
            pltpu.SMEM((BLK_DEV,), jnp.int32),
            pltpu.SMEM((BLK_DEV + GROUP,), jnp.int32),
            pltpu.VMEM((BLK_DEV + GROUP, 1, LANES), jnp.float32),
            pltpu.VMEM((BLK_DEV + GROUP, TILE, TILE), jnp.bfloat16),
            pltpu.VMEM((2 * SUBLANES, LANES), jnp.float32),
            pltpu.SemaphoreType.DMA,
            pltpu.SemaphoreType.DMA((2, BLK_DEV)),
        ],
        compiler_params=SMALL,
        cost_estimate=pl.CostEstimate(flops=2**22, bytes_accessed=2**22, transcendentals=0),
        name="field",
    )(*operands)


def project_kernel(last, own_ref, halo_ref, members_ref, modes_ref, out_ref):
    m = mode_index()
    halo = halo_ref[...]
    row = lax.broadcasted_iota(jnp.int32, (OWN_TILES, LANES), 0)
    takes = ((row == 0) & (m == 0)) | ((row == OWN_TILES - 1) & (m == last))
    weights = own_ref[...] + jnp.where(takes, halo, 0.0)
    contract = (((1,), (1,)), ((), ()))
    highs, lows = [], []
    for j in range(OWN_TILES):
        cells = slice(j * TILE, (j + 1) * TILE)
        high, low = split2(members_ref[:, cells].astype(jnp.float32) * weights[j : j + 1, :])
        highs.append(high)
        lows.append(low)
    modes = modes_ref[...]
    total = lax.dot_general(modes, jnp.concatenate(highs, 1), contract, preferred_element_type=jnp.float32)
    total += lax.dot_general(modes, jnp.concatenate(lows, 1), contract, preferred_element_type=jnp.float32)
    out_ref[...] = jnp.zeros_like(out_ref)
    out_ref[:, 0:MEMBERS] = total


def project(own, halo, members, modes, last):
    return pl.pallas_call(
        functools.partial(project_kernel, last),
        out_shape=jax.ShapeDtypeStruct((MODES, LANES), jnp.float32),
        in_specs=[VMEM] * 4,
        out_specs=VMEM,
        compiler_params=SMALL,
        name="project",
    )(own, halo, members, modes)


def finish_kernel(total_count, coeff_ref, members_ref, modes_ref, inc_ref, own_ref):
    m = mode_index()
    coeff = coeff_ref[:, 0:MEMBERS]
    own_ref[...] = coeff_ref[pl.ds(m * MODE_DEV, MODE_DEV), 0:MEMBERS]
    spread = jnp.sum(jnp.sum(coeff * coeff, axis=0, keepdims=True), axis=1, keepdims=True)
    factor = lax.rsqrt(1.0 + spread / total_count)
    both = jnp.concatenate(split2(coeff), axis=1)
    members = members_ref[...]
    mixed = jnp.dot(both, jnp.concatenate([members, members], axis=0), preferred_element_type=jnp.float32)
    mixed = mixed * modes_ref[...].astype(jnp.float32)
    summed = jnp.sum(mixed, axis=0, keepdims=True) * (factor / (MEMBERS - 1))
    for j in range(OWN_TILES):
        inc_ref[j : j + 1, :] = summed[:, j * TILE : (j + 1) * TILE]


def finish(coeff, members, modes):
    return pl.pallas_call(
        functools.partial(finish_kernel, MEMBERS * MODES),
        out_shape=(
            jax.ShapeDtypeStruct((OWN_TILES, LANES), jnp.float32),
            jax.ShapeDtypeStruct((MODE_DEV, MEMBERS), jnp.float32),
        ),
        in_specs=[VMEM] * 3,
        out_specs=(VMEM, VMEM),
        compiler_params=SMALL,
        name="finish",
    )(coeff, members, modes)


def exchange(x, axis):
    return lax.all_to_all(x, axis, split_axis=0, concat_axis=0, tiled=True)


def everywhere(x, axis):
    return exchange(jnp.broadcast_to(x[None], (lax.axis_size(axis),) + x.shape), axis)


def on_device(members, modes, obs_weights, innovations, tile_start):
    mode_count = lax.axis_size(MODE)
    space_count = lax.axis_size(SPACE)
    last = mode_count - 1
    all_modes = lax.all_to_all(modes, MODE, split_axis=1, concat_axis=0, tiled=True)
    own, halo = field(tile_start, innovations, obs_weights, last)
    route = []
    for s in range(space_count):
        behind, ahead = (s - 1) % space_count, (s + 1) % space_count
        route.append((s * mode_count, behind * mode_count + last))
        route.append((s * mode_count + last, ahead * mode_count))
    halo = lax.ppermute(halo, SPACE + MODE, route)
    terms = project(own, halo, members, all_modes, last)
    ring = lax.axis_size(RING)
    part = jnp.sum(exchange(terms.reshape(ring, MODES // ring, LANES), RING), axis=0)
    part = jnp.sum(everywhere(part, "y"), axis=0)
    part = jnp.sum(everywhere(part, "z"), axis=0)
    coeff = everywhere(part, RING)
    increment, own_coeff = finish(coeff.reshape(MODES, LANES), members, all_modes)
    return increment.reshape(OWN), own_coeff.T


def solution(mesh):
    finer = Mesh(mesh.devices.reshape(8, 2, 2, 8, 2), SPACE + MODE)
    in_specs = (P(None, SPACE + MODE), P(MODE, SPACE), P(SPACE, None, None), P(SPACE, None), P(SPACE))
    out_specs = (P(SPACE + MODE), P(None, MODE))
    return jax.shard_map(
        on_device, mesh=finer, in_specs=in_specs, out_specs=out_specs, check_vma=False
    )
```

```python
import functools

import jax
import jax.numpy as jnp
from jax import lax
from jax.experimental import pallas as pl
from jax.experimental.pallas import tpu as pltpu
from jax.sharding import Mesh
from jax.sharding import PartitionSpec as P

MEMBERS = 80
MODE_DEV = 4
MODES = 128
CELLS_DEV = 32768
TILE = 128
BLK_DEV = 128
OWN = 1024
OWN_TILES = OWN // TILE
LANES = 128
SUBLANES = 8
GROUP = 4
PIECE = 16
VMEM = pl.BlockSpec(memory_space=pltpu.VMEM)
SMALL = pltpu.CompilerParams(vmem_limit_bytes=12 * 2**20)
MODE = ("xhi", "zhi", "zlo", "core")
SPACE = ("y", "xlo")
NEAR = ("xlo", "xhi", "zlo", "core")
FAR = ("y", "zhi")


def mode_index():
    at = lax.axis_index(MODE[0])
    for axis in MODE[1:]:
        at = at * lax.axis_size(axis) + lax.axis_index(axis)
    return at


def split2(x):
    high = x.astype(jnp.bfloat16)
    return high, (x - high.astype(jnp.float32)).astype(jnp.bfloat16)


def field_kernel(last, begin_ref, innov_ref, obs_ref, own_ref, halo_ref, start_ref, ids, rows, held, acc, halo, begin_sem, row_sem, sems):
    m = mode_index()
    begin = pltpu.make_async_copy(begin_ref, start_ref, begin_sem)
    begin.start()
    pieces = [
        pltpu.make_async_copy(obs_ref.at[pl.ds(i * PIECE, PIECE)], held.at[pl.ds(i * PIECE, PIECE)], sems.at[i])
        for i in range(BLK_DEV // PIECE)
    ]
    pieces.append(pltpu.make_async_copy(innov_ref, rows, row_sem))
    for piece in pieces:
        piece.start()
    base = m * OWN
    first = jnp.where(m == 0, CELLS_DEV + TILE, 0)
    edge = (m == 0) | (m == last)
    acc[...] = jnp.zeros_like(acc)
    halo[...] = jnp.zeros_like(halo)
    begin.wait()

    def scan(b, count):
        start = start_ref[b]
        place = start - base
        far = start - first
        ids[count] = b
        hit = ((place > 0) & (place < OWN + TILE)) | (edge & (far > -TILE) & (far < TILE))
        return count + jnp.where(hit, 1, 0)

    count = lax.fori_loop(0, BLK_DEV, scan, jnp.int32(0), unroll=16)
    lane = lax.broadcasted_iota(jnp.int32, (1, LANES), 1)
    for piece in pieces:
        piece.wait()

    def add(g, carry):
        found = []
        for u in range(GROUP):
            i = g * GROUP + u
            valid = i < count
            b = jnp.where(valid, ids[i], 0)
            start = start_ref[b]
            row = rows[pl.ds(b, 1), :]
            high = row.astype(jnp.bfloat16).astype(jnp.float32)
            mid = (row - high).astype(jnp.bfloat16).astype(jnp.float32)
            low = row - high - mid
            parts = jnp.concatenate([high, mid, low, jnp.zeros((SUBLANES - 3, LANES), jnp.float32)], axis=0)
            adj = jnp.dot(parts.astype(jnp.bfloat16), held[b], preferred_element_type=jnp.float32)
            adj = adj + pltpu.roll(adj, SUBLANES - 1, 0) + pltpu.roll(adj, SUBLANES - 2, 0)
            off = lax.bitwise_and(start, TILE - 1)
            rolled = pltpu.roll(adj, off, 1)[0:1, :]
            front = jnp.where(lane >= off, rolled, 0.0)
            back = jnp.where(lane < off, rolled, 0.0)
            found.append((valid, start - base, start - first, front, back))
        for valid, place, far, front, back in found:

            @pl.when(valid & (place > 0) & (place < OWN + TILE))
            def _():
                seg = lax.shift_right_logical(place, 7)
                acc[pl.ds(seg, 1), :] += front
                acc[pl.ds(seg + 1, 1), :] += back

            @pl.when(valid & edge & (far > -TILE) & (far < TILE))
            def _():
                halo[...] += jnp.where(far >= 0, front, back)

        return carry

    lax.fori_loop(0, lax.shift_right_logical(count + GROUP - 1, 2), add, 0)
    own_ref[...] = acc[1 : 1 + OWN_TILES, :]
    halo_ref[...] = halo[...]


def field(tile_start, innovations, obs_weights, last):
    kept = [pltpu.with_memory_space_constraint(x, pltpu.HBM) for x in (tile_start, innovations, obs_weights)]
    return pl.pallas_call(
        functools.partial(field_kernel, last),
        out_shape=(
            jax.ShapeDtypeStruct((OWN_TILES, LANES), jnp.float32),
            jax.ShapeDtypeStruct((1, LANES), jnp.float32),
        ),
        in_specs=[pl.BlockSpec(memory_space=pltpu.HBM)] * 3,
        out_specs=(VMEM, VMEM),
        scratch_shapes=[
            pltpu.SMEM((BLK_DEV,), jnp.int32),
            pltpu.SMEM((BLK_DEV + GROUP,), jnp.int32),
            pltpu.VMEM((BLK_DEV, LANES), jnp.float32),
            pltpu.VMEM((BLK_DEV, TILE, TILE), jnp.bfloat16),
            pltpu.VMEM((2 * SUBLANES, LANES), jnp.float32),
            pltpu.VMEM((1, LANES), jnp.float32),
            pltpu.SemaphoreType.DMA,
            pltpu.SemaphoreType.DMA,
            pltpu.SemaphoreType.DMA((BLK_DEV // PIECE,)),
        ],
        compiler_params=SMALL,
        cost_estimate=pl.CostEstimate(flops=2**22, bytes_accessed=2**22, transcendentals=0),
        name="field",
    )(*kept)


def project_kernel(last, own_ref, halo_ref, members_ref, modes_ref, out_ref):
    m = mode_index()
    halo = halo_ref[...]
    row = lax.broadcasted_iota(jnp.int32, (OWN_TILES, LANES), 0)
    takes = ((row == 0) & (m == 0)) | ((row == OWN_TILES - 1) & (m == last))
    weights = own_ref[...] + jnp.where(takes, halo, 0.0)
    contract = (((1,), (1,)), ((), ()))
    highs, lows = [], []
    for j in range(OWN_TILES):
        cells = slice(j * TILE, (j + 1) * TILE)
        high, low = split2(members_ref[:, cells].astype(jnp.float32) * weights[j : j + 1, :])
        highs.append(high)
        lows.append(low)
    modes = modes_ref[...]
    total = lax.dot_general(modes, jnp.concatenate(highs, 1), contract, preferred_element_type=jnp.float32)
    total += lax.dot_general(modes, jnp.concatenate(lows, 1), contract, preferred_element_type=jnp.float32)
    out_ref[...] = jnp.zeros_like(out_ref)
    out_ref[:, 0:MEMBERS] = total


def project(own, halo, members, modes, last):
    return pl.pallas_call(
        functools.partial(project_kernel, last),
        out_shape=jax.ShapeDtypeStruct((MODES, LANES), jnp.float32),
        in_specs=[VMEM] * 4,
        out_specs=VMEM,
        compiler_params=SMALL,
        name="project",
    )(own, halo, members, modes)


def finish_kernel(total_count, coeff_ref, members_ref, modes_ref, inc_ref, own_ref):
    m = mode_index()
    coeff = coeff_ref[:, 0:MEMBERS]
    own_ref[...] = coeff_ref[pl.ds(m * MODE_DEV, MODE_DEV), 0:MEMBERS]
    spread = jnp.sum(jnp.sum(coeff * coeff, axis=0, keepdims=True), axis=1, keepdims=True)
    factor = lax.rsqrt(1.0 + spread / total_count)
    both = jnp.concatenate(split2(coeff), axis=1)
    members = members_ref[...]
    mixed = jnp.dot(both, jnp.concatenate([members, members], axis=0), preferred_element_type=jnp.float32)
    mixed = mixed * modes_ref[...].astype(jnp.float32)
    summed = jnp.sum(mixed, axis=0, keepdims=True) * (factor / (MEMBERS - 1))
    for j in range(OWN_TILES):
        inc_ref[j : j + 1, :] = summed[:, j * TILE : (j + 1) * TILE]


def finish(coeff, members, modes):
    return pl.pallas_call(
        functools.partial(finish_kernel, MEMBERS * MODES),
        out_shape=(
            jax.ShapeDtypeStruct((OWN_TILES, LANES), jnp.float32),
            jax.ShapeDtypeStruct((MODE_DEV, MEMBERS), jnp.float32),
        ),
        in_specs=[VMEM] * 3,
        out_specs=(VMEM, VMEM),
        compiler_params=SMALL,
        name="finish",
    )(coeff, members, modes)


def exchange(x, axis):
    return lax.all_to_all(x, axis, split_axis=0, concat_axis=0, tiled=True)


def everywhere(x, axis):
    return exchange(jnp.broadcast_to(x[None], (lax.axis_size(axis),) + x.shape), axis)


def on_device(members, modes, obs_weights, innovations, tile_start):
    mode_count = lax.axis_size(MODE)
    space_count = lax.axis_size(SPACE)
    last = mode_count - 1
    all_modes = lax.all_to_all(modes, MODE, split_axis=1, concat_axis=0, tiled=True)
    own, halo = field(tile_start, innovations, obs_weights, last)
    route = []
    for s in range(space_count):
        behind, ahead = (s - 1) % space_count, (s + 1) % space_count
        route.append((s * mode_count, ahead * mode_count))
        route.append((s * mode_count + last, behind * mode_count + last))
    halo = lax.ppermute(halo, SPACE + MODE, route)
    terms = project(own, halo, members, all_modes, last)
    near = lax.axis_size(NEAR)
    part = jnp.sum(exchange(terms.reshape(near, MODES // near, LANES), NEAR), axis=0)
    part = jnp.sum(everywhere(part, FAR), axis=0)
    coeff = everywhere(part, NEAR)
    increment, own_coeff = finish(coeff.reshape(MODES, LANES), members, all_modes)
    return increment.reshape(OWN), own_coeff.T


def solution(mesh):
    finer = Mesh(mesh.devices.reshape(8, 2, 2, 4, 2, 2), SPACE + MODE)
    in_specs = (P(None, SPACE + MODE), P(MODE, SPACE), P(SPACE, None, None), P(SPACE, None), P(SPACE))
    out_specs = (P(SPACE + MODE), P(None, MODE))
    return jax.shard_map(
        on_device, mesh=finer, in_specs=in_specs, out_specs=out_specs, check_vma=False
    )
```

```python
import functools

import jax
import jax.numpy as jnp
from jax import lax
from jax.experimental import pallas as pl
from jax.experimental.pallas import tpu as pltpu
from jax.sharding import Mesh
from jax.sharding import PartitionSpec as P

MEMBERS = 80
MODE_DEV = 4
MODES = 128
CELLS_DEV = 32768
TILE = 128
BLK_DEV = 128
OWN = 1024
OWN_TILES = OWN // TILE
LANES = 128
SUBLANES = 8
GROUP = 4
PIECE = 16
VMEM = pl.BlockSpec(memory_space=pltpu.VMEM)
SMALL = pltpu.CompilerParams(vmem_limit_bytes=12 * 2**20)
MODE = ("xhi", "zhi", "zlo", "core")
SPACE = ("y", "xlo")
NEAR = ("xlo", "xhi", "zlo", "core")
FAR = ("y", "zhi")


def mode_index():
    at = lax.axis_index(MODE[0])
    for axis in MODE[1:]:
        at = at * lax.axis_size(axis) + lax.axis_index(axis)
    return at


def split2(x):
    high = x.astype(jnp.bfloat16)
    return high, (x - high.astype(jnp.float32)).astype(jnp.bfloat16)


def field_kernel(last, begin_ref, innov_ref, obs_ref, own_ref, halo_ref, start_ref, ids, rows, held, acc, halo, begin_sem, row_sem, sems):
    m = mode_index()
    begin = pltpu.make_async_copy(begin_ref, start_ref, begin_sem)
    begin.start()
    pieces = [
        pltpu.make_async_copy(obs_ref.at[pl.ds(i * PIECE, PIECE)], held.at[pl.ds(i * PIECE, PIECE)], sems.at[i])
        for i in range(BLK_DEV // PIECE)
    ]
    pieces.append(pltpu.make_async_copy(innov_ref, rows, row_sem))
    for piece in pieces:
        piece.start()
    base = m * OWN
    first = jnp.where(m == 0, CELLS_DEV + TILE, 0)
    edge = (m == 0) | (m == last)
    acc[...] = jnp.zeros_like(acc)
    halo[...] = jnp.zeros_like(halo)
    begin.wait()

    def scan(b, count):
        start = start_ref[b]
        place = start - base
        far = start - first
        ids[count] = b
        hit = ((place > 0) & (place < OWN + TILE)) | (edge & (far > -TILE) & (far < TILE))
        return count + jnp.where(hit, 1, 0)

    count = lax.fori_loop(0, BLK_DEV, scan, jnp.int32(0), unroll=16)
    lane = lax.broadcasted_iota(jnp.int32, (1, LANES), 1)
    for piece in pieces:
        piece.wait()

    def add(g, carry):
        found = []
        for u in range(GROUP):
            i = g * GROUP + u
            valid = i < count
            b = jnp.where(valid, ids[i], 0)
            start = start_ref[b]
            row = rows[pl.ds(b, 1), :]
            high = row.astype(jnp.bfloat16).astype(jnp.float32)
            mid = (row - high).astype(jnp.bfloat16).astype(jnp.float32)
            low = row - high - mid
            parts = jnp.concatenate([high, mid, low, jnp.zeros((SUBLANES - 3, LANES), jnp.float32)], axis=0)
            adj = jnp.dot(parts.astype(jnp.bfloat16), held[b], preferred_element_type=jnp.float32)
            adj = adj + pltpu.roll(adj, SUBLANES - 1, 0) + pltpu.roll(adj, SUBLANES - 2, 0)
            off = lax.bitwise_and(start, TILE - 1)
            rolled = pltpu.roll(adj, off, 1)[0:1, :]
            front = jnp.where(lane >= off, rolled, 0.0)
            back = jnp.where(lane < off, rolled, 0.0)
            found.append((valid, start - base, start - first, front, back))
        for valid, place, far, front, back in found:

            @pl.when(valid & (place > 0) & (place < OWN + TILE))
            def _():
                seg = lax.shift_right_logical(place, 7)
                acc[pl.ds(seg, 1), :] += front
                acc[pl.ds(seg + 1, 1), :] += back

            @pl.when(valid & edge & (far > -TILE) & (far < TILE))
            def _():
                halo[...] += jnp.where(far >= 0, front, back)

        return carry

    lax.fori_loop(0, lax.shift_right_logical(count + GROUP - 1, 2), add, 0)
    own_ref[...] = acc[1 : 1 + OWN_TILES, :]
    halo_ref[...] = halo[...]


def field(tile_start, innovations, obs_weights, last):
    kept = [pltpu.with_memory_space_constraint(x, pltpu.HBM) for x in (tile_start, innovations, obs_weights)]
    return pl.pallas_call(
        functools.partial(field_kernel, last),
        out_shape=(
            jax.ShapeDtypeStruct((OWN_TILES, LANES), jnp.float32),
            jax.ShapeDtypeStruct((1, LANES), jnp.float32),
        ),
        in_specs=[pl.BlockSpec(memory_space=pltpu.HBM)] * 3,
        out_specs=(VMEM, VMEM),
        scratch_shapes=[
            pltpu.SMEM((BLK_DEV,), jnp.int32),
            pltpu.SMEM((BLK_DEV + GROUP,), jnp.int32),
            pltpu.VMEM((BLK_DEV, LANES), jnp.float32),
            pltpu.VMEM((BLK_DEV, TILE, TILE), jnp.bfloat16),
            pltpu.VMEM((2 * SUBLANES, LANES), jnp.float32),
            pltpu.VMEM((1, LANES), jnp.float32),
            pltpu.SemaphoreType.DMA,
            pltpu.SemaphoreType.DMA,
            pltpu.SemaphoreType.DMA((BLK_DEV // PIECE,)),
        ],
        compiler_params=SMALL,
        cost_estimate=pl.CostEstimate(flops=2**22, bytes_accessed=2**22, transcendentals=0),
        name="field",
    )(*kept)


def project_kernel(last, chunks, rows, own_ref, halo_ref, members_ref, modes_ref, out_ref):
    m = mode_index()
    halo = halo_ref[...]
    row = lax.broadcasted_iota(jnp.int32, (OWN_TILES, LANES), 0)
    takes = ((row == 0) & (m == 0)) | ((row == OWN_TILES - 1) & (m == last))
    weights = own_ref[...] + jnp.where(takes, halo, 0.0)
    contract = (((1,), (1,)), ((), ()))
    highs, lows = [], []
    for j in range(OWN_TILES):
        cells = slice(j * TILE, (j + 1) * TILE)
        high, low = split2(members_ref[:, cells].astype(jnp.float32) * weights[j : j + 1, :])
        highs.append(high)
        lows.append(low)
    modes = modes_ref[...]
    total = lax.dot_general(jnp.concatenate(highs, 1), modes, contract, preferred_element_type=jnp.float32)
    total += lax.dot_general(jnp.concatenate(lows, 1), modes, contract, preferred_element_type=jnp.float32)
    out_ref[...] = jnp.zeros_like(out_ref)
    for c in range(chunks):
        out_ref[c, 0:rows, :] = total[c * rows : (c + 1) * rows, :]


def project(own, halo, members, modes, last, chunks):
    return pl.pallas_call(
        functools.partial(project_kernel, last, chunks, MEMBERS // chunks),
        out_shape=jax.ShapeDtypeStruct((chunks, SUBLANES, LANES), jnp.float32),
        in_specs=[VMEM] * 4,
        out_specs=VMEM,
        compiler_params=SMALL,
        name="project",
    )(own, halo, members, modes)


def finish_kernel(total_count, chunks, rows, coeff_ref, members_ref, modes_ref, inc_ref, own_ref, turned):
    m = mode_index()
    coeff = jnp.concatenate([coeff_ref[c, 0:rows, :] for c in range(chunks)], axis=0).T
    turned[...] = coeff
    own_ref[...] = turned[pl.ds(m * MODE_DEV, MODE_DEV), :]
    spread = jnp.sum(jnp.sum(coeff * coeff, axis=0, keepdims=True), axis=1, keepdims=True)
    factor = lax.rsqrt(1.0 + spread / total_count)
    both = jnp.concatenate(split2(coeff), axis=1)
    members = members_ref[...]
    mixed = jnp.dot(both, jnp.concatenate([members, members], axis=0), preferred_element_type=jnp.float32)
    mixed = mixed * modes_ref[...].astype(jnp.float32)
    summed = jnp.sum(mixed, axis=0, keepdims=True) * (factor / (MEMBERS - 1))
    for j in range(OWN_TILES):
        inc_ref[j : j + 1, :] = summed[:, j * TILE : (j + 1) * TILE]


def finish(coeff, members, modes):
    return pl.pallas_call(
        functools.partial(finish_kernel, MEMBERS * MODES, coeff.shape[0], MEMBERS // coeff.shape[0]),
        out_shape=(
            jax.ShapeDtypeStruct((OWN_TILES, LANES), jnp.float32),
            jax.ShapeDtypeStruct((MODE_DEV, MEMBERS), jnp.float32),
        ),
        in_specs=[VMEM] * 3,
        out_specs=(VMEM, VMEM),
        scratch_shapes=[pltpu.VMEM((MODES, MEMBERS), jnp.float32)],
        compiler_params=SMALL,
        name="finish",
    )(coeff, members, modes)


def exchange(x, axis):
    return lax.all_to_all(x, axis, split_axis=0, concat_axis=0, tiled=True)


def everywhere(x, axis):
    return exchange(jnp.broadcast_to(x[None], (lax.axis_size(axis),) + x.shape), axis)


def on_device(members, modes, obs_weights, innovations, tile_start):
    mode_count = lax.axis_size(MODE)
    space_count = lax.axis_size(SPACE)
    last = mode_count - 1
    all_modes = lax.all_to_all(modes, MODE, split_axis=1, concat_axis=0, tiled=True)
    own, halo = field(tile_start, innovations, obs_weights, last)
    route = []
    for s in range(space_count):
        behind, ahead = (s - 1) % space_count, (s + 1) % space_count
        route.append((s * mode_count, ahead * mode_count))
        route.append((s * mode_count + last, behind * mode_count + last))
    halo = lax.ppermute(halo, SPACE + MODE, route)
    near = lax.axis_size(NEAR)
    rows = MEMBERS // near
    terms = project(own, halo, members, all_modes, last, near)
    part = jnp.sum(exchange(terms, NEAR), axis=0)[:rows]
    part = jnp.sum(everywhere(part.reshape(1, rows * LANES), FAR), axis=0)
    part = jnp.pad(part.reshape(rows, LANES), ((0, SUBLANES - rows), (0, 0)))
    increment, own_coeff = finish(everywhere(part, NEAR), members, all_modes)
    return increment.reshape(OWN), own_coeff.T


def solution(mesh):
    finer = Mesh(mesh.devices.reshape(8, 2, 2, 4, 2, 2), SPACE + MODE)
    in_specs = (P(None, SPACE + MODE), P(MODE, SPACE), P(SPACE, None, None), P(SPACE, None), P(SPACE))
    out_specs = (P(SPACE + MODE), P(None, MODE))
    return jax.shard_map(
        on_device, mesh=finer, in_specs=in_specs, out_specs=out_specs, check_vma=False
    )
```

```python
import functools

import jax
import jax.numpy as jnp
from jax import lax
from jax.experimental import pallas as pl
from jax.experimental.pallas import tpu as pltpu
from jax.sharding import Mesh
from jax.sharding import PartitionSpec as P

MEMBERS = 80
MODE_DEV = 4
MODES = 128
CELLS_DEV = 32768
TILE = 128
BLK_DEV = 128
OWN = 1024
OWN_TILES = OWN // TILE
LANES = 128
SUBLANES = 8
GROUP = 4
PIECE = 16
VMEM = pl.BlockSpec(memory_space=pltpu.VMEM)
SMALL = pltpu.CompilerParams(vmem_limit_bytes=12 * 2**20)
MODE = ("xhi", "zhi", "zlo", "core")
SPACE = ("y", "xlo")
NEAR = ("xlo", "xhi", "zlo", "core")
FAR = ("y", "zhi")


def mode_index():
    at = lax.axis_index(MODE[0])
    for axis in MODE[1:]:
        at = at * lax.axis_size(axis) + lax.axis_index(axis)
    return at


def split2(x):
    high = x.astype(jnp.bfloat16)
    return high, (x - high.astype(jnp.float32)).astype(jnp.bfloat16)


def field_kernel(last, begin_ref, innov_ref, obs_ref, own_ref, halo_ref, start_ref, ids, rows, held, acc, halo, begin_sem, row_sem, sems):
    m = mode_index()
    begin = pltpu.make_async_copy(begin_ref, start_ref, begin_sem)
    begin.start()
    pieces = [
        pltpu.make_async_copy(obs_ref.at[pl.ds(i * PIECE, PIECE)], held.at[pl.ds(i * PIECE, PIECE)], sems.at[i])
        for i in range(BLK_DEV // PIECE)
    ]
    pieces.append(pltpu.make_async_copy(innov_ref, rows, row_sem))
    for piece in pieces:
        piece.start()
    base = m * OWN
    first = jnp.where(m == 0, CELLS_DEV + TILE, 0)
    edge = (m == 0) | (m == last)
    acc[...] = jnp.zeros_like(acc)
    halo[...] = jnp.zeros_like(halo)
    begin.wait()

    def scan(b, count):
        start = start_ref[b]
        place = start - base
        far = start - first
        ids[count] = b
        hit = ((place > 0) & (place < OWN + TILE)) | (edge & (far > -TILE) & (far < TILE))
        return count + jnp.where(hit, 1, 0)

    count = lax.fori_loop(0, BLK_DEV, scan, jnp.int32(0), unroll=16)
    lane = lax.broadcasted_iota(jnp.int32, (1, LANES), 1)
    for piece in pieces:
        piece.wait()

    def add(g, carry):
        found = []
        for u in range(GROUP):
            i = g * GROUP + u
            valid = i < count
            b = jnp.where(valid, ids[i], 0)
            start = start_ref[b]
            row = rows[pl.ds(b, 1), :]
            high = row.astype(jnp.bfloat16).astype(jnp.float32)
            mid = (row - high).astype(jnp.bfloat16).astype(jnp.float32)
            low = row - high - mid
            parts = jnp.concatenate([high, mid, low, jnp.zeros((SUBLANES - 3, LANES), jnp.float32)], axis=0)
            adj = jnp.dot(parts.astype(jnp.bfloat16), held[b], preferred_element_type=jnp.float32)
            adj = adj + pltpu.roll(adj, SUBLANES - 1, 0) + pltpu.roll(adj, SUBLANES - 2, 0)
            off = lax.bitwise_and(start, TILE - 1)
            rolled = pltpu.roll(adj, off, 1)[0:1, :]
            front = jnp.where(lane >= off, rolled, 0.0)
            back = jnp.where(lane < off, rolled, 0.0)
            found.append((valid, start - base, start - first, front, back))
        for valid, place, far, front, back in found:

            @pl.when(valid & (place > 0) & (place < OWN + TILE))
            def _():
                seg = lax.shift_right_logical(place, 7)
                acc[pl.ds(seg, 1), :] += front
                acc[pl.ds(seg + 1, 1), :] += back

            @pl.when(valid & edge & (far > -TILE) & (far < TILE))
            def _():
                halo[...] += jnp.where(far >= 0, front, back)

        return carry

    lax.fori_loop(0, lax.shift_right_logical(count + GROUP - 1, 2), add, 0)
    own_ref[...] = acc[1 : 1 + OWN_TILES, :]
    halo_ref[...] = halo[...]


def field(tile_start, innovations, obs_weights, last):
    kept = [pltpu.with_memory_space_constraint(x, pltpu.HBM) for x in (tile_start, innovations, obs_weights)]
    return pl.pallas_call(
        functools.partial(field_kernel, last),
        out_shape=(
            jax.ShapeDtypeStruct((OWN_TILES, LANES), jnp.float32),
            jax.ShapeDtypeStruct((1, LANES), jnp.float32),
        ),
        in_specs=[pl.BlockSpec(memory_space=pltpu.HBM)] * 3,
        out_specs=(VMEM, VMEM),
        scratch_shapes=[
            pltpu.SMEM((BLK_DEV,), jnp.int32),
            pltpu.SMEM((BLK_DEV + GROUP,), jnp.int32),
            pltpu.VMEM((BLK_DEV, LANES), jnp.float32),
            pltpu.VMEM((BLK_DEV, TILE, TILE), jnp.bfloat16),
            pltpu.VMEM((2 * SUBLANES, LANES), jnp.float32),
            pltpu.VMEM((1, LANES), jnp.float32),
            pltpu.SemaphoreType.DMA,
            pltpu.SemaphoreType.DMA,
            pltpu.SemaphoreType.DMA((BLK_DEV // PIECE,)),
        ],
        compiler_params=SMALL,
        cost_estimate=pl.CostEstimate(flops=2**22, bytes_accessed=2**22, transcendentals=0),
        name="field",
    )(*kept)


def project_kernel(last, own_ref, halo_ref, members_ref, modes_ref, out_ref):
    m = mode_index()
    halo = halo_ref[...]
    row = lax.broadcasted_iota(jnp.int32, (OWN_TILES, LANES), 0)
    takes = ((row == 0) & (m == 0)) | ((row == OWN_TILES - 1) & (m == last))
    weights = own_ref[...] + jnp.where(takes, halo, 0.0)
    contract = (((1,), (1,)), ((), ()))
    highs, lows = [], []
    for j in range(OWN_TILES):
        cells = slice(j * TILE, (j + 1) * TILE)
        high, low = split2(members_ref[:, cells].astype(jnp.float32) * weights[j : j + 1, :])
        highs.append(high)
        lows.append(low)
    modes = modes_ref[...]
    total = lax.dot_general(jnp.concatenate(highs, 1), modes, contract, preferred_element_type=jnp.float32)
    total += lax.dot_general(jnp.concatenate(lows, 1), modes, contract, preferred_element_type=jnp.float32)
    out_ref[...] = total


def project(own, halo, members, modes, last):
    return pl.pallas_call(
        functools.partial(project_kernel, last),
        out_shape=jax.ShapeDtypeStruct((MEMBERS, MODES), jnp.float32),
        in_specs=[VMEM] * 4,
        out_specs=VMEM,
        compiler_params=SMALL,
        name="project",
    )(own, halo, members, modes)


def finish_kernel(total_count, coeff_ref, members_ref, modes_ref, inc_ref, own_ref, turned):
    m = mode_index()
    coeff = coeff_ref[...].T
    turned[...] = coeff
    own_ref[...] = turned[pl.ds(m * MODE_DEV, MODE_DEV), :]
    spread = jnp.sum(jnp.sum(coeff * coeff, axis=0, keepdims=True), axis=1, keepdims=True)
    factor = lax.rsqrt(1.0 + spread / total_count)
    both = jnp.concatenate(split2(coeff), axis=1)
    members = members_ref[...]
    mixed = jnp.dot(both, jnp.concatenate([members, members], axis=0), preferred_element_type=jnp.float32)
    mixed = mixed * modes_ref[...].astype(jnp.float32)
    summed = jnp.sum(mixed, axis=0, keepdims=True) * (factor / (MEMBERS - 1))
    for j in range(OWN_TILES):
        inc_ref[j : j + 1, :] = summed[:, j * TILE : (j + 1) * TILE]


def finish(coeff, members, modes):
    return pl.pallas_call(
        functools.partial(finish_kernel, MEMBERS * MODES),
        out_shape=(
            jax.ShapeDtypeStruct((OWN_TILES, LANES), jnp.float32),
            jax.ShapeDtypeStruct((MODE_DEV, MEMBERS), jnp.float32),
        ),
        in_specs=[VMEM] * 3,
        out_specs=(VMEM, VMEM),
        scratch_shapes=[pltpu.VMEM((MODES, MEMBERS), jnp.float32)],
        compiler_params=SMALL,
        name="finish",
    )(coeff, members, modes)


def exchange(x, axis):
    return lax.all_to_all(x, axis, split_axis=0, concat_axis=0, tiled=True)


def everywhere(x, axis):
    return exchange(jnp.broadcast_to(x[None], (lax.axis_size(axis),) + x.shape), axis)


def on_device(members, modes, obs_weights, innovations, tile_start):
    mode_count = lax.axis_size(MODE)
    space_count = lax.axis_size(SPACE)
    last = mode_count - 1
    all_modes = lax.all_to_all(modes, MODE, split_axis=1, concat_axis=0, tiled=True)
    own, halo = field(tile_start, innovations, obs_weights, last)
    route = []
    for s in range(space_count):
        behind, ahead = (s - 1) % space_count, (s + 1) % space_count
        route.append((s * mode_count, ahead * mode_count))
        route.append((s * mode_count + last, behind * mode_count + last))
    halo = lax.ppermute(halo, SPACE + MODE, route)
    terms = project(own, halo, members, all_modes, last)
    part = jnp.sum(exchange(terms.reshape(lax.axis_size(NEAR), 1, -1), NEAR), axis=0)
    part = jnp.sum(everywhere(part, FAR), axis=0)
    coeff = everywhere(part, NEAR)
    increment, own_coeff = finish(coeff.reshape(MEMBERS, MODES), members, all_modes)
    return increment.reshape(OWN), own_coeff.T


def solution(mesh):
    finer = Mesh(mesh.devices.reshape(8, 2, 2, 4, 2, 2), SPACE + MODE)
    in_specs = (P(None, SPACE + MODE), P(MODE, SPACE), P(SPACE, None, None), P(SPACE, None), P(SPACE))
    out_specs = (P(SPACE + MODE), P(None, MODE))
    return jax.shard_map(
        on_device, mesh=finer, in_specs=in_specs, out_specs=out_specs, check_vma=False
    )
```

```python
import functools

import jax
import jax.numpy as jnp
from jax import lax
from jax.experimental import pallas as pl
from jax.experimental.pallas import tpu as pltpu
from jax.sharding import Mesh
from jax.sharding import PartitionSpec as P

MEMBERS = 80
MODE_DEV = 4
MODES = 128
CELLS_DEV = 32768
TILE = 128
BLK_DEV = 128
OWN = 1024
OWN_TILES = OWN // TILE
LANES = 128
SUBLANES = 8
GROUP = 4
PIECE = 16
VMEM = pl.BlockSpec(memory_space=pltpu.VMEM)
SMALL = pltpu.CompilerParams(vmem_limit_bytes=12 * 2**20)
MODE = ("xhi", "zhi", "zlo", "core")
SPACE = ("y", "xlo")
NEAR = ("zhi", "zlo", "core")
FAR = ("y", "xlo", "xhi")


def mode_index():
    at = lax.axis_index(MODE[0])
    for axis in MODE[1:]:
        at = at * lax.axis_size(axis) + lax.axis_index(axis)
    return at


def split2(x):
    high = x.astype(jnp.bfloat16)
    return high, (x - high.astype(jnp.float32)).astype(jnp.bfloat16)


def field_kernel(last, begin_ref, innov_ref, obs_ref, own_ref, halo_ref, start_ref, ids, rows, held, acc, halo, begin_sem, row_sem, sems):
    m = mode_index()
    begin = pltpu.make_async_copy(begin_ref, start_ref, begin_sem)
    begin.start()
    pieces = [
        pltpu.make_async_copy(obs_ref.at[pl.ds(i * PIECE, PIECE)], held.at[pl.ds(i * PIECE, PIECE)], sems.at[i])
        for i in range(BLK_DEV // PIECE)
    ]
    pieces.append(pltpu.make_async_copy(innov_ref, rows, row_sem))
    for piece in pieces:
        piece.start()
    base = m * OWN
    first = jnp.where(m == 0, CELLS_DEV + TILE, 0)
    edge = (m == 0) | (m == last)
    acc[...] = jnp.zeros_like(acc)
    halo[...] = jnp.zeros_like(halo)
    begin.wait()

    def scan(b, count):
        start = start_ref[b]
        place = start - base
        far = start - first
        ids[count] = b
        hit = ((place > 0) & (place < OWN + TILE)) | (edge & (far > -TILE) & (far < TILE))
        return count + jnp.where(hit, 1, 0)

    count = lax.fori_loop(0, BLK_DEV, scan, jnp.int32(0), unroll=16)
    lane = lax.broadcasted_iota(jnp.int32, (1, LANES), 1)
    for piece in pieces:
        piece.wait()

    def add(g, carry):
        found = []
        for u in range(GROUP):
            i = g * GROUP + u
            valid = i < count
            b = jnp.where(valid, ids[i], 0)
            start = start_ref[b]
            row = rows[pl.ds(b, 1), :]
            high = row.astype(jnp.bfloat16).astype(jnp.float32)
            mid = (row - high).astype(jnp.bfloat16).astype(jnp.float32)
            low = row - high - mid
            parts = jnp.concatenate([high, mid, low, jnp.zeros((SUBLANES - 3, LANES), jnp.float32)], axis=0)
            adj = jnp.dot(parts.astype(jnp.bfloat16), held[b], preferred_element_type=jnp.float32)
            adj = adj + pltpu.roll(adj, SUBLANES - 1, 0) + pltpu.roll(adj, SUBLANES - 2, 0)
            off = lax.bitwise_and(start, TILE - 1)
            rolled = pltpu.roll(adj, off, 1)[0:1, :]
            front = jnp.where(lane >= off, rolled, 0.0)
            back = jnp.where(lane < off, rolled, 0.0)
            found.append((valid, start - base, start - first, front, back))
        for valid, place, far, front, back in found:

            @pl.when(valid & (place > 0) & (place < OWN + TILE))
            def _():
                seg = lax.shift_right_logical(place, 7)
                acc[pl.ds(seg, 1), :] += front
                acc[pl.ds(seg + 1, 1), :] += back

            @pl.when(valid & edge & (far > -TILE) & (far < TILE))
            def _():
                halo[...] += jnp.where(far >= 0, front, back)

        return carry

    lax.fori_loop(0, lax.shift_right_logical(count + GROUP - 1, 2), add, 0)
    own_ref[...] = acc[1 : 1 + OWN_TILES, :]
    halo_ref[...] = halo[...]


def field(tile_start, innovations, obs_weights, last):
    kept = [pltpu.with_memory_space_constraint(x, pltpu.HBM) for x in (tile_start, innovations, obs_weights)]
    return pl.pallas_call(
        functools.partial(field_kernel, last),
        out_shape=(
            jax.ShapeDtypeStruct((OWN_TILES, LANES), jnp.float32),
            jax.ShapeDtypeStruct((1, LANES), jnp.float32),
        ),
        in_specs=[pl.BlockSpec(memory_space=pltpu.HBM)] * 3,
        out_specs=(VMEM, VMEM),
        scratch_shapes=[
            pltpu.SMEM((BLK_DEV,), jnp.int32),
            pltpu.SMEM((BLK_DEV + GROUP,), jnp.int32),
            pltpu.VMEM((BLK_DEV, LANES), jnp.float32),
            pltpu.VMEM((BLK_DEV, TILE, TILE), jnp.bfloat16),
            pltpu.VMEM((2 * SUBLANES, LANES), jnp.float32),
            pltpu.VMEM((1, LANES), jnp.float32),
            pltpu.SemaphoreType.DMA,
            pltpu.SemaphoreType.DMA,
            pltpu.SemaphoreType.DMA((BLK_DEV // PIECE,)),
        ],
        compiler_params=SMALL,
        cost_estimate=pl.CostEstimate(flops=2**22, bytes_accessed=2**22, transcendentals=0),
        name="field",
    )(*kept)


def project_kernel(last, own_ref, halo_ref, members_ref, modes_ref, out_ref):
    m = mode_index()
    halo = halo_ref[...]
    row = lax.broadcasted_iota(jnp.int32, (OWN_TILES, LANES), 0)
    takes = ((row == 0) & (m == 0)) | ((row == OWN_TILES - 1) & (m == last))
    weights = own_ref[...] + jnp.where(takes, halo, 0.0)
    contract = (((1,), (1,)), ((), ()))
    highs, lows = [], []
    for j in range(OWN_TILES):
        cells = slice(j * TILE, (j + 1) * TILE)
        high, low = split2(members_ref[:, cells].astype(jnp.float32) * weights[j : j + 1, :])
        highs.append(high)
        lows.append(low)
    modes = modes_ref[...]
    total = lax.dot_general(jnp.concatenate(highs, 1), modes, contract, preferred_element_type=jnp.float32)
    total += lax.dot_general(jnp.concatenate(lows, 1), modes, contract, preferred_element_type=jnp.float32)
    out_ref[...] = total


def project(own, halo, members, modes, last):
    return pl.pallas_call(
        functools.partial(project_kernel, last),
        out_shape=jax.ShapeDtypeStruct((MEMBERS, MODES), jnp.float32),
        in_specs=[VMEM] * 4,
        out_specs=VMEM,
        compiler_params=SMALL,
        name="project",
    )(own, halo, members, modes)


def finish_kernel(total_count, coeff_ref, members_ref, modes_ref, inc_ref, own_ref, turned):
    m = mode_index()
    coeff = coeff_ref[...]
    high, low = split2(coeff)
    modes = modes_ref[...]
    mixed = jnp.dot(high, modes, preferred_element_type=jnp.float32)
    mixed += jnp.dot(low, modes, preferred_element_type=jnp.float32)
    spread = jnp.sum(jnp.sum(coeff * coeff, axis=0, keepdims=True), axis=1, keepdims=True)
    factor = lax.rsqrt(1.0 + spread / total_count)
    turned[...] = coeff.T
    own_ref[...] = turned[pl.ds(m * MODE_DEV, MODE_DEV), :]
    mixed = mixed * members_ref[...].astype(jnp.float32)
    summed = jnp.sum(mixed, axis=0, keepdims=True) * (factor / (MEMBERS - 1))
    for j in range(OWN_TILES):
        inc_ref[j : j + 1, :] = summed[:, j * TILE : (j + 1) * TILE]


def finish(coeff, members, modes):
    return pl.pallas_call(
        functools.partial(finish_kernel, MEMBERS * MODES),
        out_shape=(
            jax.ShapeDtypeStruct((OWN_TILES, LANES), jnp.float32),
            jax.ShapeDtypeStruct((MODE_DEV, MEMBERS), jnp.float32),
        ),
        in_specs=[VMEM] * 3,
        out_specs=(VMEM, VMEM),
        scratch_shapes=[pltpu.VMEM((MODES, MEMBERS), jnp.float32)],
        compiler_params=SMALL,
        name="finish",
    )(coeff, members, modes)


def exchange(x, axis):
    return lax.all_to_all(x, axis, split_axis=0, concat_axis=0, tiled=True)


def everywhere(x, axis):
    return exchange(jnp.broadcast_to(x[None], (lax.axis_size(axis),) + x.shape), axis)


def on_device(members, modes, obs_weights, innovations, tile_start):
    mode_count = lax.axis_size(MODE)
    space_count = lax.axis_size(SPACE)
    last = mode_count - 1
    all_modes = lax.all_to_all(modes, MODE, split_axis=1, concat_axis=0, tiled=True)
    own, halo = field(tile_start, innovations, obs_weights, last)
    route = []
    for s in range(space_count):
        behind, ahead = (s - 1) % space_count, (s + 1) % space_count
        route.append((s * mode_count, ahead * mode_count))
        route.append((s * mode_count + last, behind * mode_count + last))
    halo = lax.ppermute(halo, SPACE + MODE, route)
    terms = project(own, halo, members, all_modes, last)
    part = jnp.sum(exchange(terms.reshape(lax.axis_size(NEAR), 1, -1), NEAR), axis=0)
    part = jnp.sum(everywhere(part, FAR), axis=0)
    coeff = everywhere(part, NEAR)
    increment, own_coeff = finish(coeff.reshape(MEMBERS, MODES), members, all_modes)
    return increment.reshape(OWN), own_coeff.T


def solution(mesh):
    finer = Mesh(mesh.devices.reshape(8, 2, 2, 4, 2, 2), SPACE + MODE)
    in_specs = (P(None, SPACE + MODE), P(MODE, SPACE), P(SPACE, None, None), P(SPACE, None), P(SPACE))
    out_specs = (P(SPACE + MODE), P(None, MODE))
    return jax.shard_map(
        on_device, mesh=finer, in_specs=in_specs, out_specs=out_specs, check_vma=False
    )
```

```python
import functools

import jax
import jax.numpy as jnp
from jax import lax
from jax.experimental import pallas as pl
from jax.experimental.pallas import tpu as pltpu
from jax.sharding import Mesh
from jax.sharding import PartitionSpec as P

MEMBERS = 80
MODE_DEV = 4
MODES = 128
CELLS_DEV = 32768
TILE = 128
BLK_DEV = 128
OWN = 1024
OWN_TILES = OWN // TILE
LANES = 128
SUBLANES = 8
GROUP = 4
PIECE = 16
VMEM = pl.BlockSpec(memory_space=pltpu.VMEM)
SMALL = pltpu.CompilerParams(vmem_limit_bytes=12 * 2**20)
MODE = ("xhi", "zhi", "zlo", "core")
SPACE = ("y", "xlo")
NEAR = ("xlo", "xhi", "zlo", "core")
FAR = ("zhi", "y")


def mode_index():
    at = lax.axis_index(MODE[0])
    for axis in MODE[1:]:
        at = at * lax.axis_size(axis) + lax.axis_index(axis)
    return at


def split2(x):
    high = x.astype(jnp.bfloat16)
    return high, (x - high.astype(jnp.float32)).astype(jnp.bfloat16)


def field_kernel(last, begin_ref, innov_ref, obs_ref, own_ref, halo_ref, start_ref, ids, rows, held, acc, halo, begin_sem, row_sem, sems):
    m = mode_index()
    begin = pltpu.make_async_copy(begin_ref, start_ref, begin_sem)
    begin.start()
    pieces = [
        pltpu.make_async_copy(obs_ref.at[pl.ds(i * PIECE, PIECE)], held.at[pl.ds(i * PIECE, PIECE)], sems.at[i])
        for i in range(BLK_DEV // PIECE)
    ]
    pieces.append(pltpu.make_async_copy(innov_ref, rows, row_sem))
    for piece in pieces:
        piece.start()
    base = m * OWN
    first = jnp.where(m == 0, CELLS_DEV + TILE, 0)
    edge = (m == 0) | (m == last)
    acc[...] = jnp.zeros_like(acc)
    halo[...] = jnp.zeros_like(halo)
    begin.wait()

    def scan(b, count):
        start = start_ref[b]
        place = start - base
        far = start - first
        ids[count] = b
        hit = ((place > 0) & (place < OWN + TILE)) | (edge & (far > -TILE) & (far < TILE))
        return count + jnp.where(hit, 1, 0)

    count = lax.fori_loop(0, BLK_DEV, scan, jnp.int32(0), unroll=16)
    lane = lax.broadcasted_iota(jnp.int32, (1, LANES), 1)
    for piece in pieces:
        piece.wait()

    def add(g, carry):
        found = []
        for u in range(GROUP):
            i = g * GROUP + u
            valid = i < count
            b = jnp.where(valid, ids[i], 0)
            start = start_ref[b]
            row = rows[pl.ds(b, 1), :]
            high = row.astype(jnp.bfloat16).astype(jnp.float32)
            mid = (row - high).astype(jnp.bfloat16).astype(jnp.float32)
            low = row - high - mid
            parts = jnp.concatenate([high, mid, low, jnp.zeros((SUBLANES - 3, LANES), jnp.float32)], axis=0)
            adj = jnp.dot(parts.astype(jnp.bfloat16), held[b], preferred_element_type=jnp.float32)
            adj = adj + pltpu.roll(adj, SUBLANES - 1, 0) + pltpu.roll(adj, SUBLANES - 2, 0)
            off = lax.bitwise_and(start, TILE - 1)
            rolled = pltpu.roll(adj, off, 1)[0:1, :]
            front = jnp.where(lane >= off, rolled, 0.0)
            back = jnp.where(lane < off, rolled, 0.0)
            found.append((valid, start - base, start - first, front, back))
        for valid, place, far, front, back in found:

            @pl.when(valid & (place > 0) & (place < OWN + TILE))
            def _():
                seg = lax.shift_right_logical(place, 7)
                acc[pl.ds(seg, 1), :] += front
                acc[pl.ds(seg + 1, 1), :] += back

            @pl.when(valid & edge & (far > -TILE) & (far < TILE))
            def _():
                halo[...] += jnp.where(far >= 0, front, back)

        return carry

    lax.fori_loop(0, lax.shift_right_logical(count + GROUP - 1, 2), add, 0)
    own_ref[...] = acc[1 : 1 + OWN_TILES, :]
    halo_ref[...] = halo[...]


def field(tile_start, innovations, obs_weights, last):
    kept = [pltpu.with_memory_space_constraint(x, pltpu.HBM) for x in (tile_start, innovations, obs_weights)]
    return pl.pallas_call(
        functools.partial(field_kernel, last),
        out_shape=(
            jax.ShapeDtypeStruct((OWN_TILES, LANES), jnp.float32),
            jax.ShapeDtypeStruct((1, LANES), jnp.float32),
        ),
        in_specs=[pl.BlockSpec(memory_space=pltpu.HBM)] * 3,
        out_specs=(VMEM, VMEM),
        scratch_shapes=[
            pltpu.SMEM((BLK_DEV,), jnp.int32),
            pltpu.SMEM((BLK_DEV + GROUP,), jnp.int32),
            pltpu.VMEM((BLK_DEV, LANES), jnp.float32),
            pltpu.VMEM((BLK_DEV, TILE, TILE), jnp.bfloat16),
            pltpu.VMEM((2 * SUBLANES, LANES), jnp.float32),
            pltpu.VMEM((1, LANES), jnp.float32),
            pltpu.SemaphoreType.DMA,
            pltpu.SemaphoreType.DMA,
            pltpu.SemaphoreType.DMA((BLK_DEV // PIECE,)),
        ],
        compiler_params=SMALL,
        cost_estimate=pl.CostEstimate(flops=2**22, bytes_accessed=2**22, transcendentals=0),
        name="field",
    )(*kept)


def project_kernel(last, own_ref, halo_ref, members_ref, modes_ref, out_ref):
    m = mode_index()
    halo = halo_ref[...]
    row = lax.broadcasted_iota(jnp.int32, (OWN_TILES, LANES), 0)
    takes = ((row == 0) & (m == 0)) | ((row == OWN_TILES - 1) & (m == last))
    weights = own_ref[...] + jnp.where(takes, halo, 0.0)
    contract = (((1,), (1,)), ((), ()))
    highs, lows = [], []
    for j in range(OWN_TILES):
        cells = slice(j * TILE, (j + 1) * TILE)
        high, low = split2(members_ref[:, cells].astype(jnp.float32) * weights[j : j + 1, :])
        highs.append(high)
        lows.append(low)
    modes = modes_ref[...]
    total = lax.dot_general(jnp.concatenate(highs, 1), modes, contract, preferred_element_type=jnp.float32)
    total += lax.dot_general(jnp.concatenate(lows, 1), modes, contract, preferred_element_type=jnp.float32)
    out_ref[...] = total


def project(own, halo, members, modes, last):
    return pl.pallas_call(
        functools.partial(project_kernel, last),
        out_shape=jax.ShapeDtypeStruct((MEMBERS, MODES), jnp.float32),
        in_specs=[VMEM] * 4,
        out_specs=VMEM,
        compiler_params=SMALL,
        name="project",
    )(own, halo, members, modes)


def finish_kernel(total_count, coeff_ref, members_ref, modes_ref, inc_ref, own_ref, turned):
    m = mode_index()
    coeff = coeff_ref[...]
    high, low = split2(coeff)
    modes = modes_ref[...]
    mixed = jnp.dot(high, modes, preferred_element_type=jnp.float32)
    mixed += jnp.dot(low, modes, preferred_element_type=jnp.float32)
    spread = jnp.sum(jnp.sum(coeff * coeff, axis=0, keepdims=True), axis=1, keepdims=True)
    factor = lax.rsqrt(1.0 + spread / total_count)
    turned[...] = coeff.T
    own_ref[...] = turned[pl.ds(m * MODE_DEV, MODE_DEV), :]
    mixed = mixed * members_ref[...].astype(jnp.float32)
    summed = jnp.sum(mixed, axis=0, keepdims=True) * (factor / (MEMBERS - 1))
    for j in range(OWN_TILES):
        inc_ref[j : j + 1, :] = summed[:, j * TILE : (j + 1) * TILE]


def finish(coeff, members, modes):
    return pl.pallas_call(
        functools.partial(finish_kernel, MEMBERS * MODES),
        out_shape=(
            jax.ShapeDtypeStruct((OWN_TILES, LANES), jnp.float32),
            jax.ShapeDtypeStruct((MODE_DEV, MEMBERS), jnp.float32),
        ),
        in_specs=[VMEM] * 3,
        out_specs=(VMEM, VMEM),
        scratch_shapes=[pltpu.VMEM((MODES, MEMBERS), jnp.float32)],
        compiler_params=SMALL,
        name="finish",
    )(coeff, members, modes)


def exchange(x, axis):
    return lax.all_to_all(x, axis, split_axis=0, concat_axis=0, tiled=True)


def everywhere(x, axis):
    return exchange(jnp.broadcast_to(x[None], (lax.axis_size(axis),) + x.shape), axis)


def on_device(members, modes, obs_weights, innovations, tile_start):
    mode_count = lax.axis_size(MODE)
    space_count = lax.axis_size(SPACE)
    last = mode_count - 1
    all_modes = lax.all_to_all(modes, MODE, split_axis=1, concat_axis=0, tiled=True)
    own, halo = field(tile_start, innovations, obs_weights, last)
    route = []
    for s in range(space_count):
        behind, ahead = (s - 1) % space_count, (s + 1) % space_count
        route.append((s * mode_count, ahead * mode_count))
        route.append((s * mode_count + last, behind * mode_count + last))
    halo = lax.ppermute(halo, SPACE + MODE, route)
    terms = project(own, halo, members, all_modes, last)
    part = jnp.sum(exchange(terms.reshape(lax.axis_size(NEAR), 1, -1), NEAR), axis=0)
    part = jnp.sum(everywhere(part, FAR), axis=0)
    coeff = everywhere(part, NEAR)
    increment, own_coeff = finish(coeff.reshape(MEMBERS, MODES), members, all_modes)
    return increment.reshape(OWN), own_coeff.T


def solution(mesh):
    finer = Mesh(mesh.devices.reshape(8, 2, 2, 4, 2, 2), SPACE + MODE)
    in_specs = (P(None, SPACE + MODE), P(MODE, SPACE), P(SPACE, None, None), P(SPACE, None), P(SPACE))
    out_specs = (P(SPACE + MODE), P(None, MODE))
    return jax.shard_map(
        on_device, mesh=finer, in_specs=in_specs, out_specs=out_specs, check_vma=False
    )
```

```python
import functools

import jax
import jax.numpy as jnp
import numpy as np
from jax import lax
from jax.experimental import pallas as pl
from jax.experimental.pallas import tpu as pltpu
from jax.sharding import Mesh
from jax.sharding import PartitionSpec as P

MEMBERS = 80
MODE_DEV = 4
MODES = 128
CELLS_DEV = 32768
TILE = 128
BLK_DEV = 128
OWN = 1024
OWN_TILES = OWN // TILE
LANES = 128
SUBLANES = 8
GROUP = 4
PIECE = 16
VMEM = pl.BlockSpec(memory_space=pltpu.VMEM)
SMALL = pltpu.CompilerParams(vmem_limit_bytes=12 * 2**20)
MODE = ("xhi", "zhi", "zlo", "core")
SPACE = ("y", "xlo")
NEAR = ("xlo", "xhi", "zlo", "core")
FAR = ("y", "zhi")


def mode_index():
    at = lax.axis_index(MODE[0])
    for axis in MODE[1:]:
        at = at * lax.axis_size(axis) + lax.axis_index(axis)
    return at


def split2(x):
    high = x.astype(jnp.bfloat16)
    return high, (x - high.astype(jnp.float32)).astype(jnp.bfloat16)


def field_kernel(last, begin_ref, innov_ref, obs_ref, own_ref, halo_ref, start_ref, ids, rows, held, acc, halo, begin_sem, row_sem, sems):
    m = mode_index()
    begin = pltpu.make_async_copy(begin_ref, start_ref, begin_sem)
    begin.start()
    pieces = [
        pltpu.make_async_copy(obs_ref.at[pl.ds(i * PIECE, PIECE)], held.at[pl.ds(i * PIECE, PIECE)], sems.at[i])
        for i in range(BLK_DEV // PIECE)
    ]
    pieces.append(pltpu.make_async_copy(innov_ref, rows, row_sem))
    for piece in pieces:
        piece.start()
    base = m * OWN
    first = jnp.where(m == 0, CELLS_DEV + TILE, 0)
    edge = (m == 0) | (m == last)
    acc[...] = jnp.zeros_like(acc)
    halo[...] = jnp.zeros_like(halo)
    begin.wait()

    def scan(b, count):
        start = start_ref[b]
        place = start - base
        far = start - first
        ids[count] = b
        hit = ((place > 0) & (place < OWN + TILE)) | (edge & (far > -TILE) & (far < TILE))
        return count + jnp.where(hit, 1, 0)

    count = lax.fori_loop(0, BLK_DEV, scan, jnp.int32(0), unroll=16)
    lane = lax.broadcasted_iota(jnp.int32, (1, LANES), 1)
    for piece in pieces:
        piece.wait()

    def add(g, carry):
        found = []
        for u in range(GROUP):
            i = g * GROUP + u
            valid = i < count
            b = jnp.where(valid, ids[i], 0)
            start = start_ref[b]
            row = rows[pl.ds(b, 1), :]
            high = row.astype(jnp.bfloat16).astype(jnp.float32)
            mid = (row - high).astype(jnp.bfloat16).astype(jnp.float32)
            low = row - high - mid
            parts = jnp.concatenate([high, mid, low, jnp.zeros((SUBLANES - 3, LANES), jnp.float32)], axis=0)
            adj = jnp.dot(parts.astype(jnp.bfloat16), held[b], preferred_element_type=jnp.float32)
            adj = adj + pltpu.roll(adj, SUBLANES - 1, 0) + pltpu.roll(adj, SUBLANES - 2, 0)
            off = lax.bitwise_and(start, TILE - 1)
            rolled = pltpu.roll(adj, off, 1)[0:1, :]
            front = jnp.where(lane >= off, rolled, 0.0)
            back = jnp.where(lane < off, rolled, 0.0)
            found.append((valid, start - base, start - first, front, back))
        for valid, place, far, front, back in found:

            @pl.when(valid & (place > 0) & (place < OWN + TILE))
            def _():
                seg = lax.shift_right_logical(place, 7)
                acc[pl.ds(seg, 1), :] += front
                acc[pl.ds(seg + 1, 1), :] += back

            @pl.when(valid & edge & (far > -TILE) & (far < TILE))
            def _():
                halo[...] += jnp.where(far >= 0, front, back)

        return carry

    lax.fori_loop(0, lax.shift_right_logical(count + GROUP - 1, 2), add, 0)
    own_ref[...] = acc[1 : 1 + OWN_TILES, :]
    halo_ref[...] = halo[...]


def field(tile_start, innovations, obs_weights, last):
    kept = [pltpu.with_memory_space_constraint(x, pltpu.HBM) for x in (tile_start, innovations, obs_weights)]
    return pl.pallas_call(
        functools.partial(field_kernel, last),
        out_shape=(
            jax.ShapeDtypeStruct((OWN_TILES, LANES), jnp.float32),
            jax.ShapeDtypeStruct((1, LANES), jnp.float32),
        ),
        in_specs=[pl.BlockSpec(memory_space=pltpu.HBM)] * 3,
        out_specs=(VMEM, VMEM),
        scratch_shapes=[
            pltpu.SMEM((BLK_DEV,), jnp.int32),
            pltpu.SMEM((BLK_DEV + GROUP,), jnp.int32),
            pltpu.VMEM((BLK_DEV, LANES), jnp.float32),
            pltpu.VMEM((BLK_DEV, TILE, TILE), jnp.bfloat16),
            pltpu.VMEM((2 * SUBLANES, LANES), jnp.float32),
            pltpu.VMEM((1, LANES), jnp.float32),
            pltpu.SemaphoreType.DMA,
            pltpu.SemaphoreType.DMA,
            pltpu.SemaphoreType.DMA((BLK_DEV // PIECE,)),
        ],
        compiler_params=SMALL,
        cost_estimate=pl.CostEstimate(flops=2**22, bytes_accessed=2**22, transcendentals=0),
        name="field",
    )(*kept)


def project_kernel(last, own_ref, halo_ref, members_ref, modes_ref, out_ref):
    m = mode_index()
    halo = halo_ref[...]
    row = lax.broadcasted_iota(jnp.int32, (OWN_TILES, LANES), 0)
    takes = ((row == 0) & (m == 0)) | ((row == OWN_TILES - 1) & (m == last))
    weights = own_ref[...] + jnp.where(takes, halo, 0.0)
    contract = (((1,), (1,)), ((), ()))
    highs, lows = [], []
    for j in range(OWN_TILES):
        cells = slice(j * TILE, (j + 1) * TILE)
        high, low = split2(members_ref[:, cells].astype(jnp.float32) * weights[j : j + 1, :])
        highs.append(high)
        lows.append(low)
    modes = modes_ref[...]
    total = lax.dot_general(jnp.concatenate(highs, 1), modes, contract, preferred_element_type=jnp.float32)
    total += lax.dot_general(jnp.concatenate(lows, 1), modes, contract, preferred_element_type=jnp.float32)
    out_ref[...] = total


def project(own, halo, members, modes, last):
    return pl.pallas_call(
        functools.partial(project_kernel, last),
        out_shape=jax.ShapeDtypeStruct((MEMBERS, MODES), jnp.float32),
        in_specs=[VMEM] * 4,
        out_specs=VMEM,
        compiler_params=SMALL,
        name="project",
    )(own, halo, members, modes)


def finish_kernel(total_count, coeff_ref, members_ref, modes_ref, inc_ref, own_ref, turned):
    m = mode_index()
    coeff = coeff_ref[...]
    high, low = split2(coeff)
    modes = modes_ref[...]
    mixed = jnp.dot(high, modes, preferred_element_type=jnp.float32)
    mixed += jnp.dot(low, modes, preferred_element_type=jnp.float32)
    spread = jnp.sum(jnp.sum(coeff * coeff, axis=0, keepdims=True), axis=1, keepdims=True)
    factor = lax.rsqrt(1.0 + spread / total_count)
    turned[...] = coeff.T
    own_ref[...] = turned[pl.ds(m * MODE_DEV, MODE_DEV), :]
    mixed = mixed * members_ref[...].astype(jnp.float32)
    summed = jnp.sum(mixed, axis=0, keepdims=True) * (factor / (MEMBERS - 1))
    for j in range(OWN_TILES):
        inc_ref[j : j + 1, :] = summed[:, j * TILE : (j + 1) * TILE]


def finish(coeff, members, modes):
    return pl.pallas_call(
        functools.partial(finish_kernel, MEMBERS * MODES),
        out_shape=(
            jax.ShapeDtypeStruct((OWN_TILES, LANES), jnp.float32),
            jax.ShapeDtypeStruct((MODE_DEV, MEMBERS), jnp.float32),
        ),
        in_specs=[VMEM] * 3,
        out_specs=(VMEM, VMEM),
        scratch_shapes=[pltpu.VMEM((MODES, MEMBERS), jnp.float32)],
        compiler_params=SMALL,
        name="finish",
    )(coeff, members, modes)


def from_middle(axis):
    sizes = [lax.axis_size(a) for a in axis]
    places = np.arange(np.prod(sizes)).reshape(sizes)
    for d, size in enumerate(sizes):
        places = np.roll(places, -(size // 2), axis=d)
    return [[int(place) for place in places.reshape(-1)]]


def exchange(x, axis):
    return lax.all_to_all(x, axis, split_axis=0, concat_axis=0, axis_index_groups=from_middle(axis), tiled=True)


def everywhere(x, axis):
    return exchange(jnp.broadcast_to(x[None], (lax.axis_size(axis),) + x.shape), axis)


def on_device(members, modes, obs_weights, innovations, tile_start):
    mode_count = lax.axis_size(MODE)
    space_count = lax.axis_size(SPACE)
    last = mode_count - 1
    all_modes = lax.all_to_all(modes, MODE, split_axis=1, concat_axis=0, tiled=True)
    own, halo = field(tile_start, innovations, obs_weights, last)
    route = []
    for s in range(space_count):
        behind, ahead = (s - 1) % space_count, (s + 1) % space_count
        route.append((s * mode_count, ahead * mode_count))
        route.append((s * mode_count + last, behind * mode_count + last))
    halo = lax.ppermute(halo, SPACE + MODE, route)
    terms = project(own, halo, members, all_modes, last)
    part = jnp.sum(exchange(terms.reshape(lax.axis_size(NEAR), 1, -1), NEAR), axis=0)
    part = jnp.sum(everywhere(part, FAR), axis=0)
    coeff = everywhere(part, NEAR)
    increment, own_coeff = finish(coeff.reshape(MEMBERS, MODES), members, all_modes)
    return increment.reshape(OWN), own_coeff.T


def solution(mesh):
    finer = Mesh(mesh.devices.reshape(8, 2, 2, 4, 2, 2), SPACE + MODE)
    in_specs = (P(None, SPACE + MODE), P(MODE, SPACE), P(SPACE, None, None), P(SPACE, None), P(SPACE))
    out_specs = (P(SPACE + MODE), P(None, MODE))
    return jax.shard_map(
        on_device, mesh=finer, in_specs=in_specs, out_specs=out_specs, check_vma=False
    )
```

```python
import functools

import jax
import jax.numpy as jnp
import numpy as np
from jax import lax
from jax.experimental import pallas as pl
from jax.experimental.pallas import tpu as pltpu
from jax.sharding import Mesh
from jax.sharding import PartitionSpec as P

MEMBERS = 80
MODE_DEV = 4
MODES = 128
CELLS_DEV = 32768
TILE = 128
BLK_DEV = 128
OWN = 1024
OWN_TILES = OWN // TILE
LANES = 128
SUBLANES = 8
GROUP = 4
PIECE = 16
VMEM = pl.BlockSpec(memory_space=pltpu.VMEM)
SMALL = pltpu.CompilerParams(vmem_limit_bytes=12 * 2**20)
MODE = ("xhi", "zhi", "zlo", "core")
SPACE = ("y", "xlo")
NEAR = ("xlo", "xhi", "zlo", "core")
FAR = ("y", "zhi")
FIRST = {NEAR: {"xhi": 1, "zlo": 1}, FAR: {"y": 4, "zhi": 2}, MODE: {"xhi": 1, "zhi": 2}}


def mode_index():
    at = lax.axis_index(MODE[0])
    for axis in MODE[1:]:
        at = at * lax.axis_size(axis) + lax.axis_index(axis)
    return at


def split2(x):
    high = x.astype(jnp.bfloat16)
    return high, (x - high.astype(jnp.float32)).astype(jnp.bfloat16)


def field_kernel(last, begin_ref, innov_ref, obs_ref, own_ref, halo_ref, start_ref, ids, rows, held, acc, halo, begin_sem, row_sem, sems):
    m = mode_index()
    begin = pltpu.make_async_copy(begin_ref, start_ref, begin_sem)
    begin.start()
    pieces = [
        pltpu.make_async_copy(obs_ref.at[pl.ds(i * PIECE, PIECE)], held.at[pl.ds(i * PIECE, PIECE)], sems.at[i])
        for i in range(BLK_DEV // PIECE)
    ]
    pieces.append(pltpu.make_async_copy(innov_ref, rows, row_sem))
    for piece in pieces:
        piece.start()
    base = m * OWN
    first = jnp.where(m == 0, CELLS_DEV + TILE, 0)
    edge = (m == 0) | (m == last)
    acc[...] = jnp.zeros_like(acc)
    halo[...] = jnp.zeros_like(halo)
    begin.wait()

    def scan(b, count):
        start = start_ref[b]
        place = start - base
        far = start - first
        ids[count] = b
        hit = ((place > 0) & (place < OWN + TILE)) | (edge & (far > -TILE) & (far < TILE))
        return count + jnp.where(hit, 1, 0)

    count = lax.fori_loop(0, BLK_DEV, scan, jnp.int32(0), unroll=16)
    lane = lax.broadcasted_iota(jnp.int32, (1, LANES), 1)
    for piece in pieces:
        piece.wait()

    def add(g, carry):
        found = []
        for u in range(GROUP):
            i = g * GROUP + u
            valid = i < count
            b = jnp.where(valid, ids[i], 0)
            start = start_ref[b]
            row = rows[pl.ds(b, 1), :]
            high = row.astype(jnp.bfloat16).astype(jnp.float32)
            mid = (row - high).astype(jnp.bfloat16).astype(jnp.float32)
            low = row - high - mid
            parts = jnp.concatenate([high, mid, low, jnp.zeros((SUBLANES - 3, LANES), jnp.float32)], axis=0)
            adj = jnp.dot(parts.astype(jnp.bfloat16), held[b], preferred_element_type=jnp.float32)
            adj = adj + pltpu.roll(adj, SUBLANES - 1, 0) + pltpu.roll(adj, SUBLANES - 2, 0)
            off = lax.bitwise_and(start, TILE - 1)
            rolled = pltpu.roll(adj, off, 1)[0:1, :]
            front = jnp.where(lane >= off, rolled, 0.0)
            back = jnp.where(lane < off, rolled, 0.0)
            found.append((valid, start - base, start - first, front, back))
        for valid, place, far, front, back in found:

            @pl.when(valid & (place > 0) & (place < OWN + TILE))
            def _():
                seg = lax.shift_right_logical(place, 7)
                acc[pl.ds(seg, 1), :] += front
                acc[pl.ds(seg + 1, 1), :] += back

            @pl.when(valid & edge & (far > -TILE) & (far < TILE))
            def _():
                halo[...] += jnp.where(far >= 0, front, back)

        return carry

    lax.fori_loop(0, lax.shift_right_logical(count + GROUP - 1, 2), add, 0)
    own_ref[...] = acc[1 : 1 + OWN_TILES, :]
    halo_ref[...] = halo[...]


def field(tile_start, innovations, obs_weights, last):
    kept = [pltpu.with_memory_space_constraint(x, pltpu.HBM) for x in (tile_start, innovations, obs_weights)]
    return pl.pallas_call(
        functools.partial(field_kernel, last),
        out_shape=(
            jax.ShapeDtypeStruct((OWN_TILES, LANES), jnp.float32),
            jax.ShapeDtypeStruct((1, LANES), jnp.float32),
        ),
        in_specs=[pl.BlockSpec(memory_space=pltpu.HBM)] * 3,
        out_specs=(VMEM, VMEM),
        scratch_shapes=[
            pltpu.SMEM((BLK_DEV,), jnp.int32),
            pltpu.SMEM((BLK_DEV + GROUP,), jnp.int32),
            pltpu.VMEM((BLK_DEV, LANES), jnp.float32),
            pltpu.VMEM((BLK_DEV, TILE, TILE), jnp.bfloat16),
            pltpu.VMEM((2 * SUBLANES, LANES), jnp.float32),
            pltpu.VMEM((1, LANES), jnp.float32),
            pltpu.SemaphoreType.DMA,
            pltpu.SemaphoreType.DMA,
            pltpu.SemaphoreType.DMA((BLK_DEV // PIECE,)),
        ],
        compiler_params=SMALL,
        cost_estimate=pl.CostEstimate(flops=2**22, bytes_accessed=2**22, transcendentals=0),
        name="field",
    )(*kept)


def lay_kernel(modes_ref, out_ref, sems):
    part = modes_ref.shape[1] // 4
    copies = [
        pltpu.make_async_copy(
            modes_ref.at[:, pl.ds(q * part, part)], out_ref.at[:, pl.ds((3 - q) * part, part)], sems.at[q]
        )
        for q in range(4)
    ]
    for copy in copies:
        copy.start()
    for copy in copies:
        copy.wait()


def lay(modes):
    return pl.pallas_call(
        lay_kernel,
        out_shape=jax.ShapeDtypeStruct(modes.shape, modes.dtype),
        in_specs=[pl.BlockSpec(memory_space=pltpu.HBM)],
        out_specs=VMEM,
        scratch_shapes=[pltpu.SemaphoreType.DMA((4,))],
        compiler_params=SMALL,
        name="lay",
    )(pltpu.with_memory_space_constraint(modes, pltpu.HBM))


def project_kernel(last, own_ref, halo_ref, members_ref, modes_ref, out_ref):
    m = mode_index()
    halo = halo_ref[...]
    row = lax.broadcasted_iota(jnp.int32, (OWN_TILES, LANES), 0)
    takes = ((row == 0) & (m == 0)) | ((row == OWN_TILES - 1) & (m == last))
    weights = own_ref[...] + jnp.where(takes, halo, 0.0)
    contract = (((1,), (1,)), ((), ()))
    highs, lows = [], []
    for j in range(OWN_TILES):
        cells = slice(j * TILE, (j + 1) * TILE)
        high, low = split2(members_ref[:, cells].astype(jnp.float32) * weights[j : j + 1, :])
        highs.append(high)
        lows.append(low)
    modes = modes_ref[...]
    total = lax.dot_general(jnp.concatenate(highs, 1), modes, contract, preferred_element_type=jnp.float32)
    total += lax.dot_general(jnp.concatenate(lows, 1), modes, contract, preferred_element_type=jnp.float32)
    out_ref[...] = total


def project(own, halo, members, modes, last):
    return pl.pallas_call(
        functools.partial(project_kernel, last),
        out_shape=jax.ShapeDtypeStruct((MEMBERS, MODES), jnp.float32),
        in_specs=[VMEM] * 4,
        out_specs=VMEM,
        compiler_params=SMALL,
        name="project",
    )(own, halo, members, modes)


def finish_kernel(total_count, coeff_ref, members_ref, modes_ref, inc_ref, own_ref, turned):
    m = mode_place()
    coeff = coeff_ref[...]
    high, low = split2(coeff)
    modes = modes_ref[...]
    mixed = jnp.dot(high, modes, preferred_element_type=jnp.float32)
    mixed += jnp.dot(low, modes, preferred_element_type=jnp.float32)
    spread = jnp.sum(jnp.sum(coeff * coeff, axis=0, keepdims=True), axis=1, keepdims=True)
    factor = lax.rsqrt(1.0 + spread / total_count)
    turned[...] = coeff.T
    own_ref[...] = turned[pl.ds(m * MODE_DEV, MODE_DEV), :]
    mixed = mixed * members_ref[...].astype(jnp.float32)
    summed = jnp.sum(mixed, axis=0, keepdims=True) * (factor / (MEMBERS - 1))
    for j in range(OWN_TILES):
        inc_ref[j : j + 1, :] = summed[:, j * TILE : (j + 1) * TILE]


def finish(coeff, members, modes):
    return pl.pallas_call(
        functools.partial(finish_kernel, MEMBERS * MODES),
        out_shape=(
            jax.ShapeDtypeStruct((OWN_TILES, LANES), jnp.float32),
            jax.ShapeDtypeStruct((MODE_DEV, MEMBERS), jnp.float32),
        ),
        in_specs=[VMEM] * 3,
        out_specs=(VMEM, VMEM),
        scratch_shapes=[pltpu.VMEM((MODES, MEMBERS), jnp.float32)],
        compiler_params=SMALL,
        name="finish",
    )(coeff, members, modes)


def places(axis):
    sizes = [lax.axis_size(a) for a in axis]
    order = np.arange(np.prod(sizes)).reshape(sizes)
    for d, a in enumerate(axis):
        order = np.roll(order, -FIRST[axis].get(a, 0), axis=d)
    return [[int(place) for place in order.reshape(-1)]]


def mode_place():
    at = 0
    for axis in MODE:
        size = lax.axis_size(axis)
        at = at * size + lax.rem(lax.axis_index(axis) + (size - FIRST[MODE].get(axis, 0)), size)
    return at


def exchange(x, axis):
    return lax.all_to_all(x, axis, split_axis=0, concat_axis=0, axis_index_groups=places(axis), tiled=True)


def everywhere(x, axis):
    return exchange(jnp.broadcast_to(x[None], (lax.axis_size(axis),) + x.shape), axis)


def on_device(members, modes, obs_weights, innovations, tile_start):
    mode_count = lax.axis_size(MODE)
    space_count = lax.axis_size(SPACE)
    last = mode_count - 1
    laid = lay(modes)
    all_modes = lax.all_to_all(
        laid, MODE, split_axis=1, concat_axis=0, axis_index_groups=places(MODE), tiled=True
    )
    own, halo = field(tile_start, innovations, obs_weights, last)
    route = []
    for s in range(space_count):
        behind, ahead = (s - 1) % space_count, (s + 1) % space_count
        route.append((s * mode_count, ahead * mode_count))
        route.append((s * mode_count + last, behind * mode_count + last))
    halo = lax.ppermute(halo, SPACE + MODE, route)
    terms = project(own, halo, members, all_modes, last)
    part = jnp.sum(exchange(terms.reshape(lax.axis_size(NEAR), 1, -1), NEAR), axis=0)
    part = jnp.sum(everywhere(part, FAR), axis=0)
    coeff = everywhere(part, NEAR)
    increment, own_coeff = finish(coeff.reshape(MEMBERS, MODES), members, all_modes)
    return increment.reshape(OWN), own_coeff.T


def solution(mesh):
    finer = Mesh(mesh.devices.reshape(8, 2, 2, 4, 2, 2), SPACE + MODE)
    in_specs = (P(None, SPACE + MODE), P(MODE, SPACE), P(SPACE, None, None), P(SPACE, None), P(SPACE))
    out_specs = (P(SPACE + MODE), P(None, MODE))
    return jax.shard_map(
        on_device, mesh=finer, in_specs=in_specs, out_specs=out_specs, check_vma=False
    )
```

```python
import functools

import jax
import jax.numpy as jnp
import numpy as np
from jax import lax
from jax.experimental import pallas as pl
from jax.experimental.pallas import tpu as pltpu
from jax.sharding import Mesh
from jax.sharding import PartitionSpec as P

MEMBERS = 80
MODE_DEV = 4
MODES = 128
CELLS_DEV = 32768
TILE = 128
BLK_DEV = 128
OWN = 1024
OWN_TILES = OWN // TILE
LANES = 128
SUBLANES = 8
GROUP = 4
PIECE = 16
VMEM = pl.BlockSpec(memory_space=pltpu.VMEM)
SMALL = pltpu.CompilerParams(vmem_limit_bytes=12 * 2**20)
MODE = ("xhi", "zhi", "zlo", "core")
SPACE = ("y", "xlo")
NEAR = ("xlo", "xhi", "zlo", "core")
FAR = ("y", "zhi")
FIRST = {NEAR: {"xhi": 1, "zlo": 1}, FAR: {"y": 4, "zhi": 2}, MODE: {"xhi": 1, "zhi": 2}}


def mode_index():
    at = lax.axis_index(MODE[0])
    for axis in MODE[1:]:
        at = at * lax.axis_size(axis) + lax.axis_index(axis)
    return at


def split2(x):
    high = x.astype(jnp.bfloat16)
    return high, (x - high.astype(jnp.float32)).astype(jnp.bfloat16)


def find_field(last, begin_ref, innov_ref, obs_ref, own_ref, halo_ref, start_ref, ids, rows, held, acc, halo, begin_sem, row_sem, sems):
    m = mode_index()
    begin = pltpu.make_async_copy(begin_ref, start_ref, begin_sem)
    begin.start()
    pieces = [
        pltpu.make_async_copy(obs_ref.at[pl.ds(i * PIECE, PIECE)], held.at[pl.ds(i * PIECE, PIECE)], sems.at[i])
        for i in range(BLK_DEV // PIECE)
    ]
    pieces.append(pltpu.make_async_copy(innov_ref, rows, row_sem))
    for piece in pieces:
        piece.start()
    base = m * OWN
    first = jnp.where(m == 0, CELLS_DEV + TILE, 0)
    edge = (m == 0) | (m == last)
    acc[...] = jnp.zeros_like(acc)
    halo[...] = jnp.zeros_like(halo)
    begin.wait()

    def scan(b, count):
        start = start_ref[b]
        place = start - base
        far = start - first
        ids[count] = b
        hit = ((place > 0) & (place < OWN + TILE)) | (edge & (far > -TILE) & (far < TILE))
        return count + jnp.where(hit, 1, 0)

    count = lax.fori_loop(0, BLK_DEV, scan, jnp.int32(0), unroll=16)
    lane = lax.broadcasted_iota(jnp.int32, (1, LANES), 1)
    for piece in pieces:
        piece.wait()

    def add(g, carry):
        found = []
        for u in range(GROUP):
            i = g * GROUP + u
            valid = i < count
            b = jnp.where(valid, ids[i], 0)
            start = start_ref[b]
            row = rows[pl.ds(b, 1), :]
            high = row.astype(jnp.bfloat16).astype(jnp.float32)
            mid = (row - high).astype(jnp.bfloat16).astype(jnp.float32)
            low = row - high - mid
            parts = jnp.concatenate([high, mid, low, jnp.zeros((SUBLANES - 3, LANES), jnp.float32)], axis=0)
            adj = jnp.dot(parts.astype(jnp.bfloat16), held[b], preferred_element_type=jnp.float32)
            adj = adj + pltpu.roll(adj, SUBLANES - 1, 0) + pltpu.roll(adj, SUBLANES - 2, 0)
            off = lax.bitwise_and(start, TILE - 1)
            rolled = pltpu.roll(adj, off, 1)[0:1, :]
            front = jnp.where(lane >= off, rolled, 0.0)
            back = jnp.where(lane < off, rolled, 0.0)
            found.append((valid, start - base, start - first, front, back))
        for valid, place, far, front, back in found:

            @pl.when(valid & (place > 0) & (place < OWN + TILE))
            def _():
                seg = lax.shift_right_logical(place, 7)
                acc[pl.ds(seg, 1), :] += front
                acc[pl.ds(seg + 1, 1), :] += back

            @pl.when(valid & edge & (far > -TILE) & (far < TILE))
            def _():
                halo[...] += jnp.where(far >= 0, front, back)

        return carry

    lax.fori_loop(0, lax.shift_right_logical(count + GROUP - 1, 2), add, 0)
    own_ref[...] = acc[1 : 1 + OWN_TILES, :]
    halo_ref[...] = halo[...]


def waits_long():
    return lax.axis_index("zhi") < lax.axis_size("zhi") // 2


def early_kernel(last, modes_ref, begin_ref, innov_ref, obs_ref, laid_ref, own_ref, halo_ref, lay_sems, *scratch):
    part = modes_ref.shape[1] // 4
    copies = [
        pltpu.make_async_copy(
            modes_ref.at[:, pl.ds(q * part, part)], laid_ref.at[:, pl.ds((3 - q) * part, part)], lay_sems.at[q]
        )
        for q in range(4)
    ]
    for copy in copies:
        copy.start()

    @pl.when(waits_long())
    def _():
        find_field(last, begin_ref, innov_ref, obs_ref, own_ref, halo_ref, *scratch)

    for copy in copies:
        copy.wait()


def late_kernel(last, begin_ref, innov_ref, obs_ref, early_own_ref, early_halo_ref, own_ref, halo_ref, *scratch):
    @pl.when(waits_long())
    def _():
        own_ref[...] = early_own_ref[...]
        halo_ref[...] = early_halo_ref[...]

    @pl.when(jnp.logical_not(waits_long()))
    def _():
        find_field(last, begin_ref, innov_ref, obs_ref, own_ref, halo_ref, *scratch)


HBM = pl.BlockSpec(memory_space=pltpu.HBM)
FIELD = (jax.ShapeDtypeStruct((OWN_TILES, LANES), jnp.float32), jax.ShapeDtypeStruct((1, LANES), jnp.float32))


def field_scratch():
    return [
        pltpu.SMEM((BLK_DEV,), jnp.int32),
        pltpu.SMEM((BLK_DEV + GROUP,), jnp.int32),
        pltpu.VMEM((BLK_DEV, LANES), jnp.float32),
        pltpu.VMEM((BLK_DEV, TILE, TILE), jnp.bfloat16),
        pltpu.VMEM((2 * SUBLANES, LANES), jnp.float32),
        pltpu.VMEM((1, LANES), jnp.float32),
        pltpu.SemaphoreType.DMA,
        pltpu.SemaphoreType.DMA,
        pltpu.SemaphoreType.DMA((BLK_DEV // PIECE,)),
    ]


def in_hbm(*operands):
    return [pltpu.with_memory_space_constraint(x, pltpu.HBM) for x in operands]


def early(modes, tile_start, innovations, obs_weights, last):
    return pl.pallas_call(
        functools.partial(early_kernel, last),
        out_shape=(jax.ShapeDtypeStruct(modes.shape, modes.dtype),) + FIELD,
        in_specs=[HBM] * 4,
        out_specs=(VMEM,) * 3,
        scratch_shapes=[pltpu.SemaphoreType.DMA((4,))] + field_scratch(),
        compiler_params=SMALL,
        name="early",
    )(*in_hbm(modes, tile_start, innovations, obs_weights))


def late(tile_start, innovations, obs_weights, own, halo, last):
    return pl.pallas_call(
        functools.partial(late_kernel, last),
        out_shape=FIELD,
        in_specs=[HBM] * 3 + [VMEM] * 2,
        out_specs=(VMEM,) * 2,
        scratch_shapes=field_scratch(),
        compiler_params=SMALL,
        cost_estimate=pl.CostEstimate(flops=2**22, bytes_accessed=2**22, transcendentals=0),
        name="late",
    )(*in_hbm(tile_start, innovations, obs_weights), own, halo)


def project_kernel(last, own_ref, halo_ref, members_ref, modes_ref, out_ref):
    m = mode_index()
    halo = halo_ref[...]
    row = lax.broadcasted_iota(jnp.int32, (OWN_TILES, LANES), 0)
    takes = ((row == 0) & (m == 0)) | ((row == OWN_TILES - 1) & (m == last))
    weights = own_ref[...] + jnp.where(takes, halo, 0.0)
    contract = (((1,), (1,)), ((), ()))
    highs, lows = [], []
    for j in range(OWN_TILES):
        cells = slice(j * TILE, (j + 1) * TILE)
        high, low = split2(members_ref[:, cells].astype(jnp.float32) * weights[j : j + 1, :])
        highs.append(high)
        lows.append(low)
    modes = modes_ref[...]
    total = lax.dot_general(jnp.concatenate(highs, 1), modes, contract, preferred_element_type=jnp.float32)
    total += lax.dot_general(jnp.concatenate(lows, 1), modes, contract, preferred_element_type=jnp.float32)
    out_ref[...] = total


def project(own, halo, members, modes, last):
    return pl.pallas_call(
        functools.partial(project_kernel, last),
        out_shape=jax.ShapeDtypeStruct((MEMBERS, MODES), jnp.float32),
        in_specs=[VMEM] * 4,
        out_specs=VMEM,
        compiler_params=SMALL,
        name="project",
    )(own, halo, members, modes)


def finish_kernel(total_count, coeff_ref, members_ref, modes_ref, inc_ref, own_ref, turned):
    m = mode_place()
    coeff = coeff_ref[...]
    high, low = split2(coeff)
    modes = modes_ref[...]
    mixed = jnp.dot(high, modes, preferred_element_type=jnp.float32)
    mixed += jnp.dot(low, modes, preferred_element_type=jnp.float32)
    spread = jnp.sum(jnp.sum(coeff * coeff, axis=0, keepdims=True), axis=1, keepdims=True)
    factor = lax.rsqrt(1.0 + spread / total_count)
    turned[...] = coeff.T
    own_ref[...] = turned[pl.ds(m * MODE_DEV, MODE_DEV), :]
    mixed = mixed * members_ref[...].astype(jnp.float32)
    summed = jnp.sum(mixed, axis=0, keepdims=True) * (factor / (MEMBERS - 1))
    for j in range(OWN_TILES):
        inc_ref[j : j + 1, :] = summed[:, j * TILE : (j + 1) * TILE]


def finish(coeff, members, modes):
    return pl.pallas_call(
        functools.partial(finish_kernel, MEMBERS * MODES),
        out_shape=(
            jax.ShapeDtypeStruct((OWN_TILES, LANES), jnp.float32),
            jax.ShapeDtypeStruct((MODE_DEV, MEMBERS), jnp.float32),
        ),
        in_specs=[VMEM] * 3,
        out_specs=(VMEM, VMEM),
        scratch_shapes=[pltpu.VMEM((MODES, MEMBERS), jnp.float32)],
        compiler_params=SMALL,
        name="finish",
    )(coeff, members, modes)


def places(axis):
    sizes = [lax.axis_size(a) for a in axis]
    order = np.arange(np.prod(sizes)).reshape(sizes)
    for d, a in enumerate(axis):
        order = np.roll(order, -FIRST[axis].get(a, 0), axis=d)
    return [[int(place) for place in order.reshape(-1)]]


def mode_place():
    at = 0
    for axis in MODE:
        size = lax.axis_size(axis)
        at = at * size + lax.rem(lax.axis_index(axis) + (size - FIRST[MODE].get(axis, 0)), size)
    return at


def exchange(x, axis):
    return lax.all_to_all(x, axis, split_axis=0, concat_axis=0, axis_index_groups=places(axis), tiled=True)


def everywhere(x, axis):
    return exchange(jnp.broadcast_to(x[None], (lax.axis_size(axis),) + x.shape), axis)


def on_device(members, modes, obs_weights, innovations, tile_start):
    mode_count = lax.axis_size(MODE)
    space_count = lax.axis_size(SPACE)
    last = mode_count - 1
    laid, own, halo = early(modes, tile_start, innovations, obs_weights, last)
    all_modes = lax.all_to_all(
        laid, MODE, split_axis=1, concat_axis=0, axis_index_groups=places(MODE), tiled=True
    )
    own, halo = late(tile_start, innovations, obs_weights, own, halo, last)
    route = []
    for s in range(space_count):
        behind, ahead = (s - 1) % space_count, (s + 1) % space_count
        route.append((s * mode_count, ahead * mode_count))
        route.append((s * mode_count + last, behind * mode_count + last))
    halo = lax.ppermute(halo, SPACE + MODE, route)
    terms = project(own, halo, members, all_modes, last)
    part = jnp.sum(exchange(terms.reshape(lax.axis_size(NEAR), 1, -1), NEAR), axis=0)
    part = jnp.sum(everywhere(part, FAR), axis=0)
    coeff = everywhere(part, NEAR)
    increment, own_coeff = finish(coeff.reshape(MEMBERS, MODES), members, all_modes)
    return increment.reshape(OWN), own_coeff.T


def solution(mesh):
    finer = Mesh(mesh.devices.reshape(8, 2, 2, 4, 2, 2), SPACE + MODE)
    in_specs = (P(None, SPACE + MODE), P(MODE, SPACE), P(SPACE, None, None), P(SPACE, None), P(SPACE))
    out_specs = (P(SPACE + MODE), P(None, MODE))
    return jax.shard_map(
        on_device, mesh=finer, in_specs=in_specs, out_specs=out_specs, check_vma=False
    )
```

```python
import functools

import jax
import jax.numpy as jnp
import numpy as np
from jax import lax
from jax.experimental import pallas as pl
from jax.experimental.pallas import tpu as pltpu
from jax.sharding import Mesh
from jax.sharding import PartitionSpec as P

MEMBERS = 80
MODE_DEV = 4
MODES = 128
CELLS_DEV = 32768
TILE = 128
BLK_DEV = 128
OWN = 1024
OWN_TILES = OWN // TILE
LANES = 128
SUBLANES = 8
GROUP = 4
PIECE = 16
VMEM = pl.BlockSpec(memory_space=pltpu.VMEM)
SMALL = pltpu.CompilerParams(vmem_limit_bytes=12 * 2**20)
MODE = ("xhi", "zhi", "zlo", "core")
SPACE = ("y", "xlo")
NEAR = ("xlo", "xhi", "zlo", "core")
FAR = ("y", "zhi")
FIRST = {NEAR: {"xhi": 1, "zlo": 1}, FAR: {"y": 4, "zhi": 2}, MODE: {"xhi": 1, "zhi": 2}}


def mode_index():
    at = lax.axis_index(MODE[0])
    for axis in MODE[1:]:
        at = at * lax.axis_size(axis) + lax.axis_index(axis)
    return at


def split2(x):
    high = x.astype(jnp.bfloat16)
    return high, (x - high.astype(jnp.float32)).astype(jnp.bfloat16)


def find_field(last, begin_ref, innov_ref, obs_ref, own_ref, halo_ref, start_ref, ids, rows, held, acc, halo, begin_sem, row_sem, sems):
    m = mode_index()
    begin = pltpu.make_async_copy(begin_ref, start_ref, begin_sem)
    begin.start()
    pieces = [
        pltpu.make_async_copy(obs_ref.at[pl.ds(i * PIECE, PIECE)], held.at[pl.ds(i * PIECE, PIECE)], sems.at[i])
        for i in range(BLK_DEV // PIECE)
    ]
    pieces.append(pltpu.make_async_copy(innov_ref, rows, row_sem))
    for piece in pieces:
        piece.start()
    base = m * OWN
    first = jnp.where(m == 0, CELLS_DEV + TILE, 0)
    edge = (m == 0) | (m == last)
    acc[...] = jnp.zeros_like(acc)
    halo[...] = jnp.zeros_like(halo)
    begin.wait()

    def scan(b, count):
        start = start_ref[b]
        place = start - base
        far = start - first
        ids[count] = b
        hit = ((place > 0) & (place < OWN + TILE)) | (edge & (far > -TILE) & (far < TILE))
        return count + jnp.where(hit, 1, 0)

    count = lax.fori_loop(0, BLK_DEV, scan, jnp.int32(0), unroll=16)
    lane = lax.broadcasted_iota(jnp.int32, (1, LANES), 1)
    for piece in pieces:
        piece.wait()

    def add(g, carry):
        found = []
        for u in range(GROUP):
            i = g * GROUP + u
            valid = i < count
            b = jnp.where(valid, ids[i], 0)
            start = start_ref[b]
            row = rows[pl.ds(b, 1), :]
            high = row.astype(jnp.bfloat16).astype(jnp.float32)
            mid = (row - high).astype(jnp.bfloat16).astype(jnp.float32)
            low = row - high - mid
            parts = jnp.concatenate([high, mid, low, jnp.zeros((SUBLANES - 3, LANES), jnp.float32)], axis=0)
            adj = jnp.dot(parts.astype(jnp.bfloat16), held[b], preferred_element_type=jnp.float32)
            adj = adj + pltpu.roll(adj, SUBLANES - 1, 0) + pltpu.roll(adj, SUBLANES - 2, 0)
            off = lax.bitwise_and(start, TILE - 1)
            rolled = pltpu.roll(adj, off, 1)[0:1, :]
            front = jnp.where(lane >= off, rolled, 0.0)
            back = jnp.where(lane < off, rolled, 0.0)
            found.append((valid, start - base, start - first, front, back))
        for valid, place, far, front, back in found:

            @pl.when(valid & (place > 0) & (place < OWN + TILE))
            def _():
                seg = lax.shift_right_logical(place, 7)
                acc[pl.ds(seg, 1), :] += front
                acc[pl.ds(seg + 1, 1), :] += back

            @pl.when(valid & edge & (far > -TILE) & (far < TILE))
            def _():
                halo[...] += jnp.where(far >= 0, front, back)

        return carry

    lax.fori_loop(0, lax.shift_right_logical(count + GROUP - 1, 2), add, 0)
    own_ref[...] = acc[1 : 1 + OWN_TILES, :]
    halo_ref[...] = halo[...]


def waits_long():
    return lax.axis_index("zhi") < lax.axis_size("zhi") // 2


def early_kernel(last, modes_ref, begin_ref, innov_ref, obs_ref, laid_ref, own_ref, halo_ref, lay_sems, *scratch):
    part = modes_ref.shape[1] // 4
    copies = [
        pltpu.make_async_copy(
            modes_ref.at[:, pl.ds(q * part, part)], laid_ref.at[:, pl.ds((3 - q) * part, part)], lay_sems.at[q]
        )
        for q in range(4)
    ]
    for copy in copies:
        copy.start()

    @pl.when(waits_long())
    def _():
        find_field(last, begin_ref, innov_ref, obs_ref, own_ref, halo_ref, *scratch)

    for copy in copies:
        copy.wait()


def late_kernel(last, begin_ref, innov_ref, obs_ref, early_own_ref, early_halo_ref, own_ref, halo_ref, *scratch):
    @pl.when(waits_long())
    def _():
        own_ref[...] = early_own_ref[...]
        halo_ref[...] = early_halo_ref[...]

    @pl.when(jnp.logical_not(waits_long()))
    def _():
        find_field(last, begin_ref, innov_ref, obs_ref, own_ref, halo_ref, *scratch)


HBM = pl.BlockSpec(memory_space=pltpu.HBM)
FIELD = (jax.ShapeDtypeStruct((OWN_TILES, LANES), jnp.float32), jax.ShapeDtypeStruct((1, LANES), jnp.float32))


def field_scratch():
    return [
        pltpu.SMEM((BLK_DEV,), jnp.int32),
        pltpu.SMEM((BLK_DEV + GROUP,), jnp.int32),
        pltpu.VMEM((BLK_DEV, LANES), jnp.float32),
        pltpu.VMEM((BLK_DEV, TILE, TILE), jnp.bfloat16),
        pltpu.VMEM((2 * SUBLANES, LANES), jnp.float32),
        pltpu.VMEM((1, LANES), jnp.float32),
        pltpu.SemaphoreType.DMA,
        pltpu.SemaphoreType.DMA,
        pltpu.SemaphoreType.DMA((BLK_DEV // PIECE,)),
    ]


def in_hbm(*operands):
    return [pltpu.with_memory_space_constraint(x, pltpu.HBM) for x in operands]


def early(modes, tile_start, innovations, obs_weights, last):
    return pl.pallas_call(
        functools.partial(early_kernel, last),
        out_shape=(jax.ShapeDtypeStruct(modes.shape, modes.dtype),) + FIELD,
        in_specs=[HBM] * 4,
        out_specs=(VMEM,) * 3,
        scratch_shapes=[pltpu.SemaphoreType.DMA((4,))] + field_scratch(),
        compiler_params=SMALL,
        name="early",
    )(*in_hbm(modes, tile_start, innovations, obs_weights))


def late(tile_start, innovations, obs_weights, own, halo, last):
    return pl.pallas_call(
        functools.partial(late_kernel, last),
        out_shape=FIELD,
        in_specs=[HBM] * 3 + [VMEM] * 2,
        out_specs=(VMEM,) * 2,
        scratch_shapes=field_scratch(),
        compiler_params=SMALL,
        cost_estimate=pl.CostEstimate(flops=2**22, bytes_accessed=2**22, transcendentals=0),
        name="late",
    )(*in_hbm(tile_start, innovations, obs_weights), own, halo)


def project_kernel(last, own_ref, halo_ref, members_ref, modes_ref, out_ref):
    m = mode_index()
    halo = halo_ref[...]
    row = lax.broadcasted_iota(jnp.int32, (OWN_TILES, LANES), 0)
    takes = ((row == 0) & (m == 0)) | ((row == OWN_TILES - 1) & (m == last))
    weights = own_ref[...] + jnp.where(takes, halo, 0.0)
    contract = (((1,), (1,)), ((), ()))
    highs, lows = [], []
    for j in range(OWN_TILES):
        cells = slice(j * TILE, (j + 1) * TILE)
        high, low = split2(members_ref[:, cells].astype(jnp.float32) * weights[j : j + 1, :])
        highs.append(high)
        lows.append(low)
    modes = modes_ref[...]
    total = lax.dot_general(jnp.concatenate(highs, 1), modes, contract, preferred_element_type=jnp.float32)
    total += lax.dot_general(jnp.concatenate(lows, 1), modes, contract, preferred_element_type=jnp.float32)
    out_ref[...] = total


def project(own, halo, members, modes, last):
    return pl.pallas_call(
        functools.partial(project_kernel, last),
        out_shape=jax.ShapeDtypeStruct((MEMBERS, MODES), jnp.float32),
        in_specs=[VMEM] * 4,
        out_specs=VMEM,
        compiler_params=SMALL,
        name="project",
    )(own, halo, members, modes)


def finish_kernel(total_count, coeff_ref, members_ref, modes_ref, inc_ref, own_ref, turned):
    m = mode_place()
    coeff = coeff_ref[...]
    high, low = split2(coeff)
    modes = modes_ref[...]
    mixed = jnp.dot(high, modes, preferred_element_type=jnp.float32)
    mixed += jnp.dot(low, modes, preferred_element_type=jnp.float32)
    spread = jnp.sum(jnp.sum(coeff * coeff, axis=0, keepdims=True), axis=1, keepdims=True)
    factor = lax.rsqrt(1.0 + spread / total_count)
    turned[...] = coeff.T
    own_ref[...] = turned[pl.ds(m * MODE_DEV, MODE_DEV), :]
    mixed = mixed * members_ref[...].astype(jnp.float32)
    summed = jnp.sum(mixed, axis=0, keepdims=True) * (factor / (MEMBERS - 1))
    for j in range(OWN_TILES):
        inc_ref[j : j + 1, :] = summed[:, j * TILE : (j + 1) * TILE]


def finish(coeff, members, modes):
    return pl.pallas_call(
        functools.partial(finish_kernel, MEMBERS * MODES),
        out_shape=(
            jax.ShapeDtypeStruct((OWN_TILES, LANES), jnp.float32),
            jax.ShapeDtypeStruct((MODE_DEV, MEMBERS), jnp.float32),
        ),
        in_specs=[VMEM] * 3,
        out_specs=(VMEM, VMEM),
        scratch_shapes=[pltpu.VMEM((MODES, MEMBERS), jnp.float32)],
        compiler_params=SMALL,
        name="finish",
    )(coeff, members, modes)


def places(axis):
    sizes = [lax.axis_size(a) for a in axis]
    order = np.arange(np.prod(sizes)).reshape(sizes)
    for d, a in enumerate(axis):
        order = np.roll(order, -FIRST[axis].get(a, 0), axis=d)
    return [[int(place) for place in order.reshape(-1)]]


def mode_place():
    at = 0
    for axis in MODE:
        size = lax.axis_size(axis)
        at = at * size + lax.rem(lax.axis_index(axis) + (size - FIRST[MODE].get(axis, 0)), size)
    return at


def far_groups():
    sizes = [lax.axis_size(a) for a in FAR]
    order = np.array(places(FAR)).reshape(sizes)
    cores = lax.axis_size("core")
    return [[int(p) * cores + c for p in (order.T if c else order).reshape(-1)] for c in range(cores)]


def exchange(x, axis):
    groups = far_groups() if axis == FAR else places(axis)
    axis = FAR + ("core",) if axis == FAR else axis
    return lax.all_to_all(x, axis, split_axis=0, concat_axis=0, axis_index_groups=groups, tiled=True)


def everywhere(x, axis):
    return exchange(jnp.broadcast_to(x[None], (lax.axis_size(axis),) + x.shape), axis)


def on_device(members, modes, obs_weights, innovations, tile_start):
    mode_count = lax.axis_size(MODE)
    space_count = lax.axis_size(SPACE)
    last = mode_count - 1
    laid, own, halo = early(modes, tile_start, innovations, obs_weights, last)
    all_modes = lax.all_to_all(
        laid, MODE, split_axis=1, concat_axis=0, axis_index_groups=places(MODE), tiled=True
    )
    own, halo = late(tile_start, innovations, obs_weights, own, halo, last)
    route = []
    for s in range(space_count):
        behind, ahead = (s - 1) % space_count, (s + 1) % space_count
        route.append((s * mode_count, ahead * mode_count))
        route.append((s * mode_count + last, behind * mode_count + last))
    halo = lax.ppermute(halo, SPACE + MODE, route)
    terms = project(own, halo, members, all_modes, last)
    part = jnp.sum(exchange(terms.reshape(lax.axis_size(NEAR), 1, -1), NEAR), axis=0)
    part = jnp.sum(everywhere(part, FAR), axis=0)
    coeff = everywhere(part, NEAR)
    increment, own_coeff = finish(coeff.reshape(MEMBERS, MODES), members, all_modes)
    return increment.reshape(OWN), own_coeff.T


def solution(mesh):
    finer = Mesh(mesh.devices.reshape(8, 2, 2, 4, 2, 2), SPACE + MODE)
    in_specs = (P(None, SPACE + MODE), P(MODE, SPACE), P(SPACE, None, None), P(SPACE, None), P(SPACE))
    out_specs = (P(SPACE + MODE), P(None, MODE))
    return jax.shard_map(
        on_device, mesh=finer, in_specs=in_specs, out_specs=out_specs, check_vma=False
    )
```

```python
import functools

import jax
import jax.numpy as jnp
import numpy as np
from jax import lax
from jax.experimental import pallas as pl
from jax.experimental.pallas import tpu as pltpu
from jax.sharding import Mesh
from jax.sharding import PartitionSpec as P

MEMBERS = 80
MODE_DEV = 4
MODES = 128
CELLS_DEV = 32768
TILE = 128
BLK_DEV = 128
OWN = 1024
OWN_TILES = OWN // TILE
LANES = 128
SUBLANES = 8
GROUP = 4
PIECE = 16
PIECES = 8
VMEM = pl.BlockSpec(memory_space=pltpu.VMEM)
SMALL = pltpu.CompilerParams(vmem_limit_bytes=12 * 2**20)
MODE = ("xhi", "zhi", "zlo", "core")
SPACE = ("y", "xlo")
NEAR = ("xlo", "xhi", "zlo", "core")
FAR = ("y", "zhi")
FIRST = {NEAR: {"xhi": 1, "zlo": 1}, FAR: {"y": 4, "zhi": 2}, MODE: {"xhi": 1, "zhi": 2}}


def mode_index():
    at = lax.axis_index(MODE[0])
    for axis in MODE[1:]:
        at = at * lax.axis_size(axis) + lax.axis_index(axis)
    return at


def split2(x):
    high = x.astype(jnp.bfloat16)
    return high, (x - high.astype(jnp.float32)).astype(jnp.bfloat16)


def find_field(last, begin_ref, innov_ref, obs_ref, own_ref, halo_ref, start_ref, ids, rows, held, acc, halo, begin_sem, row_sem, sems):
    m = mode_index()
    begin = pltpu.make_async_copy(begin_ref, start_ref, begin_sem)
    begin.start()
    pieces = [
        pltpu.make_async_copy(obs_ref.at[pl.ds(i * PIECE, PIECE)], held.at[pl.ds(i * PIECE, PIECE)], sems.at[i])
        for i in range(BLK_DEV // PIECE)
    ]
    pieces.append(pltpu.make_async_copy(innov_ref, rows, row_sem))
    for piece in pieces:
        piece.start()
    base = m * OWN
    first = jnp.where(m == 0, CELLS_DEV + TILE, 0)
    edge = (m == 0) | (m == last)
    acc[...] = jnp.zeros_like(acc)
    halo[...] = jnp.zeros_like(halo)
    begin.wait()

    def scan(b, count):
        start = start_ref[b]
        place = start - base
        far = start - first
        ids[count] = b
        hit = ((place > 0) & (place < OWN + TILE)) | (edge & (far > -TILE) & (far < TILE))
        return count + jnp.where(hit, 1, 0)

    count = lax.fori_loop(0, BLK_DEV, scan, jnp.int32(0), unroll=16)
    lane = lax.broadcasted_iota(jnp.int32, (1, LANES), 1)
    for piece in pieces:
        piece.wait()

    def add(g, carry):
        found = []
        for u in range(GROUP):
            i = g * GROUP + u
            valid = i < count
            b = jnp.where(valid, ids[i], 0)
            start = start_ref[b]
            row = rows[pl.ds(b, 1), :]
            high = row.astype(jnp.bfloat16).astype(jnp.float32)
            mid = (row - high).astype(jnp.bfloat16).astype(jnp.float32)
            low = row - high - mid
            parts = jnp.concatenate([high, mid, low, jnp.zeros((SUBLANES - 3, LANES), jnp.float32)], axis=0)
            adj = jnp.dot(parts.astype(jnp.bfloat16), held[b], preferred_element_type=jnp.float32)
            adj = adj + pltpu.roll(adj, SUBLANES - 1, 0) + pltpu.roll(adj, SUBLANES - 2, 0)
            off = lax.bitwise_and(start, TILE - 1)
            rolled = pltpu.roll(adj, off, 1)[0:1, :]
            front = jnp.where(lane >= off, rolled, 0.0)
            back = jnp.where(lane < off, rolled, 0.0)
            found.append((valid, start - base, start - first, front, back))
        for valid, place, far, front, back in found:

            @pl.when(valid & (place > 0) & (place < OWN + TILE))
            def _():
                seg = lax.shift_right_logical(place, 7)
                acc[pl.ds(seg, 1), :] += front
                acc[pl.ds(seg + 1, 1), :] += back

            @pl.when(valid & edge & (far > -TILE) & (far < TILE))
            def _():
                halo[...] += jnp.where(far >= 0, front, back)

        return carry

    lax.fori_loop(0, lax.shift_right_logical(count + GROUP - 1, 2), add, 0)
    own_ref[...] = acc[1 : 1 + OWN_TILES, :]
    halo_ref[...] = halo[...]


def waits_long():
    return lax.axis_index("zhi") < lax.axis_size("zhi") // 2


def early_kernel(last, modes_ref, begin_ref, innov_ref, obs_ref, laid_ref, own_ref, halo_ref, lay_sems, *scratch):
    part = modes_ref.shape[0] // PIECES
    copies = []
    for q in range(PIECES):
        to = (3 - 4 * q // PIECES) * (PIECES // 4) + q % (PIECES // 4)
        copies.append(
            pltpu.make_async_copy(modes_ref.at[pl.ds(q * part, part)], laid_ref.at[pl.ds(to * part, part)], lay_sems.at[q])
        )
    for copy in copies:
        copy.start()

    @pl.when(waits_long())
    def _():
        find_field(last, begin_ref, innov_ref, obs_ref, own_ref, halo_ref, *scratch)

    for copy in copies:
        copy.wait()


def late_kernel(last, begin_ref, innov_ref, obs_ref, early_own_ref, early_halo_ref, own_ref, halo_ref, *scratch):
    @pl.when(waits_long())
    def _():
        own_ref[...] = early_own_ref[...]
        halo_ref[...] = early_halo_ref[...]

    @pl.when(jnp.logical_not(waits_long()))
    def _():
        find_field(last, begin_ref, innov_ref, obs_ref, own_ref, halo_ref, *scratch)


HBM = pl.BlockSpec(memory_space=pltpu.HBM)
FIELD = (jax.ShapeDtypeStruct((OWN_TILES, LANES), jnp.float32), jax.ShapeDtypeStruct((1, LANES), jnp.float32))


def field_scratch():
    return [
        pltpu.SMEM((BLK_DEV,), jnp.int32),
        pltpu.SMEM((BLK_DEV + GROUP,), jnp.int32),
        pltpu.VMEM((BLK_DEV, LANES), jnp.float32),
        pltpu.VMEM((BLK_DEV, TILE, TILE), jnp.bfloat16),
        pltpu.VMEM((2 * SUBLANES, LANES), jnp.float32),
        pltpu.VMEM((1, LANES), jnp.float32),
        pltpu.SemaphoreType.DMA,
        pltpu.SemaphoreType.DMA,
        pltpu.SemaphoreType.DMA((BLK_DEV // PIECE,)),
    ]


def in_hbm(*operands):
    return [pltpu.with_memory_space_constraint(x, pltpu.HBM) for x in operands]


def early(modes, tile_start, innovations, obs_weights, last):
    return pl.pallas_call(
        functools.partial(early_kernel, last),
        out_shape=(jax.ShapeDtypeStruct(modes.shape, modes.dtype),) + FIELD,
        in_specs=[HBM] * 4,
        out_specs=(VMEM,) * 3,
        scratch_shapes=[pltpu.SemaphoreType.DMA((PIECES,))] + field_scratch(),
        compiler_params=SMALL,
        name="early",
    )(*in_hbm(modes, tile_start, innovations, obs_weights))


def late(tile_start, innovations, obs_weights, own, halo, last):
    return pl.pallas_call(
        functools.partial(late_kernel, last),
        out_shape=FIELD,
        in_specs=[HBM] * 3 + [VMEM] * 2,
        out_specs=(VMEM,) * 2,
        scratch_shapes=field_scratch(),
        compiler_params=SMALL,
        cost_estimate=pl.CostEstimate(flops=2**22, bytes_accessed=2**22, transcendentals=0),
        name="late",
    )(*in_hbm(tile_start, innovations, obs_weights), own, halo)


def project_kernel(last, own_ref, halo_ref, members_ref, modes_ref, out_ref):
    m = mode_index()
    halo = halo_ref[...]
    row = lax.broadcasted_iota(jnp.int32, (OWN_TILES, LANES), 0)
    takes = ((row == 0) & (m == 0)) | ((row == OWN_TILES - 1) & (m == last))
    weights = own_ref[...] + jnp.where(takes, halo, 0.0)
    contract = (((1,), (1,)), ((), ()))
    highs, lows = [], []
    for j in range(OWN_TILES):
        cells = slice(j * TILE, (j + 1) * TILE)
        high, low = split2(members_ref[:, cells].astype(jnp.float32) * weights[j : j + 1, :])
        highs.append(high)
        lows.append(low)
    modes = modes_ref[...]
    total = lax.dot_general(jnp.concatenate(highs, 1), modes, contract, preferred_element_type=jnp.float32)
    total += lax.dot_general(jnp.concatenate(lows, 1), modes, contract, preferred_element_type=jnp.float32)
    out_ref[...] = total


def project(own, halo, members, modes, last):
    return pl.pallas_call(
        functools.partial(project_kernel, last),
        out_shape=jax.ShapeDtypeStruct((MEMBERS, MODES), jnp.float32),
        in_specs=[VMEM] * 4,
        out_specs=VMEM,
        compiler_params=SMALL,
        name="project",
    )(own, halo, members, modes)


def finish_kernel(total_count, coeff_ref, members_ref, modes_ref, inc_ref, own_ref, turned):
    m = mode_place()
    coeff = coeff_ref[...]
    high, low = split2(coeff)
    modes = modes_ref[...]
    mixed = jnp.dot(high, modes, preferred_element_type=jnp.float32)
    mixed += jnp.dot(low, modes, preferred_element_type=jnp.float32)
    spread = jnp.sum(jnp.sum(coeff * coeff, axis=0, keepdims=True), axis=1, keepdims=True)
    factor = lax.rsqrt(1.0 + spread / total_count)
    turned[...] = coeff.T
    own_ref[...] = turned[pl.ds(m * MODE_DEV, MODE_DEV), :]
    mixed = mixed * members_ref[...].astype(jnp.float32)
    summed = jnp.sum(mixed, axis=0, keepdims=True) * (factor / (MEMBERS - 1))
    for j in range(OWN_TILES):
        inc_ref[j : j + 1, :] = summed[:, j * TILE : (j + 1) * TILE]


def finish(coeff, members, modes):
    return pl.pallas_call(
        functools.partial(finish_kernel, MEMBERS * MODES),
        out_shape=(
            jax.ShapeDtypeStruct((OWN_TILES, LANES), jnp.float32),
            jax.ShapeDtypeStruct((MODE_DEV, MEMBERS), jnp.float32),
        ),
        in_specs=[VMEM] * 3,
        out_specs=(VMEM, VMEM),
        scratch_shapes=[pltpu.VMEM((MODES, MEMBERS), jnp.float32)],
        compiler_params=SMALL,
        name="finish",
    )(coeff, members, modes)


def places(axis):
    sizes = [lax.axis_size(a) for a in axis]
    order = np.arange(np.prod(sizes)).reshape(sizes)
    for d, a in enumerate(axis):
        order = np.roll(order, -FIRST[axis].get(a, 0), axis=d)
    return [[int(place) for place in order.reshape(-1)]]


def mode_place():
    at = 0
    for axis in MODE:
        size = lax.axis_size(axis)
        at = at * size + lax.rem(lax.axis_index(axis) + (size - FIRST[MODE].get(axis, 0)), size)
    return at


def exchange(x, axis):
    return lax.all_to_all(x, axis, split_axis=0, concat_axis=0, axis_index_groups=places(axis), tiled=True)


def everywhere(x, axis):
    return exchange(jnp.broadcast_to(x[None], (lax.axis_size(axis),) + x.shape), axis)


def on_device(members, modes, obs_weights, innovations, tile_start):
    mode_count = lax.axis_size(MODE)
    space_count = lax.axis_size(SPACE)
    last = mode_count - 1
    columns = modes.reshape(MODE_DEV, -1, LANES).transpose(1, 0, 2)
    laid, own, halo = early(columns, tile_start, innovations, obs_weights, last)
    laid = laid.transpose(1, 0, 2).reshape(modes.shape)
    all_modes = lax.all_to_all(
        laid, MODE, split_axis=1, concat_axis=0, axis_index_groups=places(MODE), tiled=True
    )
    own, halo = late(tile_start, innovations, obs_weights, own, halo, last)
    route = []
    for s in range(space_count):
        behind, ahead = (s - 1) % space_count, (s + 1) % space_count
        route.append((s * mode_count, ahead * mode_count))
        route.append((s * mode_count + last, behind * mode_count + last))
    halo = lax.ppermute(halo, SPACE + MODE, route)
    terms = project(own, halo, members, all_modes, last)
    part = jnp.sum(exchange(terms.reshape(lax.axis_size(NEAR), 1, -1), NEAR), axis=0)
    part = jnp.sum(everywhere(part, FAR), axis=0)
    coeff = everywhere(part, NEAR)
    increment, own_coeff = finish(coeff.reshape(MEMBERS, MODES), members, all_modes)
    return increment.reshape(OWN), own_coeff.T


def solution(mesh):
    finer = Mesh(mesh.devices.reshape(8, 2, 2, 4, 2, 2), SPACE + MODE)
    in_specs = (P(None, SPACE + MODE), P(MODE, SPACE), P(SPACE, None, None), P(SPACE, None), P(SPACE))
    out_specs = (P(SPACE + MODE), P(None, MODE))
    return jax.shard_map(
        on_device, mesh=finer, in_specs=in_specs, out_specs=out_specs, check_vma=False
    )
```

```python
import functools

import jax
import jax.numpy as jnp
import numpy as np
from jax import lax
from jax.experimental import pallas as pl
from jax.experimental.pallas import tpu as pltpu
from jax.sharding import Mesh
from jax.sharding import PartitionSpec as P

MEMBERS = 80
MODE_DEV = 4
MODES = 128
CELLS_DEV = 32768
TILE = 128
BLK_DEV = 128
OWN = 1024
OWN_TILES = OWN // TILE
LANES = 128
SUBLANES = 8
GROUP = 4
PIECE = 16
VMEM = pl.BlockSpec(memory_space=pltpu.VMEM)
SMALL = pltpu.CompilerParams(vmem_limit_bytes=12 * 2**20)
MODE = ("xhi", "zhi", "zlo", "core")
SPACE = ("y", "xlo")
NEAR = ("xlo", "xhi", "zlo", "core")
FAR = ("y", "zhi")
FIRST = {NEAR: {"xhi": 1, "zlo": 1}, FAR: {"y": 4, "zhi": 2}, MODE: {"xhi": 1, "zhi": 2}}


def mode_index():
    at = lax.axis_index(MODE[0])
    for axis in MODE[1:]:
        at = at * lax.axis_size(axis) + lax.axis_index(axis)
    return at


def split2(x):
    high = x.astype(jnp.bfloat16)
    return high, (x - high.astype(jnp.float32)).astype(jnp.bfloat16)


def find_field(last, begin_ref, innov_ref, obs_ref, own_ref, halo_ref, start_ref, ids, rows, held, acc, halo, begin_sem, row_sem, sems):
    m = mode_index()
    begin = pltpu.make_async_copy(begin_ref, start_ref, begin_sem)
    begin.start()
    pieces = [
        pltpu.make_async_copy(obs_ref.at[pl.ds(i * PIECE, PIECE)], held.at[pl.ds(i * PIECE, PIECE)], sems.at[i])
        for i in range(BLK_DEV // PIECE)
    ]
    pieces.append(pltpu.make_async_copy(innov_ref, rows, row_sem))
    for piece in pieces:
        piece.start()
    base = m * OWN
    first = jnp.where(m == 0, CELLS_DEV + TILE, 0)
    edge = (m == 0) | (m == last)
    acc[...] = jnp.zeros_like(acc)
    halo[...] = jnp.zeros_like(halo)
    begin.wait()

    def scan(b, count):
        start = start_ref[b]
        place = start - base
        far = start - first
        ids[count] = b
        hit = ((place > 0) & (place < OWN + TILE)) | (edge & (far > -TILE) & (far < TILE))
        return count + jnp.where(hit, 1, 0)

    count = lax.fori_loop(0, BLK_DEV, scan, jnp.int32(0), unroll=16)
    lane = lax.broadcasted_iota(jnp.int32, (1, LANES), 1)
    for piece in pieces:
        piece.wait()

    def add(g, carry):
        found = []
        for u in range(GROUP):
            i = g * GROUP + u
            valid = i < count
            b = jnp.where(valid, ids[i], 0)
            start = start_ref[b]
            row = rows[pl.ds(b, 1), :]
            high = row.astype(jnp.bfloat16).astype(jnp.float32)
            mid = (row - high).astype(jnp.bfloat16).astype(jnp.float32)
            low = row - high - mid
            parts = jnp.concatenate([high, mid, low, jnp.zeros((SUBLANES - 3, LANES), jnp.float32)], axis=0)
            adj = jnp.dot(parts.astype(jnp.bfloat16), held[b], preferred_element_type=jnp.float32)
            adj = adj + pltpu.roll(adj, SUBLANES - 1, 0) + pltpu.roll(adj, SUBLANES - 2, 0)
            off = lax.bitwise_and(start, TILE - 1)
            rolled = pltpu.roll(adj, off, 1)[0:1, :]
            front = jnp.where(lane >= off, rolled, 0.0)
            back = jnp.where(lane < off, rolled, 0.0)
            found.append((valid, start - base, start - first, front, back))
        for valid, place, far, front, back in found:

            @pl.when(valid & (place > 0) & (place < OWN + TILE))
            def _():
                seg = lax.shift_right_logical(place, 7)
                acc[pl.ds(seg, 1), :] += front
                acc[pl.ds(seg + 1, 1), :] += back

            @pl.when(valid & edge & (far > -TILE) & (far < TILE))
            def _():
                halo[...] += jnp.where(far >= 0, front, back)

        return carry

    lax.fori_loop(0, lax.shift_right_logical(count + GROUP - 1, 2), add, 0)
    own_ref[...] = acc[1 : 1 + OWN_TILES, :]
    halo_ref[...] = halo[...]


def waits_long():
    return lax.axis_index("zhi") < lax.axis_size("zhi") // 2


def early_kernel(last, begin_ref, innov_ref, obs_ref, own_ref, halo_ref, *scratch):
    @pl.when(waits_long())
    def _():
        find_field(last, begin_ref, innov_ref, obs_ref, own_ref, halo_ref, *scratch)


def late_kernel(last, begin_ref, innov_ref, obs_ref, early_own_ref, early_halo_ref, own_ref, halo_ref, *scratch):
    @pl.when(waits_long())
    def _():
        own_ref[...] = early_own_ref[...]
        halo_ref[...] = early_halo_ref[...]

    @pl.when(jnp.logical_not(waits_long()))
    def _():
        find_field(last, begin_ref, innov_ref, obs_ref, own_ref, halo_ref, *scratch)


HBM = pl.BlockSpec(memory_space=pltpu.HBM)
FIELD = (jax.ShapeDtypeStruct((OWN_TILES, LANES), jnp.float32), jax.ShapeDtypeStruct((1, LANES), jnp.float32))


def field_scratch():
    return [
        pltpu.SMEM((BLK_DEV,), jnp.int32),
        pltpu.SMEM((BLK_DEV + GROUP,), jnp.int32),
        pltpu.VMEM((BLK_DEV, LANES), jnp.float32),
        pltpu.VMEM((BLK_DEV, TILE, TILE), jnp.bfloat16),
        pltpu.VMEM((2 * SUBLANES, LANES), jnp.float32),
        pltpu.VMEM((1, LANES), jnp.float32),
        pltpu.SemaphoreType.DMA,
        pltpu.SemaphoreType.DMA,
        pltpu.SemaphoreType.DMA((BLK_DEV // PIECE,)),
    ]


def in_hbm(*operands):
    return [pltpu.with_memory_space_constraint(x, pltpu.HBM) for x in operands]


def early(tile_start, innovations, obs_weights, last):
    return pl.pallas_call(
        functools.partial(early_kernel, last),
        out_shape=FIELD,
        in_specs=[HBM] * 3,
        out_specs=(VMEM,) * 2,
        scratch_shapes=field_scratch(),
        compiler_params=SMALL,
        name="early",
    )(*in_hbm(tile_start, innovations, obs_weights))


def late(tile_start, innovations, obs_weights, own, halo, last):
    return pl.pallas_call(
        functools.partial(late_kernel, last),
        out_shape=FIELD,
        in_specs=[HBM] * 3 + [VMEM] * 2,
        out_specs=(VMEM,) * 2,
        scratch_shapes=field_scratch(),
        compiler_params=SMALL,
        cost_estimate=pl.CostEstimate(flops=2**22, bytes_accessed=2**22, transcendentals=0),
        name="late",
    )(*in_hbm(tile_start, innovations, obs_weights), own, halo)


def project_kernel(last, own_ref, halo_ref, members_ref, modes_ref, out_ref):
    m = mode_index()
    halo = halo_ref[...]
    row = lax.broadcasted_iota(jnp.int32, (OWN_TILES, LANES), 0)
    takes = ((row == 0) & (m == 0)) | ((row == OWN_TILES - 1) & (m == last))
    weights = own_ref[...] + jnp.where(takes, halo, 0.0)
    contract = (((1,), (1,)), ((), ()))
    highs, lows = [], []
    for j in range(OWN_TILES):
        cells = slice(j * TILE, (j + 1) * TILE)
        high, low = split2(members_ref[:, cells].astype(jnp.float32) * weights[j : j + 1, :])
        highs.append(high)
        lows.append(low)
    modes = modes_ref[...]
    total = lax.dot_general(jnp.concatenate(highs, 1), modes, contract, preferred_element_type=jnp.float32)
    total += lax.dot_general(jnp.concatenate(lows, 1), modes, contract, preferred_element_type=jnp.float32)
    out_ref[...] = total


def project(own, halo, members, modes, last):
    return pl.pallas_call(
        functools.partial(project_kernel, last),
        out_shape=jax.ShapeDtypeStruct((MEMBERS, MODES), jnp.float32),
        in_specs=[VMEM] * 4,
        out_specs=VMEM,
        compiler_params=SMALL,
        name="project",
    )(own, halo, members, modes)


def finish_kernel(total_count, coeff_ref, members_ref, modes_ref, inc_ref, own_ref, turned):
    m = mode_place()
    coeff = coeff_ref[...]
    high, low = split2(coeff)
    modes = modes_ref[...]
    mixed = jnp.dot(high, modes, preferred_element_type=jnp.float32)
    mixed += jnp.dot(low, modes, preferred_element_type=jnp.float32)
    spread = jnp.sum(jnp.sum(coeff * coeff, axis=0, keepdims=True), axis=1, keepdims=True)
    factor = lax.rsqrt(1.0 + spread / total_count)
    turned[...] = coeff.T
    own_ref[...] = turned[pl.ds(m * MODE_DEV, MODE_DEV), :]
    mixed = mixed * members_ref[...].astype(jnp.float32)
    summed = jnp.sum(mixed, axis=0, keepdims=True) * (factor / (MEMBERS - 1))
    for j in range(OWN_TILES):
        inc_ref[j : j + 1, :] = summed[:, j * TILE : (j + 1) * TILE]


def finish(coeff, members, modes):
    return pl.pallas_call(
        functools.partial(finish_kernel, MEMBERS * MODES),
        out_shape=(
            jax.ShapeDtypeStruct((OWN_TILES, LANES), jnp.float32),
            jax.ShapeDtypeStruct((MODE_DEV, MEMBERS), jnp.float32),
        ),
        in_specs=[VMEM] * 3,
        out_specs=(VMEM, VMEM),
        scratch_shapes=[pltpu.VMEM((MODES, MEMBERS), jnp.float32)],
        compiler_params=SMALL,
        name="finish",
    )(coeff, members, modes)


def places(axis):
    sizes = [lax.axis_size(a) for a in axis]
    order = np.arange(np.prod(sizes)).reshape(sizes)
    for d, a in enumerate(axis):
        order = np.roll(order, -FIRST[axis].get(a, 0), axis=d)
    return [[int(place) for place in order.reshape(-1)]]


def mode_place():
    at = 0
    for axis in MODE:
        size = lax.axis_size(axis)
        at = at * size + lax.rem(lax.axis_index(axis) + (size - FIRST[MODE].get(axis, 0)), size)
    return at


def exchange(x, axis):
    return lax.all_to_all(x, axis, split_axis=0, concat_axis=0, axis_index_groups=places(axis), tiled=True)


def everywhere(x, axis):
    return exchange(jnp.broadcast_to(x[None], (lax.axis_size(axis),) + x.shape), axis)


def on_device(members, modes, obs_weights, innovations, tile_start):
    mode_count = lax.axis_size(MODE)
    space_count = lax.axis_size(SPACE)
    last = mode_count - 1
    own, halo = early(tile_start, innovations, obs_weights, last)
    laid = jnp.concatenate(jnp.split(modes, 4, axis=1)[::-1], axis=1)
    laid, own, halo = lax.optimization_barrier((laid, own, halo))
    all_modes = lax.all_to_all(
        laid, MODE, split_axis=1, concat_axis=0, axis_index_groups=places(MODE), tiled=True
    )
    own, halo = late(tile_start, innovations, obs_weights, own, halo, last)
    route = []
    for s in range(space_count):
        behind, ahead = (s - 1) % space_count, (s + 1) % space_count
        route.append((s * mode_count, ahead * mode_count))
        route.append((s * mode_count + last, behind * mode_count + last))
    halo = lax.ppermute(halo, SPACE + MODE, route)
    terms = project(own, halo, members, all_modes, last)
    part = jnp.sum(exchange(terms.reshape(lax.axis_size(NEAR), 1, -1), NEAR), axis=0)
    part = jnp.sum(everywhere(part, FAR), axis=0)
    coeff = everywhere(part, NEAR)
    increment, own_coeff = finish(coeff.reshape(MEMBERS, MODES), members, all_modes)
    return increment.reshape(OWN), own_coeff.T


def solution(mesh):
    finer = Mesh(mesh.devices.reshape(8, 2, 2, 4, 2, 2), SPACE + MODE)
    in_specs = (P(None, SPACE + MODE), P(MODE, SPACE), P(SPACE, None, None), P(SPACE, None), P(SPACE))
    out_specs = (P(SPACE + MODE), P(None, MODE))
    return jax.shard_map(
        on_device, mesh=finer, in_specs=in_specs, out_specs=out_specs, check_vma=False
    )
```

```python
import functools

import jax
import jax.numpy as jnp
import numpy as np
from jax import lax
from jax.experimental import pallas as pl
from jax.experimental.pallas import tpu as pltpu
from jax.sharding import Mesh
from jax.sharding import PartitionSpec as P

MEMBERS = 80
MODE_DEV = 4
MODES = 128
CELLS_DEV = 32768
TILE = 128
BLK_DEV = 128
OWN = 1024
OWN_TILES = OWN // TILE
LANES = 128
SUBLANES = 8
GROUP = 4
PIECE = 16
VMEM = pl.BlockSpec(memory_space=pltpu.VMEM)
SMALL = pltpu.CompilerParams(vmem_limit_bytes=12 * 2**20)
MODE = ("xhi", "zhi", "zlo", "core")
SPACE = ("y", "xlo")
NEAR = ("xlo", "xhi", "zlo", "core")
FAR = ("y", "zhi")
FIRST = {NEAR: {"xhi": 1, "zlo": 1}, FAR: {"y": 4, "zhi": 2}}


def mode_index():
    at = lax.axis_index(MODE[0])
    for axis in MODE[1:]:
        at = at * lax.axis_size(axis) + lax.axis_index(axis)
    return at


def split2(x):
    high = x.astype(jnp.bfloat16)
    return high, (x - high.astype(jnp.float32)).astype(jnp.bfloat16)


def field_kernel(last, begin_ref, innov_ref, obs_ref, own_ref, halo_ref, start_ref, ids, rows, held, acc, halo, begin_sem, row_sem, sems):
    m = mode_index()
    begin = pltpu.make_async_copy(begin_ref, start_ref, begin_sem)
    begin.start()
    pieces = [
        pltpu.make_async_copy(obs_ref.at[pl.ds(i * PIECE, PIECE)], held.at[pl.ds(i * PIECE, PIECE)], sems.at[i])
        for i in range(BLK_DEV // PIECE)
    ]
    pieces.append(pltpu.make_async_copy(innov_ref, rows, row_sem))
    for piece in pieces:
        piece.start()
    base = m * OWN
    first = jnp.where(m == 0, CELLS_DEV + TILE, 0)
    edge = (m == 0) | (m == last)
    acc[...] = jnp.zeros_like(acc)
    halo[...] = jnp.zeros_like(halo)
    begin.wait()

    def scan(b, count):
        start = start_ref[b]
        place = start - base
        far = start - first
        ids[count] = b
        hit = ((place > 0) & (place < OWN + TILE)) | (edge & (far > -TILE) & (far < TILE))
        return count + jnp.where(hit, 1, 0)

    count = lax.fori_loop(0, BLK_DEV, scan, jnp.int32(0), unroll=16)
    lane = lax.broadcasted_iota(jnp.int32, (1, LANES), 1)
    for piece in pieces:
        piece.wait()

    def add(g, carry):
        found = []
        for u in range(GROUP):
            i = g * GROUP + u
            valid = i < count
            b = jnp.where(valid, ids[i], 0)
            start = start_ref[b]
            row = rows[pl.ds(b, 1), :]
            high = row.astype(jnp.bfloat16).astype(jnp.float32)
            mid = (row - high).astype(jnp.bfloat16).astype(jnp.float32)
            low = row - high - mid
            parts = jnp.concatenate([high, mid, low, jnp.zeros((SUBLANES - 3, LANES), jnp.float32)], axis=0)
            adj = jnp.dot(parts.astype(jnp.bfloat16), held[b], preferred_element_type=jnp.float32)
            adj = adj + pltpu.roll(adj, SUBLANES - 1, 0) + pltpu.roll(adj, SUBLANES - 2, 0)
            off = lax.bitwise_and(start, TILE - 1)
            rolled = pltpu.roll(adj, off, 1)[0:1, :]
            front = jnp.where(lane >= off, rolled, 0.0)
            back = jnp.where(lane < off, rolled, 0.0)
            found.append((valid, start - base, start - first, front, back))
        for valid, place, far, front, back in found:

            @pl.when(valid & (place > 0) & (place < OWN + TILE))
            def _():
                seg = lax.shift_right_logical(place, 7)
                acc[pl.ds(seg, 1), :] += front
                acc[pl.ds(seg + 1, 1), :] += back

            @pl.when(valid & edge & (far > -TILE) & (far < TILE))
            def _():
                halo[...] += jnp.where(far >= 0, front, back)

        return carry

    lax.fori_loop(0, lax.shift_right_logical(count + GROUP - 1, 2), add, 0)
    own_ref[...] = acc[1 : 1 + OWN_TILES, :]
    halo_ref[...] = halo[...]


def field(tile_start, innovations, obs_weights, last):
    kept = [pltpu.with_memory_space_constraint(x, pltpu.HBM) for x in (tile_start, innovations, obs_weights)]
    return pl.pallas_call(
        functools.partial(field_kernel, last),
        out_shape=(
            jax.ShapeDtypeStruct((OWN_TILES, LANES), jnp.float32),
            jax.ShapeDtypeStruct((1, LANES), jnp.float32),
        ),
        in_specs=[pl.BlockSpec(memory_space=pltpu.HBM)] * 3,
        out_specs=(VMEM, VMEM),
        scratch_shapes=[
            pltpu.SMEM((BLK_DEV,), jnp.int32),
            pltpu.SMEM((BLK_DEV + GROUP,), jnp.int32),
            pltpu.VMEM((BLK_DEV, LANES), jnp.float32),
            pltpu.VMEM((BLK_DEV, TILE, TILE), jnp.bfloat16),
            pltpu.VMEM((2 * SUBLANES, LANES), jnp.float32),
            pltpu.VMEM((1, LANES), jnp.float32),
            pltpu.SemaphoreType.DMA,
            pltpu.SemaphoreType.DMA,
            pltpu.SemaphoreType.DMA((BLK_DEV // PIECE,)),
        ],
        compiler_params=SMALL,
        cost_estimate=pl.CostEstimate(flops=2**22, bytes_accessed=2**22, transcendentals=0),
        name="field",
    )(*kept)


def project_kernel(last, own_ref, halo_ref, members_ref, modes_ref, out_ref):
    m = mode_index()
    halo = halo_ref[...]
    row = lax.broadcasted_iota(jnp.int32, (OWN_TILES, LANES), 0)
    takes = ((row == 0) & (m == 0)) | ((row == OWN_TILES - 1) & (m == last))
    weights = own_ref[...] + jnp.where(takes, halo, 0.0)
    contract = (((1,), (1,)), ((), ()))
    highs, lows = [], []
    for j in range(OWN_TILES):
        cells = slice(j * TILE, (j + 1) * TILE)
        high, low = split2(members_ref[:, cells].astype(jnp.float32) * weights[j : j + 1, :])
        highs.append(high)
        lows.append(low)
    modes = modes_ref[...]
    total = lax.dot_general(jnp.concatenate(highs, 1), modes, contract, preferred_element_type=jnp.float32)
    total += lax.dot_general(jnp.concatenate(lows, 1), modes, contract, preferred_element_type=jnp.float32)
    out_ref[...] = total


def project(own, halo, members, modes, last):
    return pl.pallas_call(
        functools.partial(project_kernel, last),
        out_shape=jax.ShapeDtypeStruct((MEMBERS, MODES), jnp.float32),
        in_specs=[VMEM] * 4,
        out_specs=VMEM,
        compiler_params=SMALL,
        name="project",
    )(own, halo, members, modes)


def finish_kernel(total_count, coeff_ref, members_ref, modes_ref, inc_ref, own_ref, turned):
    m = mode_index()
    coeff = coeff_ref[...]
    high, low = split2(coeff)
    modes = modes_ref[...]
    mixed = jnp.dot(high, modes, preferred_element_type=jnp.float32)
    mixed += jnp.dot(low, modes, preferred_element_type=jnp.float32)
    spread = jnp.sum(jnp.sum(coeff * coeff, axis=0, keepdims=True), axis=1, keepdims=True)
    factor = lax.rsqrt(1.0 + spread / total_count)
    turned[...] = coeff.T
    own_ref[...] = turned[pl.ds(m * MODE_DEV, MODE_DEV), :]
    mixed = mixed * members_ref[...].astype(jnp.float32)
    summed = jnp.sum(mixed, axis=0, keepdims=True) * (factor / (MEMBERS - 1))
    for j in range(OWN_TILES):
        inc_ref[j : j + 1, :] = summed[:, j * TILE : (j + 1) * TILE]


def finish(coeff, members, modes):
    return pl.pallas_call(
        functools.partial(finish_kernel, MEMBERS * MODES),
        out_shape=(
            jax.ShapeDtypeStruct((OWN_TILES, LANES), jnp.float32),
            jax.ShapeDtypeStruct((MODE_DEV, MEMBERS), jnp.float32),
        ),
        in_specs=[VMEM] * 3,
        out_specs=(VMEM, VMEM),
        scratch_shapes=[pltpu.VMEM((MODES, MEMBERS), jnp.float32)],
        compiler_params=SMALL,
        name="finish",
    )(coeff, members, modes)


def places(axis):
    sizes = [lax.axis_size(a) for a in axis]
    order = np.arange(np.prod(sizes)).reshape(sizes)
    for d, a in enumerate(axis):
        order = np.roll(order, -FIRST[axis].get(a, 0), axis=d)
    return [[int(place) for place in order.reshape(-1)]]


def exchange(x, axis):
    return lax.all_to_all(x, axis, split_axis=0, concat_axis=0, axis_index_groups=places(axis), tiled=True)


def everywhere(x, axis):
    return exchange(jnp.broadcast_to(x[None], (lax.axis_size(axis),) + x.shape), axis)


def on_device(members, modes, obs_weights, innovations, tile_start):
    mode_count = lax.axis_size(MODE)
    space_count = lax.axis_size(SPACE)
    last = mode_count - 1
    all_modes = lax.all_to_all(modes, MODE, split_axis=1, concat_axis=0, tiled=True)
    own, halo = field(tile_start, innovations, obs_weights, last)
    route = []
    for s in range(space_count):
        behind, ahead = (s - 1) % space_count, (s + 1) % space_count
        route.append((s * mode_count, ahead * mode_count))
        route.append((s * mode_count + last, behind * mode_count + last))
    halo = lax.ppermute(halo, SPACE + MODE, route)
    terms = project(own, halo, members, all_modes, last)
    part = jnp.sum(exchange(terms.reshape(lax.axis_size(NEAR), 1, -1), NEAR), axis=0)
    part = jnp.sum(everywhere(part, FAR), axis=0)
    coeff = everywhere(part, NEAR)
    increment, own_coeff = finish(coeff.reshape(MEMBERS, MODES), members, all_modes)
    return increment.reshape(OWN), own_coeff.T


def solution(mesh):
    finer = Mesh(mesh.devices.reshape(8, 2, 2, 4, 2, 2), SPACE + MODE)
    in_specs = (P(None, SPACE + MODE), P(MODE, SPACE), P(SPACE, None, None), P(SPACE, None), P(SPACE))
    out_specs = (P(SPACE + MODE), P(None, MODE))
    return jax.shard_map(
        on_device, mesh=finer, in_specs=in_specs, out_specs=out_specs, check_vma=False
    )
```

```python
import functools

import jax
import jax.numpy as jnp
import numpy as np
from jax import lax
from jax.experimental import pallas as pl
from jax.experimental.pallas import tpu as pltpu
from jax.sharding import Mesh
from jax.sharding import PartitionSpec as P

MEMBERS = 80
MODE_DEV = 4
MODES = 128
CELLS_DEV = 32768
TILE = 128
BLK_DEV = 128
OWN = 1024
OWN_TILES = OWN // TILE
LANES = 128
SUBLANES = 8
GROUP = 4
PIECE = 16
VMEM = pl.BlockSpec(memory_space=pltpu.VMEM)
SMALL = pltpu.CompilerParams(vmem_limit_bytes=12 * 2**20)
MODE = ("xhi", "zhi", "zlo", "core")
SPACE = ("y", "xlo")
NEAR = ("xlo", "xhi", "zlo", "core")
FAR = ("y", "zhi")
FIRST = {NEAR: {"xhi": 1, "zlo": 1}, FAR: {"y": 4, "zhi": 2}, MODE: {"xhi": 1, "zhi": 2}}


def mode_index():
    at = lax.axis_index(MODE[0])
    for axis in MODE[1:]:
        at = at * lax.axis_size(axis) + lax.axis_index(axis)
    return at


def split2(x):
    high = x.astype(jnp.bfloat16)
    return high, (x - high.astype(jnp.float32)).astype(jnp.bfloat16)


def find_field(last, begin_ref, innov_ref, obs_ref, own_ref, halo_ref, start_ref, ids, rows, held, acc, halo, begin_sem, row_sem, sems):
    m = mode_index()
    begin = pltpu.make_async_copy(begin_ref, start_ref, begin_sem)
    begin.start()
    pieces = [
        pltpu.make_async_copy(obs_ref.at[pl.ds(i * PIECE, PIECE)], held.at[pl.ds(i * PIECE, PIECE)], sems.at[i])
        for i in range(BLK_DEV // PIECE)
    ]
    pieces.append(pltpu.make_async_copy(innov_ref, rows, row_sem))
    for piece in pieces:
        piece.start()
    base = m * OWN
    first = jnp.where(m == 0, CELLS_DEV + TILE, 0)
    edge = (m == 0) | (m == last)
    acc[...] = jnp.zeros_like(acc)
    halo[...] = jnp.zeros_like(halo)
    begin.wait()

    def scan(b, count):
        start = start_ref[b]
        place = start - base
        far = start - first
        ids[count] = b
        hit = ((place > 0) & (place < OWN + TILE)) | (edge & (far > -TILE) & (far < TILE))
        return count + jnp.where(hit, 1, 0)

    count = lax.fori_loop(0, BLK_DEV, scan, jnp.int32(0), unroll=16)
    lane = lax.broadcasted_iota(jnp.int32, (1, LANES), 1)
    for piece in pieces:
        piece.wait()

    def add(g, carry):
        found = []
        for u in range(GROUP):
            i = g * GROUP + u
            valid = i < count
            b = jnp.where(valid, ids[i], 0)
            start = start_ref[b]
            row = rows[pl.ds(b, 1), :]
            high = row.astype(jnp.bfloat16).astype(jnp.float32)
            mid = (row - high).astype(jnp.bfloat16).astype(jnp.float32)
            low = row - high - mid
            parts = jnp.concatenate([high, mid, low, jnp.zeros((SUBLANES - 3, LANES), jnp.float32)], axis=0)
            adj = jnp.dot(parts.astype(jnp.bfloat16), held[b], preferred_element_type=jnp.float32)
            adj = adj + pltpu.roll(adj, SUBLANES - 1, 0) + pltpu.roll(adj, SUBLANES - 2, 0)
            off = lax.bitwise_and(start, TILE - 1)
            rolled = pltpu.roll(adj, off, 1)[0:1, :]
            front = jnp.where(lane >= off, rolled, 0.0)
            back = jnp.where(lane < off, rolled, 0.0)
            found.append((valid, start - base, start - first, front, back))
        for valid, place, far, front, back in found:

            @pl.when(valid & (place > 0) & (place < OWN + TILE))
            def _():
                seg = lax.shift_right_logical(place, 7)
                acc[pl.ds(seg, 1), :] += front
                acc[pl.ds(seg + 1, 1), :] += back

            @pl.when(valid & edge & (far > -TILE) & (far < TILE))
            def _():
                halo[...] += jnp.where(far >= 0, front, back)

        return carry

    lax.fori_loop(0, lax.shift_right_logical(count + GROUP - 1, 2), add, 0)
    own_ref[...] = acc[1 : 1 + OWN_TILES, :]
    halo_ref[...] = halo[...]


def waits_long():
    return lax.axis_index("zhi") < lax.axis_size("zhi") // 4


def early_kernel(last, modes_ref, begin_ref, innov_ref, obs_ref, laid_ref, own_ref, halo_ref, lay_sems, *scratch):
    part = modes_ref.shape[1] // 4
    copies = [
        pltpu.make_async_copy(
            modes_ref.at[:, pl.ds(q * part, part)], laid_ref.at[:, pl.ds((3 - q) * part, part)], lay_sems.at[q]
        )
        for q in range(4)
    ]
    for copy in copies:
        copy.start()

    @pl.when(waits_long())
    def _():
        find_field(last, begin_ref, innov_ref, obs_ref, own_ref, halo_ref, *scratch)

    for copy in copies:
        copy.wait()


def late_kernel(last, begin_ref, innov_ref, obs_ref, early_own_ref, early_halo_ref, own_ref, halo_ref, *scratch):
    @pl.when(waits_long())
    def _():
        own_ref[...] = early_own_ref[...]
        halo_ref[...] = early_halo_ref[...]

    @pl.when(jnp.logical_not(waits_long()))
    def _():
        find_field(last, begin_ref, innov_ref, obs_ref, own_ref, halo_ref, *scratch)


HBM = pl.BlockSpec(memory_space=pltpu.HBM)
FIELD = (jax.ShapeDtypeStruct((OWN_TILES, LANES), jnp.float32), jax.ShapeDtypeStruct((1, LANES), jnp.float32))


def field_scratch():
    return [
        pltpu.SMEM((BLK_DEV,), jnp.int32),
        pltpu.SMEM((BLK_DEV + GROUP,), jnp.int32),
        pltpu.VMEM((BLK_DEV, LANES), jnp.float32),
        pltpu.VMEM((BLK_DEV, TILE, TILE), jnp.bfloat16),
        pltpu.VMEM((2 * SUBLANES, LANES), jnp.float32),
        pltpu.VMEM((1, LANES), jnp.float32),
        pltpu.SemaphoreType.DMA,
        pltpu.SemaphoreType.DMA,
        pltpu.SemaphoreType.DMA((BLK_DEV // PIECE,)),
    ]


def in_hbm(*operands):
    return [pltpu.with_memory_space_constraint(x, pltpu.HBM) for x in operands]


def early(modes, tile_start, innovations, obs_weights, last):
    return pl.pallas_call(
        functools.partial(early_kernel, last),
        out_shape=(jax.ShapeDtypeStruct(modes.shape, modes.dtype),) + FIELD,
        in_specs=[HBM] * 4,
        out_specs=(VMEM,) * 3,
        scratch_shapes=[pltpu.SemaphoreType.DMA((4,))] + field_scratch(),
        compiler_params=SMALL,
        name="early",
    )(*in_hbm(modes, tile_start, innovations, obs_weights))


def late(tile_start, innovations, obs_weights, own, halo, last):
    return pl.pallas_call(
        functools.partial(late_kernel, last),
        out_shape=FIELD,
        in_specs=[HBM] * 3 + [VMEM] * 2,
        out_specs=(VMEM,) * 2,
        scratch_shapes=field_scratch(),
        compiler_params=SMALL,
        cost_estimate=pl.CostEstimate(flops=2**22, bytes_accessed=2**22, transcendentals=0),
        name="late",
    )(*in_hbm(tile_start, innovations, obs_weights), own, halo)


def project_kernel(last, own_ref, halo_ref, members_ref, modes_ref, out_ref):
    m = mode_index()
    halo = halo_ref[...]
    row = lax.broadcasted_iota(jnp.int32, (OWN_TILES, LANES), 0)
    takes = ((row == 0) & (m == 0)) | ((row == OWN_TILES - 1) & (m == last))
    weights = own_ref[...] + jnp.where(takes, halo, 0.0)
    contract = (((1,), (1,)), ((), ()))
    highs, lows = [], []
    for j in range(OWN_TILES):
        cells = slice(j * TILE, (j + 1) * TILE)
        high, low = split2(members_ref[:, cells].astype(jnp.float32) * weights[j : j + 1, :])
        highs.append(high)
        lows.append(low)
    modes = modes_ref[...]
    total = lax.dot_general(jnp.concatenate(highs, 1), modes, contract, preferred_element_type=jnp.float32)
    total += lax.dot_general(jnp.concatenate(lows, 1), modes, contract, preferred_element_type=jnp.float32)
    out_ref[...] = total


def project(own, halo, members, modes, last):
    return pl.pallas_call(
        functools.partial(project_kernel, last),
        out_shape=jax.ShapeDtypeStruct((MEMBERS, MODES), jnp.float32),
        in_specs=[VMEM] * 4,
        out_specs=VMEM,
        compiler_params=SMALL,
        name="project",
    )(own, halo, members, modes)


def finish_kernel(total_count, coeff_ref, members_ref, modes_ref, inc_ref, own_ref, turned):
    m = mode_place()
    coeff = coeff_ref[...]
    high, low = split2(coeff)
    modes = modes_ref[...]
    mixed = jnp.dot(high, modes, preferred_element_type=jnp.float32)
    mixed += jnp.dot(low, modes, preferred_element_type=jnp.float32)
    spread = jnp.sum(jnp.sum(coeff * coeff, axis=0, keepdims=True), axis=1, keepdims=True)
    factor = lax.rsqrt(1.0 + spread / total_count)
    turned[...] = coeff.T
    own_ref[...] = turned[pl.ds(m * MODE_DEV, MODE_DEV), :]
    mixed = mixed * members_ref[...].astype(jnp.float32)
    summed = jnp.sum(mixed, axis=0, keepdims=True) * (factor / (MEMBERS - 1))
    for j in range(OWN_TILES):
        inc_ref[j : j + 1, :] = summed[:, j * TILE : (j + 1) * TILE]


def finish(coeff, members, modes):
    return pl.pallas_call(
        functools.partial(finish_kernel, MEMBERS * MODES),
        out_shape=(
            jax.ShapeDtypeStruct((OWN_TILES, LANES), jnp.float32),
            jax.ShapeDtypeStruct((MODE_DEV, MEMBERS), jnp.float32),
        ),
        in_specs=[VMEM] * 3,
        out_specs=(VMEM, VMEM),
        scratch_shapes=[pltpu.VMEM((MODES, MEMBERS), jnp.float32)],
        compiler_params=SMALL,
        name="finish",
    )(coeff, members, modes)


def places(axis):
    sizes = [lax.axis_size(a) for a in axis]
    order = np.arange(np.prod(sizes)).reshape(sizes)
    for d, a in enumerate(axis):
        order = np.roll(order, -FIRST[axis].get(a, 0), axis=d)
    return [[int(place) for place in order.reshape(-1)]]


def mode_place():
    at = 0
    for axis in MODE:
        size = lax.axis_size(axis)
        at = at * size + lax.rem(lax.axis_index(axis) + (size - FIRST[MODE].get(axis, 0)), size)
    return at


def exchange(x, axis):
    return lax.all_to_all(x, axis, split_axis=0, concat_axis=0, axis_index_groups=places(axis), tiled=True)


def everywhere(x, axis):
    return exchange(jnp.broadcast_to(x[None], (lax.axis_size(axis),) + x.shape), axis)


def on_device(members, modes, obs_weights, innovations, tile_start):
    mode_count = lax.axis_size(MODE)
    space_count = lax.axis_size(SPACE)
    last = mode_count - 1
    laid, own, halo = early(modes, tile_start, innovations, obs_weights, last)
    all_modes = lax.all_to_all(
        laid, MODE, split_axis=1, concat_axis=0, axis_index_groups=places(MODE), tiled=True
    )
    own, halo = late(tile_start, innovations, obs_weights, own, halo, last)
    route = []
    for s in range(space_count):
        behind, ahead = (s - 1) % space_count, (s + 1) % space_count
        route.append((s * mode_count, ahead * mode_count))
        route.append((s * mode_count + last, behind * mode_count + last))
    halo = lax.ppermute(halo, SPACE + MODE, route)
    terms = project(own, halo, members, all_modes, last)
    part = jnp.sum(exchange(terms.reshape(lax.axis_size(NEAR), 1, -1), NEAR), axis=0)
    part = jnp.sum(everywhere(part, FAR), axis=0)
    coeff = everywhere(part, NEAR)
    increment, own_coeff = finish(coeff.reshape(MEMBERS, MODES), members, all_modes)
    return increment.reshape(OWN), own_coeff.T


def solution(mesh):
    finer = Mesh(mesh.devices.reshape(8, 2, 2, 4, 2, 2), SPACE + MODE)
    in_specs = (P(None, SPACE + MODE), P(MODE, SPACE), P(SPACE, None, None), P(SPACE, None), P(SPACE))
    out_specs = (P(SPACE + MODE), P(None, MODE))
    return jax.shard_map(
        on_device, mesh=finer, in_specs=in_specs, out_specs=out_specs, check_vma=False
    )
```

```python
import functools

import jax
import jax.numpy as jnp
import numpy as np
from jax import lax
from jax.experimental import pallas as pl
from jax.experimental.pallas import tpu as pltpu
from jax.sharding import Mesh
from jax.sharding import PartitionSpec as P

MEMBERS = 80
MODE_DEV = 4
MODES = 128
CELLS_DEV = 32768
TILE = 128
BLK_DEV = 128
OWN = 1024
OWN_TILES = OWN // TILE
LANES = 128
SUBLANES = 8
GROUP = 4
PIECE = 16
VMEM = pl.BlockSpec(memory_space=pltpu.VMEM)
SMALL = pltpu.CompilerParams(vmem_limit_bytes=12 * 2**20)
MODE = ("xhi", "zhi", "zlo", "core")
SPACE = ("y", "xlo")
NEAR = ("xlo", "xhi", "zlo", "core")
FAR = ("y", "zhi")
FIRST = {NEAR: {"xhi": 1, "zlo": 1}, FAR: {"y": 4, "zhi": 2}, MODE: {"xhi": 1, "zhi": 2}}


def mode_index():
    at = lax.axis_index(MODE[0])
    for axis in MODE[1:]:
        at = at * lax.axis_size(axis) + lax.axis_index(axis)
    return at


def split2(x):
    high = x.astype(jnp.bfloat16)
    return high, (x - high.astype(jnp.float32)).astype(jnp.bfloat16)


def find_field(last, begin_ref, innov_ref, obs_ref, own_ref, halo_ref, start_ref, ids, rows, held, acc, halo, begin_sem, row_sem, sems):
    m = mode_index()
    begin = pltpu.make_async_copy(begin_ref, start_ref, begin_sem)
    begin.start()
    pieces = [
        pltpu.make_async_copy(obs_ref.at[pl.ds(i * PIECE, PIECE)], held.at[pl.ds(i * PIECE, PIECE)], sems.at[i])
        for i in range(BLK_DEV // PIECE)
    ]
    pieces.append(pltpu.make_async_copy(innov_ref, rows, row_sem))
    for piece in pieces:
        piece.start()
    base = m * OWN
    first = jnp.where(m == 0, CELLS_DEV + TILE, 0)
    edge = (m == 0) | (m == last)
    acc[...] = jnp.zeros_like(acc)
    halo[...] = jnp.zeros_like(halo)
    begin.wait()

    def scan(b, count):
        start = start_ref[b]
        place = start - base
        far = start - first
        ids[count] = b
        hit = ((place > 0) & (place < OWN + TILE)) | (edge & (far > -TILE) & (far < TILE))
        return count + jnp.where(hit, 1, 0)

    count = lax.fori_loop(0, BLK_DEV, scan, jnp.int32(0), unroll=16)
    lane = lax.broadcasted_iota(jnp.int32, (1, LANES), 1)
    for piece in pieces:
        piece.wait()

    def add(g, carry):
        found = []
        for u in range(GROUP):
            i = g * GROUP + u
            valid = i < count
            b = jnp.where(valid, ids[i], 0)
            start = start_ref[b]
            row = rows[pl.ds(b, 1), :]
            high = row.astype(jnp.bfloat16).astype(jnp.float32)
            mid = (row - high).astype(jnp.bfloat16).astype(jnp.float32)
            low = row - high - mid
            parts = jnp.concatenate([high, mid, low, jnp.zeros((SUBLANES - 3, LANES), jnp.float32)], axis=0)
            adj = jnp.dot(parts.astype(jnp.bfloat16), held[b], preferred_element_type=jnp.float32)
            adj = adj + pltpu.roll(adj, SUBLANES - 1, 0) + pltpu.roll(adj, SUBLANES - 2, 0)
            off = lax.bitwise_and(start, TILE - 1)
            rolled = pltpu.roll(adj, off, 1)[0:1, :]
            front = jnp.where(lane >= off, rolled, 0.0)
            back = jnp.where(lane < off, rolled, 0.0)
            found.append((valid, start - base, start - first, front, back))
        for valid, place, far, front, back in found:

            @pl.when(valid & (place > 0) & (place < OWN + TILE))
            def _():
                seg = lax.shift_right_logical(place, 7)
                acc[pl.ds(seg, 1), :] += front
                acc[pl.ds(seg + 1, 1), :] += back

            @pl.when(valid & edge & (far > -TILE) & (far < TILE))
            def _():
                halo[...] += jnp.where(far >= 0, front, back)

        return carry

    lax.fori_loop(0, lax.shift_right_logical(count + GROUP - 1, 2), add, 0)
    own_ref[...] = acc[1 : 1 + OWN_TILES, :]
    halo_ref[...] = halo[...]


def waits_long():
    return (lax.axis_index("zhi") == 0) & (lax.axis_index("zlo") == 0)


def early_kernel(last, modes_ref, begin_ref, innov_ref, obs_ref, laid_ref, own_ref, halo_ref, lay_sems, *scratch):
    part = modes_ref.shape[1] // 4
    copies = [
        pltpu.make_async_copy(
            modes_ref.at[:, pl.ds(q * part, part)], laid_ref.at[:, pl.ds((3 - q) * part, part)], lay_sems.at[q]
        )
        for q in range(4)
    ]
    for copy in copies:
        copy.start()

    @pl.when(waits_long())
    def _():
        find_field(last, begin_ref, innov_ref, obs_ref, own_ref, halo_ref, *scratch)

    for copy in copies:
        copy.wait()


def late_kernel(last, begin_ref, innov_ref, obs_ref, early_own_ref, early_halo_ref, own_ref, halo_ref, *scratch):
    @pl.when(waits_long())
    def _():
        own_ref[...] = early_own_ref[...]
        halo_ref[...] = early_halo_ref[...]

    @pl.when(jnp.logical_not(waits_long()))
    def _():
        find_field(last, begin_ref, innov_ref, obs_ref, own_ref, halo_ref, *scratch)


HBM = pl.BlockSpec(memory_space=pltpu.HBM)
FIELD = (jax.ShapeDtypeStruct((OWN_TILES, LANES), jnp.float32), jax.ShapeDtypeStruct((1, LANES), jnp.float32))


def field_scratch():
    return [
        pltpu.SMEM((BLK_DEV,), jnp.int32),
        pltpu.SMEM((BLK_DEV + GROUP,), jnp.int32),
        pltpu.VMEM((BLK_DEV, LANES), jnp.float32),
        pltpu.VMEM((BLK_DEV, TILE, TILE), jnp.bfloat16),
        pltpu.VMEM((2 * SUBLANES, LANES), jnp.float32),
        pltpu.VMEM((1, LANES), jnp.float32),
        pltpu.SemaphoreType.DMA,
        pltpu.SemaphoreType.DMA,
        pltpu.SemaphoreType.DMA((BLK_DEV // PIECE,)),
    ]


def in_hbm(*operands):
    return [pltpu.with_memory_space_constraint(x, pltpu.HBM) for x in operands]


def early(modes, tile_start, innovations, obs_weights, last):
    return pl.pallas_call(
        functools.partial(early_kernel, last),
        out_shape=(jax.ShapeDtypeStruct(modes.shape, modes.dtype),) + FIELD,
        in_specs=[HBM] * 4,
        out_specs=(VMEM,) * 3,
        scratch_shapes=[pltpu.SemaphoreType.DMA((4,))] + field_scratch(),
        compiler_params=SMALL,
        name="early",
    )(*in_hbm(modes, tile_start, innovations, obs_weights))


def late(tile_start, innovations, obs_weights, own, halo, last):
    return pl.pallas_call(
        functools.partial(late_kernel, last),
        out_shape=FIELD,
        in_specs=[HBM] * 3 + [VMEM] * 2,
        out_specs=(VMEM,) * 2,
        scratch_shapes=field_scratch(),
        compiler_params=SMALL,
        cost_estimate=pl.CostEstimate(flops=2**22, bytes_accessed=2**22, transcendentals=0),
        name="late",
    )(*in_hbm(tile_start, innovations, obs_weights), own, halo)


def project_kernel(last, own_ref, halo_ref, members_ref, modes_ref, out_ref):
    m = mode_index()
    halo = halo_ref[...]
    row = lax.broadcasted_iota(jnp.int32, (OWN_TILES, LANES), 0)
    takes = ((row == 0) & (m == 0)) | ((row == OWN_TILES - 1) & (m == last))
    weights = own_ref[...] + jnp.where(takes, halo, 0.0)
    contract = (((1,), (1,)), ((), ()))
    highs, lows = [], []
    for j in range(OWN_TILES):
        cells = slice(j * TILE, (j + 1) * TILE)
        high, low = split2(members_ref[:, cells].astype(jnp.float32) * weights[j : j + 1, :])
        highs.append(high)
        lows.append(low)
    modes = modes_ref[...]
    total = lax.dot_general(jnp.concatenate(highs, 1), modes, contract, preferred_element_type=jnp.float32)
    total += lax.dot_general(jnp.concatenate(lows, 1), modes, contract, preferred_element_type=jnp.float32)
    out_ref[...] = total


def project(own, halo, members, modes, last):
    return pl.pallas_call(
        functools.partial(project_kernel, last),
        out_shape=jax.ShapeDtypeStruct((MEMBERS, MODES), jnp.float32),
        in_specs=[VMEM] * 4,
        out_specs=VMEM,
        compiler_params=SMALL,
        name="project",
    )(own, halo, members, modes)


def finish_kernel(total_count, coeff_ref, members_ref, modes_ref, inc_ref, own_ref, turned):
    m = mode_place()
    coeff = coeff_ref[...]
    high, low = split2(coeff)
    modes = modes_ref[...]
    mixed = jnp.dot(high, modes, preferred_element_type=jnp.float32)
    mixed += jnp.dot(low, modes, preferred_element_type=jnp.float32)
    spread = jnp.sum(jnp.sum(coeff * coeff, axis=0, keepdims=True), axis=1, keepdims=True)
    factor = lax.rsqrt(1.0 + spread / total_count)
    turned[...] = coeff.T
    own_ref[...] = turned[pl.ds(m * MODE_DEV, MODE_DEV), :]
    mixed = mixed * members_ref[...].astype(jnp.float32)
    summed = jnp.sum(mixed, axis=0, keepdims=True) * (factor / (MEMBERS - 1))
    for j in range(OWN_TILES):
        inc_ref[j : j + 1, :] = summed[:, j * TILE : (j + 1) * TILE]


def finish(coeff, members, modes):
    return pl.pallas_call(
        functools.partial(finish_kernel, MEMBERS * MODES),
        out_shape=(
            jax.ShapeDtypeStruct((OWN_TILES, LANES), jnp.float32),
            jax.ShapeDtypeStruct((MODE_DEV, MEMBERS), jnp.float32),
        ),
        in_specs=[VMEM] * 3,
        out_specs=(VMEM, VMEM),
        scratch_shapes=[pltpu.VMEM((MODES, MEMBERS), jnp.float32)],
        compiler_params=SMALL,
        name="finish",
    )(coeff, members, modes)


def places(axis):
    sizes = [lax.axis_size(a) for a in axis]
    order = np.arange(np.prod(sizes)).reshape(sizes)
    for d, a in enumerate(axis):
        order = np.roll(order, -FIRST[axis].get(a, 0), axis=d)
    return [[int(place) for place in order.reshape(-1)]]


def mode_place():
    at = 0
    for axis in MODE:
        size = lax.axis_size(axis)
        at = at * size + lax.rem(lax.axis_index(axis) + (size - FIRST[MODE].get(axis, 0)), size)
    return at


def exchange(x, axis):
    return lax.all_to_all(x, axis, split_axis=0, concat_axis=0, axis_index_groups=places(axis), tiled=True)


def everywhere(x, axis):
    return exchange(jnp.broadcast_to(x[None], (lax.axis_size(axis),) + x.shape), axis)


def on_device(members, modes, obs_weights, innovations, tile_start):
    mode_count = lax.axis_size(MODE)
    space_count = lax.axis_size(SPACE)
    last = mode_count - 1
    laid, own, halo = early(modes, tile_start, innovations, obs_weights, last)
    all_modes = lax.all_to_all(
        laid, MODE, split_axis=1, concat_axis=0, axis_index_groups=places(MODE), tiled=True
    )
    own, halo = late(tile_start, innovations, obs_weights, own, halo, last)
    route = []
    for s in range(space_count):
        behind, ahead = (s - 1) % space_count, (s + 1) % space_count
        route.append((s * mode_count, ahead * mode_count))
        route.append((s * mode_count + last, behind * mode_count + last))
    halo = lax.ppermute(halo, SPACE + MODE, route)
    terms = project(own, halo, members, all_modes, last)
    part = jnp.sum(exchange(terms.reshape(lax.axis_size(NEAR), 1, -1), NEAR), axis=0)
    part = jnp.sum(everywhere(part, FAR), axis=0)
    coeff = everywhere(part, NEAR)
    increment, own_coeff = finish(coeff.reshape(MEMBERS, MODES), members, all_modes)
    return increment.reshape(OWN), own_coeff.T


def solution(mesh):
    finer = Mesh(mesh.devices.reshape(8, 2, 2, 4, 2, 2), SPACE + MODE)
    in_specs = (P(None, SPACE + MODE), P(MODE, SPACE), P(SPACE, None, None), P(SPACE, None), P(SPACE))
    out_specs = (P(SPACE + MODE), P(None, MODE))
    return jax.shard_map(
        on_device, mesh=finer, in_specs=in_specs, out_specs=out_specs, check_vma=False
    )
```

```python
import functools

import jax
import jax.numpy as jnp
import numpy as np
from jax import lax
from jax.experimental import pallas as pl
from jax.experimental.pallas import tpu as pltpu
from jax.sharding import Mesh
from jax.sharding import PartitionSpec as P

MEMBERS = 80
MODE_DEV = 4
MODES = 128
CELLS_DEV = 32768
TILE = 128
BLK_DEV = 128
OWN = 1024
OWN_TILES = OWN // TILE
LANES = 128
SUBLANES = 8
GROUP = 4
PIECE = 16
VMEM = pl.BlockSpec(memory_space=pltpu.VMEM)
SMALL = pltpu.CompilerParams(vmem_limit_bytes=12 * 2**20)
MODE = ("xhi", "zhi", "zlo", "core")
SPACE = ("y", "xlo")
NEAR = ("xlo", "xhi", "zlo", "core")
FAR = ("y", "zhi")
FIRST = {NEAR: {"xhi": 1, "zlo": 1}, FAR: {"y": 4, "zhi": 3}, MODE: {"xhi": 1, "zhi": 2}}


def mode_index():
    at = lax.axis_index(MODE[0])
    for axis in MODE[1:]:
        at = at * lax.axis_size(axis) + lax.axis_index(axis)
    return at


def split2(x):
    high = x.astype(jnp.bfloat16)
    return high, (x - high.astype(jnp.float32)).astype(jnp.bfloat16)


def find_field(last, begin_ref, innov_ref, obs_ref, own_ref, halo_ref, start_ref, ids, rows, held, acc, halo, begin_sem, row_sem, sems):
    m = mode_index()
    begin = pltpu.make_async_copy(begin_ref, start_ref, begin_sem)
    begin.start()
    pieces = [
        pltpu.make_async_copy(obs_ref.at[pl.ds(i * PIECE, PIECE)], held.at[pl.ds(i * PIECE, PIECE)], sems.at[i])
        for i in range(BLK_DEV // PIECE)
    ]
    pieces.append(pltpu.make_async_copy(innov_ref, rows, row_sem))
    for piece in pieces:
        piece.start()
    base = m * OWN
    first = jnp.where(m == 0, CELLS_DEV + TILE, 0)
    edge = (m == 0) | (m == last)
    acc[...] = jnp.zeros_like(acc)
    halo[...] = jnp.zeros_like(halo)
    begin.wait()

    def scan(b, count):
        start = start_ref[b]
        place = start - base
        far = start - first
        ids[count] = b
        hit = ((place > 0) & (place < OWN + TILE)) | (edge & (far > -TILE) & (far < TILE))
        return count + jnp.where(hit, 1, 0)

    count = lax.fori_loop(0, BLK_DEV, scan, jnp.int32(0), unroll=16)
    lane = lax.broadcasted_iota(jnp.int32, (1, LANES), 1)
    for piece in pieces:
        piece.wait()

    def add(g, carry):
        found = []
        for u in range(GROUP):
            i = g * GROUP + u
            valid = i < count
            b = jnp.where(valid, ids[i], 0)
            start = start_ref[b]
            row = rows[pl.ds(b, 1), :]
            high = row.astype(jnp.bfloat16).astype(jnp.float32)
            mid = (row - high).astype(jnp.bfloat16).astype(jnp.float32)
            low = row - high - mid
            parts = jnp.concatenate([high, mid, low, jnp.zeros((SUBLANES - 3, LANES), jnp.float32)], axis=0)
            adj = jnp.dot(parts.astype(jnp.bfloat16), held[b], preferred_element_type=jnp.float32)
            adj = adj + pltpu.roll(adj, SUBLANES - 1, 0) + pltpu.roll(adj, SUBLANES - 2, 0)
            off = lax.bitwise_and(start, TILE - 1)
            rolled = pltpu.roll(adj, off, 1)[0:1, :]
            front = jnp.where(lane >= off, rolled, 0.0)
            back = jnp.where(lane < off, rolled, 0.0)
            found.append((valid, start - base, start - first, front, back))
        for valid, place, far, front, back in found:

            @pl.when(valid & (place > 0) & (place < OWN + TILE))
            def _():
                seg = lax.shift_right_logical(place, 7)
                acc[pl.ds(seg, 1), :] += front
                acc[pl.ds(seg + 1, 1), :] += back

            @pl.when(valid & edge & (far > -TILE) & (far < TILE))
            def _():
                halo[...] += jnp.where(far >= 0, front, back)

        return carry

    lax.fori_loop(0, lax.shift_right_logical(count + GROUP - 1, 2), add, 0)
    own_ref[...] = acc[1 : 1 + OWN_TILES, :]
    halo_ref[...] = halo[...]


def waits_long():
    return lax.axis_index("zhi") < lax.axis_size("zhi") // 4


def early_kernel(last, modes_ref, begin_ref, innov_ref, obs_ref, laid_ref, own_ref, halo_ref, lay_sems, *scratch):
    part = modes_ref.shape[1] // 4
    copies = [
        pltpu.make_async_copy(
            modes_ref.at[:, pl.ds(q * part, part)], laid_ref.at[:, pl.ds((3 - q) * part, part)], lay_sems.at[q]
        )
        for q in range(4)
    ]
    for copy in copies:
        copy.start()

    @pl.when(waits_long())
    def _():
        find_field(last, begin_ref, innov_ref, obs_ref, own_ref, halo_ref, *scratch)

    for copy in copies:
        copy.wait()


def late_kernel(last, begin_ref, innov_ref, obs_ref, early_own_ref, early_halo_ref, own_ref, halo_ref, *scratch):
    @pl.when(waits_long())
    def _():
        own_ref[...] = early_own_ref[...]
        halo_ref[...] = early_halo_ref[...]

    @pl.when(jnp.logical_not(waits_long()))
    def _():
        find_field(last, begin_ref, innov_ref, obs_ref, own_ref, halo_ref, *scratch)


HBM = pl.BlockSpec(memory_space=pltpu.HBM)
FIELD = (jax.ShapeDtypeStruct((OWN_TILES, LANES), jnp.float32), jax.ShapeDtypeStruct((1, LANES), jnp.float32))


def field_scratch():
    return [
        pltpu.SMEM((BLK_DEV,), jnp.int32),
        pltpu.SMEM((BLK_DEV + GROUP,), jnp.int32),
        pltpu.VMEM((BLK_DEV, LANES), jnp.float32),
        pltpu.VMEM((BLK_DEV, TILE, TILE), jnp.bfloat16),
        pltpu.VMEM((2 * SUBLANES, LANES), jnp.float32),
        pltpu.VMEM((1, LANES), jnp.float32),
        pltpu.SemaphoreType.DMA,
        pltpu.SemaphoreType.DMA,
        pltpu.SemaphoreType.DMA((BLK_DEV // PIECE,)),
    ]


def in_hbm(*operands):
    return [pltpu.with_memory_space_constraint(x, pltpu.HBM) for x in operands]


def early(modes, tile_start, innovations, obs_weights, last):
    return pl.pallas_call(
        functools.partial(early_kernel, last),
        out_shape=(jax.ShapeDtypeStruct(modes.shape, modes.dtype),) + FIELD,
        in_specs=[HBM] * 4,
        out_specs=(VMEM,) * 3,
        scratch_shapes=[pltpu.SemaphoreType.DMA((4,))] + field_scratch(),
        compiler_params=SMALL,
        name="early",
    )(*in_hbm(modes, tile_start, innovations, obs_weights))


def late(tile_start, innovations, obs_weights, own, halo, last):
    return pl.pallas_call(
        functools.partial(late_kernel, last),
        out_shape=FIELD,
        in_specs=[HBM] * 3 + [VMEM] * 2,
        out_specs=(VMEM,) * 2,
        scratch_shapes=field_scratch(),
        compiler_params=SMALL,
        cost_estimate=pl.CostEstimate(flops=2**22, bytes_accessed=2**22, transcendentals=0),
        name="late",
    )(*in_hbm(tile_start, innovations, obs_weights), own, halo)


def project_kernel(last, own_ref, halo_ref, members_ref, modes_ref, out_ref):
    m = mode_index()
    halo = halo_ref[...]
    row = lax.broadcasted_iota(jnp.int32, (OWN_TILES, LANES), 0)
    takes = ((row == 0) & (m == 0)) | ((row == OWN_TILES - 1) & (m == last))
    weights = own_ref[...] + jnp.where(takes, halo, 0.0)
    contract = (((1,), (1,)), ((), ()))
    highs, lows = [], []
    for j in range(OWN_TILES):
        cells = slice(j * TILE, (j + 1) * TILE)
        high, low = split2(members_ref[:, cells].astype(jnp.float32) * weights[j : j + 1, :])
        highs.append(high)
        lows.append(low)
    modes = modes_ref[...]
    total = lax.dot_general(jnp.concatenate(highs, 1), modes, contract, preferred_element_type=jnp.float32)
    total += lax.dot_general(jnp.concatenate(lows, 1), modes, contract, preferred_element_type=jnp.float32)
    out_ref[...] = total


def project(own, halo, members, modes, last):
    return pl.pallas_call(
        functools.partial(project_kernel, last),
        out_shape=jax.ShapeDtypeStruct((MEMBERS, MODES), jnp.float32),
        in_specs=[VMEM] * 4,
        out_specs=VMEM,
        compiler_params=SMALL,
        name="project",
    )(own, halo, members, modes)


def finish_kernel(total_count, coeff_ref, members_ref, modes_ref, inc_ref, own_ref, turned):
    m = mode_place()
    coeff = coeff_ref[...]
    high, low = split2(coeff)
    modes = modes_ref[...]
    mixed = jnp.dot(high, modes, preferred_element_type=jnp.float32)
    mixed += jnp.dot(low, modes, preferred_element_type=jnp.float32)
    spread = jnp.sum(jnp.sum(coeff * coeff, axis=0, keepdims=True), axis=1, keepdims=True)
    factor = lax.rsqrt(1.0 + spread / total_count)
    turned[...] = coeff.T
    own_ref[...] = turned[pl.ds(m * MODE_DEV, MODE_DEV), :]
    mixed = mixed * members_ref[...].astype(jnp.float32)
    summed = jnp.sum(mixed, axis=0, keepdims=True) * (factor / (MEMBERS - 1))
    for j in range(OWN_TILES):
        inc_ref[j : j + 1, :] = summed[:, j * TILE : (j + 1) * TILE]


def finish(coeff, members, modes):
    return pl.pallas_call(
        functools.partial(finish_kernel, MEMBERS * MODES),
        out_shape=(
            jax.ShapeDtypeStruct((OWN_TILES, LANES), jnp.float32),
            jax.ShapeDtypeStruct((MODE_DEV, MEMBERS), jnp.float32),
        ),
        in_specs=[VMEM] * 3,
        out_specs=(VMEM, VMEM),
        scratch_shapes=[pltpu.VMEM((MODES, MEMBERS), jnp.float32)],
        compiler_params=SMALL,
        name="finish",
    )(coeff, members, modes)


def places(axis):
    sizes = [lax.axis_size(a) for a in axis]
    order = np.arange(np.prod(sizes)).reshape(sizes)
    for d, a in enumerate(axis):
        order = np.roll(order, -FIRST[axis].get(a, 0), axis=d)
    return [[int(place) for place in order.reshape(-1)]]


def mode_place():
    at = 0
    for axis in MODE:
        size = lax.axis_size(axis)
        at = at * size + lax.rem(lax.axis_index(axis) + (size - FIRST[MODE].get(axis, 0)), size)
    return at


def exchange(x, axis):
    return lax.all_to_all(x, axis, split_axis=0, concat_axis=0, axis_index_groups=places(axis), tiled=True)


def everywhere(x, axis):
    return exchange(jnp.broadcast_to(x[None], (lax.axis_size(axis),) + x.shape), axis)


def on_device(members, modes, obs_weights, innovations, tile_start):
    mode_count = lax.axis_size(MODE)
    space_count = lax.axis_size(SPACE)
    last = mode_count - 1
    laid, own, halo = early(modes, tile_start, innovations, obs_weights, last)
    all_modes = lax.all_to_all(
        laid, MODE, split_axis=1, concat_axis=0, axis_index_groups=places(MODE), tiled=True
    )
    own, halo = late(tile_start, innovations, obs_weights, own, halo, last)
    route = []
    for s in range(space_count):
        behind, ahead = (s - 1) % space_count, (s + 1) % space_count
        route.append((s * mode_count, ahead * mode_count))
        route.append((s * mode_count + last, behind * mode_count + last))
    halo = lax.ppermute(halo, SPACE + MODE, route)
    terms = project(own, halo, members, all_modes, last)
    part = jnp.sum(exchange(terms.reshape(lax.axis_size(NEAR), 1, -1), NEAR), axis=0)
    part = jnp.sum(everywhere(part, FAR), axis=0)
    coeff = everywhere(part, NEAR)
    increment, own_coeff = finish(coeff.reshape(MEMBERS, MODES), members, all_modes)
    return increment.reshape(OWN), own_coeff.T


def solution(mesh):
    finer = Mesh(mesh.devices.reshape(8, 2, 2, 4, 2, 2), SPACE + MODE)
    in_specs = (P(None, SPACE + MODE), P(MODE, SPACE), P(SPACE, None, None), P(SPACE, None), P(SPACE))
    out_specs = (P(SPACE + MODE), P(None, MODE))
    return jax.shard_map(
        on_device, mesh=finer, in_specs=in_specs, out_specs=out_specs, check_vma=False
    )
```
